128 devices in a mesh: dp: 16 (over x, z), ctx: 8 (over y, core).
Axes of the slice: x: 4, y: 4, z: 4, core: 2. Of those that a mesh axis runs over, the one named last changes fastest.
Arguments:
- query_rows: bfloat16 [16, 1024, 8192], P('dp', 'ctx'), may hold values from -5 to 5
- key_rows: bfloat16 [16, 1024, 1024], P('dp', 'ctx'), may hold values from -5 to 5
- value_rows: bfloat16 [16, 1024, 1024], P('dp', 'ctx'), may hold values from -6 to 6
- layer_input: bfloat16 [16, 1024, 4096], P('dp', 'ctx'), may hold values from -6 to 6
- out_grad: bfloat16 [16, 1024, 8192], P('dp', 'ctx'), may hold values from -6 to 6
- parents: int32 [16, 8], P('dp'), may hold values from 0 to 7, as said below
- labels: int32 [16, 8], P('dp'), may hold values from 0 to 2
Outputs:
- attention_out: bfloat16 [16, 1024, 8192], P('dp', 'ctx')
- query_grad: bfloat16 [16, 1024, 8192], P('dp', 'ctx')
- key_grad: bfloat16 [16, 1024, 1024], P('dp', 'ctx')
- value_grad: bfloat16 [16, 1024, 1024], P('dp', 'ctx')
- value_weight_grad: float32 [4096, 1024], P(('dp', 'ctx'))
The draws below stay inside these ranges and needn't reach their ends.
Inputs may be any that keep to these rules, and one draw needn't show every extreme that they name: parents[r, b] <= b for every block b; an entry equal to its own block starts a tree; blocks 0 and 7 always start trees.
All inputs are finite; a program needn't handle non-finite values.
Results may differ from the reference program's by a relative error of at most 0.024.
Values may be sent and summed in bfloat16 or wider, within the bound.
No kernel may reach another device: no remote copies, remote signals or barrier semaphores. Data moves between devices by JAX's collectives and lax.ppermute only.
A program may use at most 128 MiB of HBM per device.

```python
import jax
import jax.numpy as jnp
from jax import lax

HQ = 64
KVH = 8
HD = 128
DX = 4096
BLK = 128
SEQ = 1024
NB = 8
ROLLS = 16


def draw_key_rows(key, part):
    key = jax.random.fold_in(key, 11)
    rows = jnp.clip(jax.random.normal(key, (ROLLS, SEQ, KVH * HD), jnp.float32), -5.0, 5.0)
    return rows.astype(jnp.bfloat16)


def draw_query_rows(key, part):
    key = jax.random.fold_in(key, 17)
    rows = jnp.clip(jax.random.normal(key, (ROLLS, SEQ, HQ * HD), jnp.float32), -5.0, 5.0)
    return rows.astype(jnp.bfloat16)


def draw_parents(key, part):
    key = jax.random.fold_in(key, 23)
    limits = jnp.arange(1, NB + 1, dtype=jnp.int32)
    picks = jax.random.randint(key, (ROLLS, NB), 0, limits[None, :])
    last_block = jnp.arange(NB, dtype=jnp.int32)[None, :] == NB - 1
    return jnp.where(last_block, NB - 1, picks).astype(jnp.int32)


def set_ends(values, stream_key, low, largest):
    shape = values.shape
    spot = [jax.random.randint(jax.random.fold_in(stream_key, axis), (), 0, shape[axis]) for axis in range(len(shape))]
    values = values.at[tuple(spot)].set(low)
    longest = shape.index(max(shape))
    spot[longest] = (spot[longest] + 1) % shape[longest]
    return values.at[tuple(spot)].set(largest)


def with_spikes(array, own_key, source, target, blocks, factor):
    def block_of(position):
        return (jnp.arange(array.shape[position]) // (array.shape[position] // blocks)).reshape((-1,) + (1,) * (array.ndim - 1 - position))

    one_side = jax.random.permutation(own_key, blocks)[block_of(target)]
    second = (block_of(target) + blocks // 2) % blocks
    return jnp.where((block_of(source) == one_side) | (block_of(source) == second), factor * array, array)


def block_levels(key, shape, pieces, low, top_value):
    level = 1.0
    for axis_at, blocks in pieces:
        heights = jax.random.uniform(jax.random.fold_in(jax.random.fold_in(key, 6), axis_at), (blocks,), jnp.float32, low / len(pieces), top_value / len(pieces))
        level = level * jnp.repeat(jnp.exp(heights), shape[axis_at] // blocks).reshape((-1,) + (1,) * (len(shape) - 1 - axis_at))
    return level


def noise(stream_key, shape, deviation, most, pieces=(), held_as=jnp.bfloat16):
    gain = block_levels(stream_key, shape, pieces, -0.22, 0.18) if pieces else 1.0
    array = jax.random.normal(stream_key, shape, jnp.float32) * deviation * gain
    return jnp.minimum(jnp.maximum(array, -most), most).astype(held_as)


def heavy_noise(key, extent, deviation, reach, shards, heavy, held_as=jnp.bfloat16):
    result = deviation * jax.random.normal(key, extent, jnp.float32)
    if shards:
        result = result * block_levels(key, extent, shards, -0.22, 0.18)
    return jnp.clip(with_spikes(result, jax.random.fold_in(key, 3), *heavy), -reach, reach).astype(held_as)


def setup_inputs(seed: int = 0) -> dict:
    splits = jax.random.split(jax.random.key(seed), 8)
    return {
        "query_rows": draw_query_rows(jax.random.fold_in(splits[7], 71), 0),
        "key_rows": draw_key_rows(jax.random.fold_in(splits[7], 71), 0),
        "value_rows": noise(splits[2], (ROLLS, SEQ, KVH * HD), 1.0, 6.0, ((0, 16), (1, 8))),
        "layer_input": heavy_noise(splits[3], (ROLLS, SEQ, DX), 1.0, 6.0, ((0, 16), (1, 8)), (0, 2, 16, 2.0)),
        "out_grad": noise(splits[4], (ROLLS, SEQ, HQ * HD), 1.0, 6.0, ((0, 16), (1, 8))),
        "parents": draw_parents(jax.random.fold_in(splits[7], 71), 0),
        "labels": set_ends(jax.random.randint(splits[6], (ROLLS, NB), 0, 3), jax.random.fold_in(splits[6], 1), 0, 2).astype(jnp.int32),
    }


def block_ancestry(parent_row):
    total_blocks = parent_row.shape[0]
    block_ids = jnp.arange(total_blocks, dtype=jnp.int32)
    ancestry = jnp.zeros((total_blocks, total_blocks), dtype=bool)
    current = block_ids
    for turn_index in range(total_blocks):
        ancestry = ancestry | (current[:, None] == block_ids[None, :])
        current = parent_row[current].astype(jnp.int32)
    return ancestry


def head_core(query_head, key_head, value_head, grad_head, allowed):
    score_scale = HD ** -0.5
    scores = jnp.dot(query_head, key_head.T, preferred_element_type=jnp.float32) * score_scale
    scores = jnp.where(allowed, scores, -jnp.inf)
    row_max = jnp.max(scores, axis=1, keepdims=True)
    shifted = jnp.exp(scores - row_max)
    weights = shifted / jnp.sum(shifted, axis=1, keepdims=True)
    weights_low = weights.astype(jnp.bfloat16)
    head_out = jnp.dot(weights_low, value_head, preferred_element_type=jnp.float32).astype(jnp.bfloat16)
    grad_weights = jnp.dot(grad_head, value_head.T, preferred_element_type=jnp.float32)
    inner_sum = jnp.sum(grad_head.astype(jnp.float32) * head_out.astype(jnp.float32), axis=1, keepdims=True)
    grad_scores = (weights * (grad_weights - inner_sum) * score_scale).astype(jnp.bfloat16)
    head_dq = jnp.dot(grad_scores, key_head, preferred_element_type=jnp.float32).astype(jnp.bfloat16)
    head_dk = jnp.dot(grad_scores.T, query_head, preferred_element_type=jnp.float32)
    head_dv = jnp.dot(weights_low.T, grad_head, preferred_element_type=jnp.float32)
    return head_out, head_dq, head_dk, head_dv


def one_rollout(inputs):
    query_seq, key_seq, value_seq, grad_seq, parent_row, label_row = inputs
    positions = jnp.arange(SEQ, dtype=jnp.int32)
    block_of = positions // BLK
    ancestry = block_ancestry(parent_row)
    allowed = ancestry[block_of][:, block_of] & (positions[None, :] <= positions[:, None])
    sign_rows = jnp.where(label_row[block_of] == 2, -1.0, 1.0).astype(jnp.float32)
    signed_grad = (grad_seq.astype(jnp.float32) * sign_rows[:, None]).astype(jnp.bfloat16)
    group_size = HQ // KVH

    def per_head(head_index):
        col_query = (head_index * HD).astype(jnp.int32)
        col_value = ((head_index // group_size) * HD).astype(jnp.int32)
        return head_core(
            lax.dynamic_slice_in_dim(query_seq, col_query, HD, 1),
            lax.dynamic_slice_in_dim(key_seq, col_value, HD, 1),
            lax.dynamic_slice_in_dim(value_seq, col_value, HD, 1),
            lax.dynamic_slice_in_dim(signed_grad, col_query, HD, 1),
            allowed,
        )

    head_out, head_dq, head_dk, head_dv = lax.map(per_head, jnp.arange(HQ, dtype=jnp.int32))
    attention_out = jnp.transpose(head_out, (1, 0, 2)).reshape(SEQ, HQ * HD)
    query_grad = jnp.transpose(head_dq, (1, 0, 2)).reshape(SEQ, HQ * HD)
    key_sum = jnp.sum(head_dk.reshape(KVH, group_size, SEQ, HD), axis=1)
    value_sum = jnp.sum(head_dv.reshape(KVH, group_size, SEQ, HD), axis=1)
    key_grad = jnp.transpose(key_sum, (1, 0, 2)).reshape(SEQ, KVH * HD).astype(jnp.bfloat16)
    value_grad = jnp.transpose(value_sum, (1, 0, 2)).reshape(SEQ, KVH * HD).astype(jnp.bfloat16)
    return attention_out, query_grad, key_grad, value_grad


def reference(query_rows, key_rows, value_rows, layer_input, out_grad, parents, labels):
    attention_out, query_grad, key_grad, value_grad = lax.map(
        one_rollout, (query_rows, key_rows, value_rows, out_grad, parents, labels))
    flat_input = layer_input.reshape(ROLLS * SEQ, DX)
    flat_grad = value_grad.reshape(ROLLS * SEQ, KVH * HD)
    value_weight_grad = jnp.dot(flat_input.T, flat_grad, preferred_element_type=jnp.float32) * (ROLLS * SEQ) ** -0.5
    return attention_out, query_grad, key_grad, value_grad, value_weight_grad
```

```python
import functools

import jax
import jax.numpy as jnp
from jax import lax
from jax.experimental import pallas as pl
from jax.experimental.pallas import tpu as pltpu
from jax.sharding import PartitionSpec as P

HD = 128
BLK = 128
GRP = 8
NY = 4
NZ = 4
NX = 4
HALF = 4
CH = 1
PER = HALF // CH
QW = GRP * HD
SLOTS = 2 * NY
PAIRS = 4
LOW = jnp.bfloat16
F32 = jnp.float32
SCALE = HD**-0.5
EXP_SCALE = SCALE * 1.4426950408889634
MASKED = -1e30


def dot_nt(a, b):
    return lax.dot_general(a, b, (((1,), (1,)), ((), ())), preferred_element_type=F32)


def dot_nn(a, b):
    return lax.dot_general(a, b, (((1,), (0,)), ((), ())), preferred_element_type=F32)


def dot_tn(a, b):
    return lax.dot_general(a, b, (((0,), (0,)), ((), ())), preferred_element_type=F32)


def attention_kernel(
    place, parents, labels,
    q_own, q_par, g_own, g_par, kv0, kv1, kv2, kv3,
    o_own, o_par, dq_own, dq_par, dkv0, dkv1, dkv2, dkv3,
    chain, k_all, v_all, k_pair, v_pair, q_st, g_st, s_st, w_st, m_st, l_st, o_st, dq_st, dk_acc, dv_acc,
):
    y = place[0]
    c = place[1]
    for d, kv in enumerate((kv0, kv1, kv2, kv3)):
        for e in range(2):
            k_all[2 * d + e] = kv[0, e]
            v_all[2 * d + e] = kv[1, e]
    dk_acc[...] = jnp.zeros_like(dk_acc)
    dv_acc[...] = jnp.zeros_like(dv_acc)
    row = lax.broadcasted_iota(jnp.int32, (BLK, BLK), 0)
    col = lax.broadcasted_iota(jnp.int32, (BLK, BLK), 1)
    causal = jnp.where(col <= row, 0.0, MASKED).astype(F32)

    def slot_of(block):
        return 2 * (y - block // 2) + jnp.bitwise_xor(block % 2, c)

    def one_block(block, q_ref, g_ref, o_ref, dq_ref):
        def walk(step, carry):
            current, count = carry
            above = parents[0, current]
            more = above != current
            nxt = jnp.where(more, above, current)
            chain[step + 1] = slot_of(nxt)
            return nxt, count + more.astype(jnp.int32)

        chain[0] = slot_of(block)
        _, count = lax.fori_loop(0, SLOTS - 1, walk, (block, jnp.int32(1)))
        pairs = (count + 1) // 2
        sign = jnp.where(labels[0, block] == 2, -1.0, 1.0).astype(F32)

        for h in range(GRP):
            rows = slice(h * BLK, (h + 1) * BLK)
            cols = slice(h * HD, (h + 1) * HD)
            q_st[rows, :] = q_ref[:, cols]
            g_st[rows, :] = (g_ref[:, cols].astype(F32) * sign).astype(LOW)
        m_st[...] = jnp.full_like(m_st, MASKED)
        l_st[...] = jnp.zeros_like(l_st)
        o_st[...] = jnp.zeros_like(o_st)
        dq_st[...] = jnp.zeros_like(dq_st)

        def score(t, _):
            for e in range(2):
                s = chain[2 * t + e]
                k_pair[t, e * BLK : (e + 1) * BLK, :] = k_all[s]
                v_pair[t, e * BLK : (e + 1) * BLK, :] = v_all[s]
            left = jnp.where(t > 0, 0.0, causal)
            right = jnp.where(2 * t + 1 < count, 0.0, MASKED).astype(F32)
            for h in range(GRP):
                rows = slice(h * BLK, (h + 1) * BLK)
                s = dot_nt(q_st[rows, :], k_pair[t])
                s_l = s[:, :BLK] + left
                s_r = s[:, BLK:] + right
                s_st[t, rows, :BLK] = s_l
                s_st[t, rows, BLK:] = s_r
                m_st[rows, :] = jnp.maximum(m_st[rows, :], jnp.maximum(s_l, s_r))
            return 0

        lax.fori_loop(0, pairs, score, 0)
        for h in range(GRP):
            rows = slice(h * BLK, (h + 1) * BLK)
            m_st[rows, :] = jnp.broadcast_to(jnp.max(m_st[rows, :], axis=1, keepdims=True), (BLK, BLK))

        def expo(t, _):
            for h in range(GRP):
                rows = slice(h * BLK, (h + 1) * BLK)
                m = m_st[rows, :]
                p_l = jnp.exp2((s_st[t, rows, :BLK] - m) * EXP_SCALE)
                p_r = jnp.exp2((s_st[t, rows, BLK:] - m) * EXP_SCALE)
                s_st[t, rows, :BLK] = p_l
                s_st[t, rows, BLK:] = p_r
                l_st[rows, :] += p_l + p_r
            return 0

        lax.fori_loop(0, pairs, expo, 0)
        for h in range(GRP):
            rows = slice(h * BLK, (h + 1) * BLK)
            total = jnp.sum(l_st[rows, :], axis=1, keepdims=True)
            l_st[rows, :] = jnp.broadcast_to(1.0 / total, (BLK, BLK))

        def values(t, _):
            for h in range(GRP):
                rows = slice(h * BLK, (h + 1) * BLK)
                r = l_st[rows, :]
                w_l = s_st[t, rows, :BLK] * r
                w_r = s_st[t, rows, BLK:] * r
                s_st[t, rows, :BLK] = w_l
                s_st[t, rows, BLK:] = w_r
                w_st[rows, :BLK] = w_l.astype(LOW)
                w_st[rows, BLK:] = w_r.astype(LOW)
                o_st[rows, :] += dot_nn(w_st[rows, :], v_pair[t])
            dv = dot_tn(w_st[...], g_st[...])
            for e in range(2):
                dv_acc[chain[2 * t + e]] += dv[e * BLK : (e + 1) * BLK, :]
            return 0

        lax.fori_loop(0, pairs, values, 0)
        for h in range(GRP):
            rows = slice(h * BLK, (h + 1) * BLK)
            out = o_st[rows, :].astype(LOW)
            o_ref[:, h * HD : (h + 1) * HD] = out
            inner = jnp.sum(g_st[rows, :].astype(F32) * out.astype(F32), axis=1, keepdims=True)
            m_st[rows, :] = jnp.broadcast_to(inner, (BLK, BLK))

        def grads(t, _):
            for h in range(GRP):
                rows = slice(h * BLK, (h + 1) * BLK)
                inner = m_st[rows, :]
                dp = dot_nt(g_st[rows, :], v_pair[t])
                ds_l = s_st[t, rows, :BLK] * (dp[:, :BLK] - inner)
                ds_r = s_st[t, rows, BLK:] * (dp[:, BLK:] - inner)
                w_st[rows, :BLK] = ds_l.astype(LOW)
                w_st[rows, BLK:] = ds_r.astype(LOW)
                dq_st[rows, :] += dot_nn(w_st[rows, :], k_pair[t])
            dk = dot_tn(w_st[...], q_st[...])
            for e in range(2):
                dk_acc[chain[2 * t + e]] += dk[e * BLK : (e + 1) * BLK, :]
            return 0

        lax.fori_loop(0, pairs, grads, 0)
        for h in range(GRP):
            rows = slice(h * BLK, (h + 1) * BLK)
            dq_ref[:, h * HD : (h + 1) * HD] = (dq_st[rows, :] * SCALE).astype(LOW)

    one_block(2 * y + c, q_own, g_own, o_own, dq_own)
    one_block(2 * y + 1 - c, q_par, g_par, o_par, dq_par)
    for d, dkv in enumerate((dkv0, dkv1, dkv2, dkv3)):
        for e in range(2):
            dkv[0, e] = (dk_acc[2 * d + e] * SCALE).astype(LOW)
            dkv[1, e] = dv_acc[2 * d + e].astype(LOW)


def attention(chunk, place, parents, labels, q, q_par, g, g_par, kvs):
    own = pl.BlockSpec((BLK, QW), lambda i, place, par, lab: (0, place[1] * HALF + chunk * PER + i))
    par = pl.BlockSpec((BLK, QW), lambda i, place, par, lab: (0, i))
    own_out = pl.BlockSpec((BLK, QW), lambda i, place, par, lab: (0, place[1] * PER + i))
    kv = pl.BlockSpec((2, 2, BLK, HD), lambda i, place, par, lab: (0, 0, 0, i))
    own_shape = jax.ShapeDtypeStruct((BLK, 2 * PER * QW), LOW)
    par_shape = jax.ShapeDtypeStruct((BLK, PER * QW), LOW)
    kv_shape = jax.ShapeDtypeStruct((2, 2, BLK, PER * HD), LOW)
    rows = GRP * BLK
    return pl.pallas_call(
        attention_kernel,
        grid_spec=pltpu.PrefetchScalarGridSpec(
            num_scalar_prefetch=3,
            grid=(PER,),
            in_specs=[own, par, own, par, kv, kv, kv, kv],
            out_specs=[own_out, par, own_out, par, kv, kv, kv, kv],
            scratch_shapes=[
                pltpu.SMEM((SLOTS,), jnp.int32),
                pltpu.VMEM((SLOTS, BLK, HD), LOW),
                pltpu.VMEM((SLOTS, BLK, HD), LOW),
                pltpu.VMEM((PAIRS, 2 * BLK, HD), LOW),
                pltpu.VMEM((PAIRS, 2 * BLK, HD), LOW),
                pltpu.VMEM((rows, HD), LOW),
                pltpu.VMEM((rows, HD), LOW),
                pltpu.VMEM((PAIRS, rows, 2 * BLK), F32),
                pltpu.VMEM((rows, 2 * BLK), LOW),
                pltpu.VMEM((rows, BLK), F32),
                pltpu.VMEM((rows, BLK), F32),
                pltpu.VMEM((rows, HD), F32),
                pltpu.VMEM((rows, HD), F32),
                pltpu.VMEM((SLOTS, BLK, HD), F32),
                pltpu.VMEM((SLOTS, BLK, HD), F32),
            ],
        ),
        out_shape=[own_shape, par_shape, own_shape, par_shape, kv_shape, kv_shape, kv_shape, kv_shape],
        compiler_params=pltpu.CompilerParams(
            dimension_semantics=("arbitrary",), vmem_limit_bytes=32 * 2**20
        ),
        cost_estimate=pl.CostEstimate(
            flops=6 * 2 * PER * rows * 2 * 4 * BLK * HD,
            bytes_accessed=8 * BLK * PER * QW * 2,
            transcendentals=PER * rows * 2 * 4 * BLK,
        ),
        name="tree_attention",
    )(place, parents, labels, q, q_par, g, g_par, *kvs)


def device(x, z, y, c):
    return (x * NZ + z) * SLOTS + y * 2 + c


def per_device(query_rows, key_rows, value_rows, layer_input, out_grad, parents, labels):
    ctx = lax.axis_index("ctx")
    dp = lax.axis_index("dp")
    y, c, z = ctx // 2, ctx % 2, dp % NZ
    place = jnp.stack([y, c]).astype(jnp.int32)
    q, k, v, g, x = query_rows[0], key_rows[0], value_rows[0], out_grad[0], layer_input[0]

    def swap(a):
        return lax.ppermute(a, "ctx", [(i, i ^ 1) for i in range(SLOTS)])

    def later(a, d):
        return lax.ppermute(a, "ctx", [(i, i + 2 * d) for i in range(SLOTS - 2 * d)])

    def earlier(a, d):
        return lax.ppermute(a, "ctx", [(i + 2 * d, i) for i in range(SLOTS - 2 * d)])

    def along_z(a, d):
        return lax.ppermute(a, "dp", [(i, i // NZ * NZ + (i + d) % NZ) for i in range(NX * NZ)])

    def cols(a, start, width):
        return lax.dynamic_slice_in_dim(a, start, width, 1)

    o_chunks, dq_chunks, dk_chunks, dv_chunks = [], [], [], []
    kv_both = jnp.stack([k, v])
    for ch in range(CH):
        width = PER * HD
        mine = lax.dynamic_slice_in_dim(kv_both, c * HALF * HD + ch * width, width, 2)
        other = lax.dynamic_slice_in_dim(kv_both, (1 - c) * HALF * HD + ch * width, width, 2)
        kv = jnp.stack([mine, swap(other)], axis=1)
        kvs = [kv] + [later(kv, d) for d in range(1, NY)]
        at = (1 - c) * HALF * QW + ch * PER * QW
        q_par = swap(cols(q, at, PER * QW))
        g_par = swap(cols(g, at, PER * QW))
        o_own, o_par, dq_own, dq_par, *dkvs = attention(ch, place, parents, labels, q, q_par, g, g_par, kvs)
        total = dkvs[0].astype(F32)
        for d in range(1, NY):
            total = total + earlier(dkvs[d], d).astype(F32)
        total = total.astype(LOW)
        o_chunks.append(lax.dynamic_update_slice_in_dim(o_own, swap(o_par), (1 - c) * PER * QW, 1))
        dq_chunks.append(lax.dynamic_update_slice_in_dim(dq_own, swap(dq_par), (1 - c) * PER * QW, 1))
        dkv_other = swap(total[:, 1])
        dkv_own = total[:, 0]
        first = jnp.where(c == 0, dkv_own, dkv_other)
        second = jnp.where(c == 0, dkv_other, dkv_own)
        both = jnp.concatenate([first, second], axis=-1)
        dk_chunks.append(both[0])
        dv_chunks.append(both[1])
        dv_low = total[1].reshape(2 * BLK, width)

    parts = x.reshape(BLK, NX, NZ, -1)
    wide = NX * parts.shape[3]

    def rows_for(d):
        return lax.dynamic_index_in_dim(parts, (z + d) % NZ, 2, keepdims=False).reshape(BLK, wide)

    x_z = [rows_for(0)] + [along_z(rows_for(d), d) for d in range(1, NZ)]
    x_z = jnp.stack(x_z)
    x_all = jnp.stack([x_z, swap(x_z)], axis=1)
    dv_all = jnp.stack([dv_low] + [along_z(dv_low, d) for d in range(1, NZ)])
    partial = jnp.dot(
        x_all.reshape(NZ * 2 * BLK, wide).T, dv_all.reshape(NZ * 2 * BLK, -1), preferred_element_type=F32
    ).astype(LOW)
    groups = [
        [device(xx, zz, yy, cc) for xx in range(NX) for yy in range(NY)] for zz in range(NZ) for cc in range(2)
    ]
    share = partial.reshape(NX * NY, -1, partial.shape[1])
    share = lax.all_to_all(share, ("dp", "ctx"), 0, 0, axis_index_groups=groups)
    summed = jnp.sum(share.astype(F32), axis=0) * (16 * SLOTS * BLK) ** -0.5
    keep = lax.dynamic_slice_in_dim(summed, c * 32, 32, 0)
    gone = swap(lax.dynamic_slice_in_dim(summed, (1 - c) * 32, 32, 0))
    weight_grad = jnp.concatenate([jnp.where(c == 0, keep, gone), jnp.where(c == 0, gone, keep)], axis=1)
    return (
        o_chunks[0][None],
        dq_chunks[0][None],
        dk_chunks[0][None],
        dv_chunks[0][None],
        weight_grad,
    )


def solution(mesh):
    rows = P("dp", "ctx", None)
    return jax.shard_map(
        per_device,
        mesh=mesh,
        in_specs=(rows,) * 5 + (P("dp", None), P("dp", None)),
        out_specs=(rows,) * 4 + (P(("dp", "ctx"), None),),
        check_vma=False,
    )
```

```python
import functools

import jax
import jax.numpy as jnp
from jax import lax
from jax.experimental import pallas as pl
from jax.experimental.pallas import tpu as pltpu
from jax.sharding import PartitionSpec as P

HD = 128
BLK = 128
GRP = 8
NY = 4
NZ = 4
NX = 4
HALF = 4
CH = 2
PER = HALF // CH
QW = GRP * HD
SLOTS = 2 * NY
PAIRS = 4
NG = 2
TF = 1024
TB = 1024
LOW = jnp.bfloat16
F32 = jnp.float32
SCALE = HD**-0.5
EXP_SCALE = SCALE * 1.4426950408889634
MASKED = -1e30


def dot_nt(a, b):
    return lax.dot_general(a, b, (((1,), (1,)), ((), ())), preferred_element_type=F32)


def dot_nn(a, b):
    return lax.dot_general(a, b, (((1,), (0,)), ((), ())), preferred_element_type=F32)


def dot_tn(a, b):
    return lax.dot_general(a, b, (((0,), (0,)), ((), ())), preferred_element_type=F32)


def attention_kernel(
    place, parents, labels,
    q_own, q_par, g_own, g_par, kv0, kv1, kv2, kv3,
    o_own, o_par, dq_own, dq_par, dk0, dk1, dk2, dk3, dv0, dv1, dv2, dv3,
    chain, k_pair, v_pair, kt_pair, vt_pair, q_st, g_st, gt_st, p_st, w_st, ds_st,
    m_st, mt_st, l_st, in_st, ot_st, dqt_st, k_all, v_all, dk_acc, dv_acc,
):
    y = place[0]
    c = place[1]
    heads = range(NG)
    for d, kv in enumerate((kv0, kv1, kv2, kv3)):
        for e in range(2):
            for n in heads:
                k_all[n, 2 * d + e] = kv[0, e, :, n * HD : (n + 1) * HD]
                v_all[n, 2 * d + e] = kv[1, e, :, n * HD : (n + 1) * HD]
    dk_acc[...] = jnp.zeros_like(dk_acc)
    dv_acc[...] = jnp.zeros_like(dv_acc)
    key_pos = lax.broadcasted_iota(jnp.int32, (BLK, BLK), 0)
    query_pos = lax.broadcasted_iota(jnp.int32, (BLK, BLK), 1)
    causal = jnp.where(key_pos <= query_pos, 0.0, MASKED).astype(F32)
    causal = jnp.concatenate([causal] * (TF // BLK), axis=1)
    tiles_f = [slice(i * TF, (i + 1) * TF) for i in range(GRP * BLK // TF)]
    tiles_b = [slice(i * TB, (i + 1) * TB) for i in range(GRP * BLK // TB)]

    def slot_of(block):
        return 2 * (y - lax.shift_right_logical(block, 1)) + jnp.bitwise_xor(jnp.bitwise_and(block, 1), c)

    def fold(a, op):
        while a.shape[0] > 8:
            half = a.shape[0] // 2
            a = op(a[:half], a[half:])
        return a

    def one_block(block, q_ref, g_ref, o_ref, dq_ref):
        def walk(step, carry):
            current, count = carry
            above = parents[0, current]
            more = above != current
            nxt = jnp.where(more, above, current)
            chain[step + 1] = slot_of(nxt)
            return nxt, count + more.astype(jnp.int32)

        chain[0] = slot_of(block)
        _, count = lax.fori_loop(0, SLOTS - 1, walk, (block, jnp.int32(1)))
        pairs = (count + 1) // 2
        sign = jnp.full((BLK, HD), jnp.where(labels[0, block] == 2, -1.0, 1.0), F32).astype(LOW)

        for n in heads:
            for h in range(GRP):
                rows = slice(h * BLK, (h + 1) * BLK)
                cols = slice(n * QW + h * HD, n * QW + (h + 1) * HD)
                q_st[n, rows, :] = q_ref[:, cols]
                g = g_ref[:, cols] * sign
                g_st[n, rows, :] = g
                gt_st[n, :, rows] = g.T

        def forward(t, first):
            second = jnp.where(2 * t + 1 < count, 0.0, MASKED).astype(F32)
            for n in heads:
                for e in range(2):
                    s = chain[2 * t + e]
                    rows = slice(e * BLK, (e + 1) * BLK)
                    k_pair[n, t, rows, :] = k_all[n, s]
                    v_pair[n, t, rows, :] = v_all[n, s]
                    kt_pair[n, t, :, rows] = k_all[n, s].T
                    vt_pair[n, t, :, rows] = v_all[n, s].T
            for cols in tiles_f:
                for n in heads:
                    s = dot_nt(k_pair[n, t], q_st[n, cols, :])
                    s_a = s[:BLK]
                    if first:
                        s_a = s_a + causal
                    s_b = s[BLK:] + second
                    top = jnp.max(fold(jnp.maximum(s_a, s_b), jnp.maximum), axis=0, keepdims=True)
                    if not first:
                        old = m_st[n, 0:1, cols]
                        top = jnp.maximum(top, old)
                        alpha = jnp.exp2((old - top) * EXP_SCALE)
                    p_a = jnp.exp2((s_a - top) * EXP_SCALE)
                    p_b = jnp.exp2((s_b - top) * EXP_SCALE)
                    p_low = jnp.concatenate([p_a.astype(LOW), p_b.astype(LOW)], axis=0)
                    p_st[n, t, :, cols] = p_low
                    total = fold(p_a + p_b, jnp.add)
                    out = dot_nn(vt_pair[n, t], p_low)
                    if first:
                        l_st[n, :, cols] = total
                        ot_st[n, :, cols] = out
                    else:
                        l_st[n, :, cols] = l_st[n, :, cols] * alpha + total
                        ot_st[n, :, cols] = ot_st[n, :, cols] * alpha + out
                    m_st[n, 0:1, cols] = top
                    mt_st[n, t, 0:1, cols] = top

        def more_forward(t, carry):
            forward(t, False)
            return carry

        forward(0, True)
        lax.fori_loop(1, pairs, more_forward, 0)
        for h in range(GRP):
            for n in heads:
                cols = slice(h * BLK, (h + 1) * BLK)
                r = 1.0 / jnp.sum(l_st[n, :, cols], axis=0, keepdims=True)
                out = (ot_st[n, :, cols] * r).astype(LOW)
                o_ref[:, n * QW + h * HD : n * QW + (h + 1) * HD] = out.T
                l_st[n, 0:1, cols] = r
                in_st[n, 0:1, cols] = jnp.sum(
                    gt_st[n, :, cols].astype(F32) * out.astype(F32), axis=0, keepdims=True
                )

        def backward(t, first):
            for cols in tiles_b:
                for n in heads:
                    f = jnp.exp2((mt_st[n, t, 0:1, cols] - m_st[n, 0:1, cols]) * EXP_SCALE) * l_st[n, 0:1, cols]
                    w = p_st[n, t, :, cols].astype(F32) * f
                    w_st[n, :, cols] = w.astype(LOW)
                    dp = dot_nn(v_pair[n, t], gt_st[n, :, cols])
                    ds = (w * (dp - in_st[n, 0:1, cols])).astype(LOW)
                    ds_st[n, :, cols] = ds
                    dq = dot_nn(kt_pair[n, t], ds)
                    if first:
                        dqt_st[n, :, cols] = dq
                    else:
                        dqt_st[n, :, cols] += dq
            for n in heads:
                dv = dot_nn(w_st[n], g_st[n])
                dk = dot_nn(ds_st[n], q_st[n])
                for e in range(2):
                    s = chain[2 * t + e]
                    dv_acc[n, s] += dv[e * BLK : (e + 1) * BLK, :]
                    dk_acc[n, s] += dk[e * BLK : (e + 1) * BLK, :]

        def more_backward(t, carry):
            backward(t, False)
            return carry

        backward(0, True)
        lax.fori_loop(1, pairs, more_backward, 0)
        for h in range(GRP):
            for n in heads:
                cols = slice(h * BLK, (h + 1) * BLK)
                dq_ref[:, n * QW + h * HD : n * QW + (h + 1) * HD] = (dqt_st[n, :, cols] * SCALE).astype(LOW).T

    one_block(2 * y + c, q_own, g_own, o_own, dq_own)
    one_block(2 * y + 1 - c, q_par, g_par, o_par, dq_par)
    for d, (dk, dv) in enumerate(((dk0, dv0), (dk1, dv1), (dk2, dv2), (dk3, dv3))):
        for e in range(2):
            for n in heads:
                dk[e, :, n * HD : (n + 1) * HD] = (dk_acc[n, 2 * d + e] * SCALE).astype(LOW)
                dv[e, :, n * HD : (n + 1) * HD] = dv_acc[n, 2 * d + e].astype(LOW)


def attention_onward_kernel(*refs):
    attention_kernel(*refs[:11], *refs[13:])


def attention(chunk, place, parents, labels, q, q_par, g, g_par, kvs, before):
    wide = NG * QW
    own = pl.BlockSpec((BLK, wide), lambda i, place, par, lab: (0, (place[1] * HALF + chunk * PER) // NG + i))
    par = pl.BlockSpec((BLK, wide), lambda i, place, par, lab: (0, chunk * PER // NG + i))
    par_out = pl.BlockSpec((BLK, wide), lambda i, place, par, lab: (0, i))
    kv = pl.BlockSpec((2, 2, BLK, NG * HD), lambda i, place, par, lab: (0, 0, 0, i))
    grad = pl.BlockSpec((2, BLK, NG * HD), lambda i, place, par, lab: (0, 0, i))
    own_shape = jax.ShapeDtypeStruct((BLK, 2 * HALF * QW), LOW)
    par_shape = jax.ShapeDtypeStruct((BLK, PER * QW), LOW)
    grad_shape = jax.ShapeDtypeStruct((2, BLK, PER * HD), LOW)
    rows = GRP * BLK
    return pl.pallas_call(
        attention_onward_kernel if before else attention_kernel,
        grid_spec=pltpu.PrefetchScalarGridSpec(
            num_scalar_prefetch=3,
            grid=(PER // NG,),
            in_specs=[own, par, own, par, kv, kv, kv, kv] + [pl.BlockSpec(memory_space=pl.ANY)] * len(before),
            out_specs=[own, par_out, own, par_out] + [grad] * 8,
            scratch_shapes=[
                pltpu.SMEM((SLOTS,), jnp.int32),
                pltpu.VMEM((NG, PAIRS, 2 * BLK, HD), LOW),
                pltpu.VMEM((NG, PAIRS, 2 * BLK, HD), LOW),
                pltpu.VMEM((NG, PAIRS, HD, 2 * BLK), LOW),
                pltpu.VMEM((NG, PAIRS, HD, 2 * BLK), LOW),
                pltpu.VMEM((NG, rows, HD), LOW),
                pltpu.VMEM((NG, rows, HD), LOW),
                pltpu.VMEM((NG, HD, rows), LOW),
                pltpu.VMEM((NG, PAIRS, 2 * BLK, rows), LOW),
                pltpu.VMEM((NG, 2 * BLK, rows), LOW),
                pltpu.VMEM((NG, 2 * BLK, rows), LOW),
                pltpu.VMEM((NG, 8, rows), F32),
                pltpu.VMEM((NG, PAIRS, 8, rows), F32),
                pltpu.VMEM((NG, 8, rows), F32),
                pltpu.VMEM((NG, 8, rows), F32),
                pltpu.VMEM((NG, HD, rows), F32),
                pltpu.VMEM((NG, HD, rows), F32),
                pltpu.VMEM((NG, SLOTS, BLK, HD), LOW),
                pltpu.VMEM((NG, SLOTS, BLK, HD), LOW),
                pltpu.VMEM((NG, SLOTS, BLK, HD), F32),
                pltpu.VMEM((NG, SLOTS, BLK, HD), F32),
            ],
        ),
        out_shape=[own_shape, par_shape, own_shape, par_shape] + [grad_shape] * 8,
        input_output_aliases={11: 0, 12: 2} if before else {},
        compiler_params=pltpu.CompilerParams(
            dimension_semantics=("arbitrary",), vmem_limit_bytes=48 * 2**20
        ),
        cost_estimate=pl.CostEstimate(
            flops=6 * 2 * PER * rows * 2 * 4 * BLK * HD * 4,
            bytes_accessed=8 * BLK * PER * QW * 2,
            transcendentals=PER * rows * 2 * 4 * BLK,
        ),
        name="tree_attention",
    )(place, parents, labels, q, q_par, g, g_par, *kvs, *before)


def weight_kernel(*refs):
    own, other, dvs, out = refs[:NZ], refs[NZ], refs[NZ + 1 : -1], refs[-1]
    total = None
    for d in range(NZ):
        for e in range(2):
            rows = own[d][...] if e == 0 else other[d]
            term = dot_tn(rows, dvs[d][e])
            total = term if total is None else total + term
    out[...] = total.astype(LOW)


def weight_partial(own, other, dvs):
    wide, cols = own[0].shape[1], dvs[0].shape[2]
    step = 256
    return pl.pallas_call(
        weight_kernel,
        grid=(wide // step,),
        in_specs=[pl.BlockSpec((BLK, step), lambda i: (0, i))] * NZ
        + [pl.BlockSpec((NZ, BLK, step), lambda i: (0, 0, i))]
        + [pl.BlockSpec((2, BLK, cols), lambda i: (0, 0, 0))] * NZ,
        out_specs=pl.BlockSpec((step, cols), lambda i: (i, 0)),
        out_shape=jax.ShapeDtypeStruct((wide, cols), LOW),
        compiler_params=pltpu.CompilerParams(vmem_limit_bytes=16 * 2**20),
        cost_estimate=pl.CostEstimate(
            flops=2 * NZ * 2 * BLK * wide * cols, bytes_accessed=NZ * 2 * BLK * (wide + cols) * 2, transcendentals=0
        ),
        name="weight_partial",
    )(*own, other, *dvs)


def split_kernel(place, k_mine, k_other, v_mine, v_other, mine, other):
    mine[0], mine[1] = k_mine[...], v_mine[...]
    other[0], other[1] = k_other[...], v_other[...]


def split_halves(place, k, v):
    width = HALF * HD
    mine = pl.BlockSpec((BLK, width), lambda i, place: (0, place[1]))
    other = pl.BlockSpec((BLK, width), lambda i, place: (0, 1 - place[1]))
    whole = pl.BlockSpec((2, BLK, width), lambda i, place: (0, 0, 0))
    return pl.pallas_call(
        split_kernel,
        grid_spec=pltpu.PrefetchScalarGridSpec(
            num_scalar_prefetch=1, grid=(1,), in_specs=[mine, other, mine, other], out_specs=[whole, whole]
        ),
        out_shape=[jax.ShapeDtypeStruct((2, BLK, width), LOW)] * 2,
        name="split_halves",
    )(place, k, k, v, v)


def device(x, z, y, c):
    return (x * NZ + z) * SLOTS + y * 2 + c


def per_device(query_rows, key_rows, value_rows, layer_input, out_grad, parents, labels):
    ctx = lax.axis_index("ctx")
    dp = lax.axis_index("dp")
    y, c, z = ctx // 2, ctx % 2, dp % NZ
    place = jnp.stack([y, c]).astype(jnp.int32)
    q, k, v, g, x = query_rows[0], key_rows[0], value_rows[0], out_grad[0], layer_input[0]

    def swap(a):
        return lax.ppermute(a, "ctx", [(i, i ^ 1) for i in range(SLOTS)])

    def later(a, d):
        return lax.ppermute(a, "ctx", [(i, i + 2 * d) for i in range(SLOTS - 2 * d)])

    def earlier(a, d):
        return lax.ppermute(a, "ctx", [(i + 2 * d, i) for i in range(SLOTS - 2 * d)])

    def along_z(a, d):
        return lax.ppermute(a, "dp", [(i, i // NZ * NZ + (i + d) % NZ) for i in range(NX * NZ)])

    def cols(a, start, width):
        return lax.dynamic_slice_in_dim(a, start, width, 1)

    width = PER * HD
    kv_mine, kv_other = split_halves(place, k, v)
    kv_pair = jnp.stack([kv_mine, swap(kv_other)], axis=1)
    q_par = swap(cols(q, (1 - c) * HALF * QW, HALF * QW))
    g_par = swap(cols(g, (1 - c) * HALF * QW, HALF * QW))
    gathered = []
    for ch in range(CH):
        kv = kv_pair[..., ch * width : (ch + 1) * width]
        gathered.append([kv] + [later(kv, d) for d in range(1, NY)])

    x, _ = lax.optimization_barrier((x, kv_pair))
    parts = x.reshape(BLK, NX, NZ, -1)
    tall = NX * parts.shape[3]

    def rows_for(d):
        return lax.dynamic_index_in_dim(parts, (z + d) % NZ, 2, keepdims=False).reshape(BLK, tall)

    x_own = [rows_for(0)] + [along_z(rows_for(d), d) for d in range(1, NZ)]
    x_other = swap(jnp.stack(x_own))
    groups = [
        [device(xx, zz, yy, cc) for xx in range(NX) for yy in range(NY)] for zz in range(NZ) for cc in range(2)
    ]

    before = ()
    o_pars, dq_pars, dk_own, dv_own, dk_other, dv_other, summed = [], [], [], [], [], [], []
    for ch in range(CH):
        o_all, o_par, dq_all, dq_par, *grads = attention(
            ch, place, parents, labels, q, q_par, g, g_par, gathered[ch], before
        )
        before = (o_all, dq_all)
        dks, dvs = grads[:NY], grads[NY:]
        dv = dvs[0].astype(F32)
        for d in range(1, NY):
            dv = dv + earlier(dvs[d], d).astype(F32)
        dv = dv.astype(LOW)
        dv_z = [dv] + [along_z(dv, d) for d in range(1, NZ)]
        share = weight_partial(x_own, x_other, dv_z).reshape(NX * NY, -1, width)
        share = lax.all_to_all(share, ("dp", "ctx"), 0, 0, axis_index_groups=groups)
        summed.append(jnp.sum(share.astype(F32), axis=0))
        dk = dks[0].astype(F32)
        for d in range(1, NY):
            dk = dk + earlier(dks[d], d).astype(F32)
        dk = dk.astype(LOW)
        o_pars.append(swap(o_par))
        dq_pars.append(swap(dq_par))
        dk_own.append(dk[0])
        dv_own.append(dv[0])
        other = swap(jnp.stack([dk[1], dv[1]]))
        dk_other.append(other[0])
        dv_other.append(other[1])

    for ch in range(CH):
        at = ((1 - c) * HALF + ch * PER) * QW
        o_all = lax.dynamic_update_slice_in_dim(o_all, o_pars[ch], at, 1)
        dq_all = lax.dynamic_update_slice_in_dim(dq_all, dq_pars[ch], at, 1)

    def in_order(own, other):
        own, other = jnp.concatenate(own, axis=1), jnp.concatenate(other, axis=1)
        return jnp.concatenate([jnp.where(c == 0, own, other), jnp.where(c == 0, other, own)], axis=1)

    summed = jnp.concatenate(summed, axis=1) * (16 * SLOTS * BLK) ** -0.5
    rows = summed.shape[0] // 2
    keep = lax.dynamic_slice_in_dim(summed, c * rows, rows, 0)
    gone = swap(lax.dynamic_slice_in_dim(summed, (1 - c) * rows, rows, 0))
    weight_grad = in_order([keep], [gone])
    return (
        o_all[None],
        dq_all[None],
        in_order(dk_own, dk_other)[None],
        in_order(dv_own, dv_other)[None],
        weight_grad,
    )


def solution(mesh):
    rows = P("dp", "ctx", None)
    return jax.shard_map(
        per_device,
        mesh=mesh,
        in_specs=(rows,) * 5 + (P("dp", None), P("dp", None)),
        out_specs=(rows,) * 4 + (P(("dp", "ctx"), None),),
        check_vma=False,
    )
```

```python
import functools

import jax
import jax.numpy as jnp
from jax import lax
from jax.experimental import pallas as pl
from jax.experimental.pallas import tpu as pltpu
from jax.sharding import PartitionSpec as P

HD = 128
BLK = 128
GRP = 8
NY = 4
NZ = 4
NX = 4
HALF = 4
CH = 1
PER = HALF // CH
QW = GRP * HD
SLOTS = 2 * NY
PAIRS = 4
NG = 2
TF = 1024
TB = 1024
LOW = jnp.bfloat16
F32 = jnp.float32
SCALE = HD**-0.5
EXP_SCALE = SCALE * 1.4426950408889634
MASKED = -1e30


def dot_nt(a, b):
    return lax.dot_general(a, b, (((1,), (1,)), ((), ())), preferred_element_type=F32)


def dot_nn(a, b):
    return lax.dot_general(a, b, (((1,), (0,)), ((), ())), preferred_element_type=F32)


def dot_tn(a, b):
    return lax.dot_general(a, b, (((0,), (0,)), ((), ())), preferred_element_type=F32)


def attention_kernel(
    place, parents, labels,
    q_own, q_par, g_own, g_par, kv,
    o_own, o_par, dq_own, dq_par, dk_out, dv_out,
    chain, k_pair, v_pair, kt_pair, vt_pair, q_st, g_st, gt_st, p_st, w_st, ds_st,
    m_st, mt_st, l_st, in_st, ot_st, dqt_st, dk_acc, dv_acc,
):
    y = place[0]
    c = place[1]
    heads = range(NG)
    dk_acc[...] = jnp.zeros_like(dk_acc)
    dv_acc[...] = jnp.zeros_like(dv_acc)
    key_pos = lax.broadcasted_iota(jnp.int32, (BLK, BLK), 0)
    query_pos = lax.broadcasted_iota(jnp.int32, (BLK, BLK), 1)
    causal = jnp.where(key_pos <= query_pos, 0.0, MASKED).astype(F32)
    causal = jnp.concatenate([causal] * (TF // BLK), axis=1)
    tiles_f = [slice(i * TF, (i + 1) * TF) for i in range(GRP * BLK // TF)]
    tiles_b = [slice(i * TB, (i + 1) * TB) for i in range(GRP * BLK // TB)]

    def fold(a, op):
        while a.shape[0] > 8:
            half = a.shape[0] // 2
            a = op(a[:half], a[half:])
        return a

    def one_block(block, q_ref, g_ref, o_ref, dq_ref):
        def walk(step, carry):
            current, count = carry
            above = parents[0, current]
            more = above != current
            nxt = jnp.where(more, above, current)
            chain[step + 1] = nxt
            return nxt, count + more.astype(jnp.int32)

        chain[0] = block
        _, count = lax.fori_loop(0, SLOTS - 1, walk, (block, jnp.int32(1)))
        pairs = (count + 1) // 2
        sign = jnp.full((BLK, HD), jnp.where(labels[0, block] == 2, -1.0, 1.0), F32).astype(LOW)

        for n in heads:
            for h in range(GRP):
                rows = slice(h * BLK, (h + 1) * BLK)
                cols = slice(n * QW + h * HD, n * QW + (h + 1) * HD)
                q_st[n, rows, :] = q_ref[:, cols]
                g = g_ref[:, cols] * sign
                g_st[n, rows, :] = g
                gt_st[n, :, rows] = g.T

        def forward(t, first):
            second = jnp.where(2 * t + 1 < count, 0.0, MASKED).astype(F32)
            for n in heads:
                for e in range(2):
                    s = chain[2 * t + e]
                    rows = slice(e * BLK, (e + 1) * BLK)
                    k = kv[s, 0, :, n * HD : (n + 1) * HD]
                    v = kv[s, 1, :, n * HD : (n + 1) * HD]
                    k_pair[n, t, rows, :] = k
                    v_pair[n, t, rows, :] = v
                    kt_pair[n, t, :, rows] = k.T
                    vt_pair[n, t, :, rows] = v.T
            for cols in tiles_f:
                for n in heads:
                    s = dot_nt(k_pair[n, t], q_st[n, cols, :])
                    s_a = s[:BLK]
                    if first:
                        s_a = s_a + causal
                    s_b = s[BLK:] + second
                    top = jnp.max(fold(jnp.maximum(s_a, s_b), jnp.maximum), axis=0, keepdims=True)
                    if not first:
                        old = m_st[n, 0:1, cols]
                        top = jnp.maximum(top, old)
                        alpha = jnp.exp2((old - top) * EXP_SCALE)
                    p_a = jnp.exp2((s_a - top) * EXP_SCALE)
                    p_b = jnp.exp2((s_b - top) * EXP_SCALE)
                    p_low = jnp.concatenate([p_a.astype(LOW), p_b.astype(LOW)], axis=0)
                    p_st[n, t, :, cols] = p_low
                    total = fold(p_a + p_b, jnp.add)
                    out = dot_nn(vt_pair[n, t], p_low)
                    if first:
                        l_st[n, :, cols] = total
                        ot_st[n, :, cols] = out
                    else:
                        l_st[n, :, cols] = l_st[n, :, cols] * alpha + total
                        ot_st[n, :, cols] = ot_st[n, :, cols] * alpha + out
                    m_st[n, 0:1, cols] = top
                    mt_st[n, t, 0:1, cols] = top

        def more_forward(t, carry):
            forward(t, False)
            return carry

        forward(0, True)
        lax.fori_loop(1, pairs, more_forward, 0)
        for h in range(GRP):
            for n in heads:
                cols = slice(h * BLK, (h + 1) * BLK)
                r = 1.0 / jnp.sum(l_st[n, :, cols], axis=0, keepdims=True)
                out = (ot_st[n, :, cols] * r).astype(LOW)
                o_ref[:, n * QW + h * HD : n * QW + (h + 1) * HD] = out.T
                l_st[n, 0:1, cols] = r
                in_st[n, 0:1, cols] = jnp.sum(
                    gt_st[n, :, cols].astype(F32) * out.astype(F32), axis=0, keepdims=True
                )

        def backward(t, first):
            for cols in tiles_b:
                for n in heads:
                    f = jnp.exp2((mt_st[n, t, 0:1, cols] - m_st[n, 0:1, cols]) * EXP_SCALE) * l_st[n, 0:1, cols]
                    w = p_st[n, t, :, cols].astype(F32) * f
                    w_st[n, :, cols] = w.astype(LOW)
                    dp = dot_nn(v_pair[n, t], gt_st[n, :, cols])
                    ds = (w * (dp - in_st[n, 0:1, cols])).astype(LOW)
                    ds_st[n, :, cols] = ds
                    dq = dot_nn(kt_pair[n, t], ds)
                    if first:
                        dqt_st[n, :, cols] = dq
                    else:
                        dqt_st[n, :, cols] += dq
            for n in heads:
                dv = dot_nn(w_st[n], g_st[n])
                dk = dot_nn(ds_st[n], q_st[n])
                for e in range(2):
                    s = chain[2 * t + e]
                    dv_acc[n, s] += dv[e * BLK : (e + 1) * BLK, :]
                    dk_acc[n, s] += dk[e * BLK : (e + 1) * BLK, :]

        def more_backward(t, carry):
            backward(t, False)
            return carry

        backward(0, True)
        lax.fori_loop(1, pairs, more_backward, 0)
        for h in range(GRP):
            for n in heads:
                cols = slice(h * BLK, (h + 1) * BLK)
                dq_ref[:, n * QW + h * HD : n * QW + (h + 1) * HD] = (dqt_st[n, :, cols] * SCALE).astype(LOW).T

    one_block(2 * y + c, q_own, g_own, o_own, dq_own)
    one_block(2 * y + 1 - c, q_par, g_par, o_par, dq_par)
    for s in range(SLOTS):
        for n in heads:
            dk_out[s, :, n * HD : (n + 1) * HD] = (dk_acc[n, s] * SCALE).astype(LOW)
            dv_out[s, :, n * HD : (n + 1) * HD] = dv_acc[n, s].astype(LOW)


def attention_onward_kernel(*refs):
    attention_kernel(*refs[:8], *refs[10:])


def attention(chunk, place, parents, labels, q, q_par, g, g_par, kv, before):
    wide = NG * QW
    own = pl.BlockSpec((BLK, wide), lambda i, place, par, lab: (0, (place[1] * HALF + chunk * PER) // NG + i))
    par = pl.BlockSpec((BLK, wide), lambda i, place, par, lab: (0, chunk * PER // NG + i))
    par_out = pl.BlockSpec((BLK, wide), lambda i, place, par, lab: (0, i))
    kv_in = pl.BlockSpec((SLOTS, 2, BLK, NG * HD), lambda i, place, par, lab: (0, 0, 0, i))
    grad = pl.BlockSpec((SLOTS, BLK, NG * HD), lambda i, place, par, lab: (0, 0, i))
    own_shape = jax.ShapeDtypeStruct((BLK, 2 * HALF * QW), LOW)
    par_shape = jax.ShapeDtypeStruct((BLK, PER * QW), LOW)
    grad_shape = jax.ShapeDtypeStruct((SLOTS, BLK, PER * HD), LOW)
    rows = GRP * BLK
    return pl.pallas_call(
        attention_onward_kernel if before else attention_kernel,
        grid_spec=pltpu.PrefetchScalarGridSpec(
            num_scalar_prefetch=3,
            grid=(PER // NG,),
            in_specs=[own, par, own, par, kv_in] + [pl.BlockSpec(memory_space=pl.ANY)] * len(before),
            out_specs=[own, par_out, own, par_out] + [grad] * 2,
            scratch_shapes=[
                pltpu.SMEM((SLOTS,), jnp.int32),
                pltpu.VMEM((NG, PAIRS, 2 * BLK, HD), LOW),
                pltpu.VMEM((NG, PAIRS, 2 * BLK, HD), LOW),
                pltpu.VMEM((NG, PAIRS, HD, 2 * BLK), LOW),
                pltpu.VMEM((NG, PAIRS, HD, 2 * BLK), LOW),
                pltpu.VMEM((NG, rows, HD), LOW),
                pltpu.VMEM((NG, rows, HD), LOW),
                pltpu.VMEM((NG, HD, rows), LOW),
                pltpu.VMEM((NG, PAIRS, 2 * BLK, rows), LOW),
                pltpu.VMEM((NG, 2 * BLK, rows), LOW),
                pltpu.VMEM((NG, 2 * BLK, rows), LOW),
                pltpu.VMEM((NG, 8, rows), F32),
                pltpu.VMEM((NG, PAIRS, 8, rows), F32),
                pltpu.VMEM((NG, 8, rows), F32),
                pltpu.VMEM((NG, 8, rows), F32),
                pltpu.VMEM((NG, HD, rows), F32),
                pltpu.VMEM((NG, HD, rows), F32),
                pltpu.VMEM((NG, SLOTS, BLK, HD), F32),
                pltpu.VMEM((NG, SLOTS, BLK, HD), F32),
            ],
        ),
        out_shape=[own_shape, par_shape, own_shape, par_shape] + [grad_shape] * 2,
        input_output_aliases={8: 0, 9: 2} if before else {},
        compiler_params=pltpu.CompilerParams(
            dimension_semantics=("arbitrary",), vmem_limit_bytes=48 * 2**20
        ),
        cost_estimate=pl.CostEstimate(
            flops=6 * 2 * PER * rows * 2 * 4 * BLK * HD * 4,
            bytes_accessed=8 * BLK * PER * QW * 2,
            transcendentals=PER * rows * 2 * 4 * BLK,
        ),
        name="tree_attention",
    )(place, parents, labels, q, q_par, g, g_par, kv, *before)


def weight_kernel(x, dv, out):
    tokens = 2 * NZ * BLK
    out[...] = dot_tn(x[...].reshape(tokens, -1), dv[...].reshape(tokens, -1)).astype(LOW)


def weight_partial(x, dv):
    tall, wide, step = x.shape[2], dv.shape[2], 256
    return pl.pallas_call(
        weight_kernel,
        grid=(tall // step,),
        in_specs=[
            pl.BlockSpec((2 * NZ, BLK, step), lambda i: (0, 0, i)),
            pl.BlockSpec((2 * NZ, BLK, wide), lambda i: (0, 0, 0)),
        ],
        out_specs=pl.BlockSpec((step, wide), lambda i: (i, 0)),
        out_shape=jax.ShapeDtypeStruct((tall, wide), LOW),
        cost_estimate=pl.CostEstimate(
            flops=2 * NZ * 2 * BLK * tall * wide, bytes_accessed=NZ * 2 * BLK * (tall + wide) * 2, transcendentals=0
        ),
        name="weight_partial",
    )(x, dv)


def kv_kernel(k, v, out):
    for half in range(2):
        at = slice(half * HALF * HD, (half + 1) * HALF * HD)
        out[half, 0] = k[:, at]
        out[half, 1] = v[:, at]


def kv_sends(k, v):
    width = HALF * HD
    row = pl.BlockSpec((BLK, 2 * width), lambda i: (0, 0))
    return pl.pallas_call(
        kv_kernel,
        grid=(NY,),
        in_specs=[row, row],
        out_specs=pl.BlockSpec((2, 2, BLK, width), lambda i: (i, 0, 0, 0)),
        out_shape=jax.ShapeDtypeStruct((SLOTS, 2, BLK, width), LOW),
        name="kv_sends",
    )(k, v)


def x_kernel(x, out):
    piece = x.shape[1] // (NX * NZ)
    for i in range(NX):
        part = x[:, pl.ds((i * NZ + pl.program_id(0)) * piece, piece)]
        for e in range(2):
            out[e, :, i * piece : (i + 1) * piece] = part


def x_sends(x):
    wide = x.shape[1] // NZ
    return pl.pallas_call(
        x_kernel,
        grid=(NZ,),
        in_specs=[pl.BlockSpec(x.shape, lambda i: (0, 0))],
        out_specs=pl.BlockSpec((2, BLK, wide), lambda i: (i, 0, 0)),
        out_shape=jax.ShapeDtypeStruct((2 * NZ, BLK, wide), LOW),
        name="x_sends",
    )(x)


def sum_kernel(parts, total, sends):
    width = parts.shape[2]
    for half in range(2):
        acc = parts[half].astype(F32)
        for i in range(1, NY):
            acc = acc + parts[2 * i + half].astype(F32)
        acc = acc.astype(LOW)
        total[:, half * width : (half + 1) * width] = acc
        for i in range(NZ):
            sends[2 * i + half] = acc


def sum_blocks(parts):
    rows, width = parts.shape[1:]
    return pl.pallas_call(
        sum_kernel,
        out_shape=[
            jax.ShapeDtypeStruct((rows, 2 * width), LOW),
            jax.ShapeDtypeStruct((2 * NZ, rows, width), LOW),
        ],
        name="sum_blocks",
    )(parts)


def finish_kernel(parts, out):
    width = parts.shape[2]
    for half in range(2):
        acc = parts[half].astype(F32)
        for i in range(1, NX * NY):
            acc = acc + parts[2 * i + half].astype(F32)
        out[:, half * width : (half + 1) * width] = acc * (16 * SLOTS * BLK) ** -0.5


def finish_weight(parts):
    rows, width = parts.shape[1:]
    return pl.pallas_call(
        finish_kernel, out_shape=jax.ShapeDtypeStruct((rows, 2 * width), F32), name="finish_weight"
    )(parts)


def device(x, z, y, c):
    return (x * NZ + z) * SLOTS + y * 2 + c


def per_device(query_rows, key_rows, value_rows, layer_input, out_grad, parents, labels):
    ctx = lax.axis_index("ctx")
    y, c = ctx // 2, ctx % 2
    place = jnp.stack([y, c]).astype(jnp.int32)
    q, k, v, g, x = query_rows[0], key_rows[0], value_rows[0], out_grad[0], layer_input[0]
    along_z = [[device(i, j, m, n) for j in range(NZ) for n in range(2)] for i in range(NX) for m in range(NY)]
    across = [[device(i, j, m, n) for i in range(NX) for m in range(NY) for n in range(2)] for j in range(NZ)]

    def swap(a):
        return lax.ppermute(a, "ctx", [(i, i ^ 1) for i in range(SLOTS)])

    def exchange(a, groups):
        return lax.all_to_all(a, ("dp", "ctx"), 0, 0, axis_index_groups=groups)

    def cols(a, start, width):
        return lax.dynamic_slice_in_dim(a, start, width, 1)

    at = (1 - c) * HALF * QW
    kv = lax.all_to_all(kv_sends(k, v), "ctx", 0, 0)
    q_par = swap(cols(q, at, HALF * QW))
    g_par = swap(cols(g, at, HALF * QW))
    x_all = exchange(x_sends(x), along_z)
    o_own, o_par, dq_own, dq_par, dk, dv = attention(0, place, parents, labels, q, q_par, g, g_par, kv, ())
    dv_terms = lax.all_to_all(dv, "ctx", 0, 0)
    dk, dv_terms = lax.optimization_barrier((dk, dv_terms))
    value_grad, dv_sends = sum_blocks(dv_terms)
    dv_all = exchange(dv_sends, along_z)
    key_grad, _ = sum_blocks(lax.all_to_all(dk, "ctx", 0, 0))
    partial = weight_partial(x_all, dv_all)
    weight_grad = finish_weight(exchange(partial.reshape(2 * NX * NY, -1, partial.shape[1]), across))
    out = lax.dynamic_update_slice_in_dim(o_own, swap(o_par), at, 1)
    query_grad = lax.dynamic_update_slice_in_dim(dq_own, swap(dq_par), at, 1)
    return out[None], query_grad[None], key_grad[None], value_grad[None], weight_grad


def solution(mesh):
    rows = P("dp", "ctx", None)
    return jax.shard_map(
        per_device,
        mesh=mesh,
        in_specs=(rows,) * 5 + (P("dp", None), P("dp", None)),
        out_specs=(rows,) * 4 + (P(("dp", "ctx"), None),),
        check_vma=False,
    )
```

```python
import jax
import jax.numpy as jnp
from jax import lax
from jax.experimental import pallas as pl
from jax.experimental.pallas import tpu as pltpu
from jax.sharding import PartitionSpec as P

HD = 128
BLK = 128
GRP = 8
NY = 4
NZ = 4
NX = 4
HALF = 4
QW = GRP * HD
SLOTS = 2 * NY
PAIRS = 4
NG = 2
LOW = jnp.bfloat16
F32 = jnp.float32
SCALE = HD**-0.5
EXP_SCALE = SCALE * 1.4426950408889634
MASKED = -1e30


def dot_nt(a, b):
    return lax.dot_general(a, b, (((1,), (1,)), ((), ())), preferred_element_type=F32)


def dot_nn(a, b):
    return lax.dot_general(a, b, (((1,), (0,)), ((), ())), preferred_element_type=F32)


def dot_tn(a, b):
    return lax.dot_general(a, b, (((0,), (0,)), ((), ())), preferred_element_type=F32)


def walk(parents, block, chain):
    def above(step, carry):
        current, count = carry
        parent = parents[0, current]
        more = parent != current
        current = jnp.where(more, parent, current)
        chain[step + 1] = current
        return current, count + more.astype(jnp.int32)

    chain[0] = block
    return lax.fori_loop(0, SLOTS - 1, above, (block, jnp.int32(1)))[1]


def fold(a, op):
    while a.shape[0] > 8:
        half = a.shape[0] // 2
        a = op(a[:half], a[half:])
    return a


def causal_mask():
    key_pos = lax.broadcasted_iota(jnp.int32, (BLK, BLK), 0)
    query_pos = lax.broadcasted_iota(jnp.int32, (BLK, BLK), 1)
    causal = jnp.where(key_pos <= query_pos, 0.0, MASKED).astype(F32)
    return jnp.concatenate([causal] * GRP, axis=1)


def block_sign(labels, block):
    return jnp.full((BLK, HD), jnp.where(labels[0, block] == 2, -1.0, 1.0), F32).astype(LOW)


def masked(s, t, count, first, causal):
    second = jnp.where(2 * t + 1 < count, 0.0, MASKED).astype(F32)
    s_a = s[:BLK]
    if first:
        s_a = s_a + causal
    return s_a, s[BLK:] + second


def over_pairs(step, pairs):
    def more(t, carry):
        step(t, False)
        return carry

    step(0, True)
    lax.fori_loop(1, pairs, more, 0)


def forward_kernel(
    place, parents, labels,
    q_own, q_par, g_own, g_par, kv,
    o_own, o_par, dv_out, stats,
    chain, k_pair, vt_pair, q_st, g_st, gt_st, p_st, w_st, m_st, mt_st, l_st, ot_st, dv_acc,
):
    y = place[0]
    c = place[1]
    heads = range(NG)
    dv_acc[...] = jnp.zeros_like(dv_acc)
    causal = causal_mask()

    def one_block(which, block, q_ref, g_ref, o_ref):
        count = walk(parents, block, chain)
        pairs = (count + 1) // 2
        sign = block_sign(labels, block)
        for n in heads:
            for h in range(GRP):
                rows = slice(h * BLK, (h + 1) * BLK)
                cols = slice(n * QW + h * HD, n * QW + (h + 1) * HD)
                q_st[n, rows, :] = q_ref[:, cols]
                g = g_ref[:, cols] * sign
                g_st[n, rows, :] = g
                gt_st[n, :, rows] = g.T

        def scores(t, first):
            for n in heads:
                for e in range(2):
                    s = chain[2 * t + e]
                    rows = slice(e * BLK, (e + 1) * BLK)
                    k_pair[n, t, rows, :] = kv[s, 0, :, n * HD : (n + 1) * HD]
                    vt_pair[n, t, :, rows] = kv[s, 1, :, n * HD : (n + 1) * HD].T
            for n in heads:
                s_a, s_b = masked(dot_nt(k_pair[n, t], q_st[n]), t, count, first, causal)
                top = jnp.max(fold(jnp.maximum(s_a, s_b), jnp.maximum), axis=0, keepdims=True)
                if not first:
                    old = m_st[n, 0:1, :]
                    top = jnp.maximum(top, old)
                    alpha = jnp.exp2((old - top) * EXP_SCALE)
                p_a = jnp.exp2((s_a - top) * EXP_SCALE)
                p_b = jnp.exp2((s_b - top) * EXP_SCALE)
                p_low = jnp.concatenate([p_a.astype(LOW), p_b.astype(LOW)], axis=0)
                p_st[n, t] = p_low
                total = fold(p_a + p_b, jnp.add)
                out = dot_nn(vt_pair[n, t], p_low)
                if first:
                    l_st[n] = total
                    ot_st[n] = out
                else:
                    l_st[n] = l_st[n] * alpha + total
                    ot_st[n] = ot_st[n] * alpha + out
                m_st[n, 0:1, :] = top
                mt_st[n, t, 0:1, :] = top

        over_pairs(scores, pairs)
        for n in heads:
            total = jnp.sum(l_st[n], axis=0, keepdims=True)
            l_st[n, 0:1, :] = 1.0 / total
            stats[n, which, 0:1, :] = m_st[n, 0:1, :] * EXP_SCALE + jnp.log2(total)
        for h in range(GRP):
            for n in heads:
                cols = slice(h * BLK, (h + 1) * BLK)
                out = (ot_st[n, :, cols] * l_st[n, 0:1, cols]).astype(LOW)
                o_ref[:, n * QW + h * HD : n * QW + (h + 1) * HD] = out.T
                stats[n, which, 1:2, cols] = jnp.sum(
                    gt_st[n, :, cols].astype(F32) * out.astype(F32), axis=0, keepdims=True
                )

        def values(t, first):
            for n in heads:
                f = jnp.exp2((mt_st[n, t, 0:1, :] - m_st[n, 0:1, :]) * EXP_SCALE) * l_st[n, 0:1, :]
                w_st[n] = (p_st[n, t].astype(F32) * f).astype(LOW)
            for n in heads:
                dv = dot_nn(w_st[n], g_st[n])
                for e in range(2):
                    dv_acc[n, chain[2 * t + e]] += dv[e * BLK : (e + 1) * BLK, :]

        over_pairs(values, pairs)

    one_block(0, 2 * y + c, q_own, g_own, o_own)
    one_block(1, 2 * y + 1 - c, q_par, g_par, o_par)
    for s in range(SLOTS):
        for n in heads:
            dv_out[s, :, n * HD : (n + 1) * HD] = dv_acc[n, s].astype(LOW)


def backward_kernel(
    place, parents, labels,
    q_own, q_par, g_own, g_par, kv, stats,
    dq_own, dq_par, dk_out,
    chain, k_pair, v_pair, kt_pair, q_st, g_st, ds_st, dqt_st, dk_acc,
):
    y = place[0]
    c = place[1]
    heads = range(NG)
    dk_acc[...] = jnp.zeros_like(dk_acc)
    causal = causal_mask()

    def one_block(which, block, q_ref, g_ref, dq_ref):
        count = walk(parents, block, chain)
        sign = block_sign(labels, block)
        for n in heads:
            for h in range(GRP):
                rows = slice(h * BLK, (h + 1) * BLK)
                cols = slice(n * QW + h * HD, n * QW + (h + 1) * HD)
                q_st[n, rows, :] = q_ref[:, cols]
                g_st[n, rows, :] = g_ref[:, cols] * sign

        def grads(t, first):
            for n in heads:
                for e in range(2):
                    s = chain[2 * t + e]
                    rows = slice(e * BLK, (e + 1) * BLK)
                    k = kv[s, 0, :, n * HD : (n + 1) * HD]
                    k_pair[n, rows, :] = k
                    kt_pair[n, :, rows] = k.T
                    v_pair[n, rows, :] = kv[s, 1, :, n * HD : (n + 1) * HD]
            for n in heads:
                s_a, s_b = masked(dot_nt(k_pair[n], q_st[n]), t, count, first, causal)
                dp = dot_nt(v_pair[n], g_st[n])
                lse, inner = stats[n, which, 0:1, :], stats[n, which, 1:2, :]
                ds_a = jnp.exp2(s_a * EXP_SCALE - lse) * (dp[:BLK] - inner)
                ds_b = jnp.exp2(s_b * EXP_SCALE - lse) * (dp[BLK:] - inner)
                ds = jnp.concatenate([ds_a.astype(LOW), ds_b.astype(LOW)], axis=0)
                ds_st[n] = ds
                dq = dot_nn(kt_pair[n], ds)
                if first:
                    dqt_st[n] = dq
                else:
                    dqt_st[n] += dq
            for n in heads:
                dk = dot_nn(ds_st[n], q_st[n])
                for e in range(2):
                    dk_acc[n, chain[2 * t + e]] += dk[e * BLK : (e + 1) * BLK, :]

        over_pairs(grads, (count + 1) // 2)
        for h in range(GRP):
            for n in heads:
                cols = slice(h * BLK, (h + 1) * BLK)
                dq_ref[:, n * QW + h * HD : n * QW + (h + 1) * HD] = (dqt_st[n, :, cols] * SCALE).astype(LOW).T

    one_block(0, 2 * y + c, q_own, g_own, dq_own)
    one_block(1, 2 * y + 1 - c, q_par, g_par, dq_par)
    for s in range(SLOTS):
        for n in heads:
            dk_out[s, :, n * HD : (n + 1) * HD] = (dk_acc[n, s] * SCALE).astype(LOW)


ROWS = GRP * BLK
OWN = pl.BlockSpec((BLK, NG * QW), lambda i, place, par, lab: (0, place[1] * (HALF // NG) + i))
PARTNER = pl.BlockSpec((BLK, NG * QW), lambda i, place, par, lab: (0, i))
KEYS = pl.BlockSpec((SLOTS, 2, BLK, NG * HD), lambda i, place, par, lab: (0, 0, 0, i))
GRADS = pl.BlockSpec((SLOTS, BLK, NG * HD), lambda i, place, par, lab: (0, 0, i))
STATS = pl.BlockSpec((NG, 2, 8, ROWS), lambda i, place, par, lab: (i, 0, 0, 0))
OWN_SHAPE = jax.ShapeDtypeStruct((BLK, 2 * HALF * QW), LOW)
PARTNER_SHAPE = jax.ShapeDtypeStruct((BLK, HALF * QW), LOW)
GRADS_SHAPE = jax.ShapeDtypeStruct((SLOTS, BLK, HALF * HD), LOW)
STATS_SHAPE = jax.ShapeDtypeStruct((HALF, 2, 8, ROWS), F32)


def attention_call(kernel, name, products, in_specs, out_specs, out_shape, scratch):
    return pl.pallas_call(
        kernel,
        grid_spec=pltpu.PrefetchScalarGridSpec(
            num_scalar_prefetch=3,
            grid=(HALF // NG,),
            in_specs=in_specs,
            out_specs=out_specs,
            scratch_shapes=[pltpu.SMEM((SLOTS,), jnp.int32)] + [pltpu.VMEM(*s) for s in scratch],
        ),
        out_shape=out_shape,
        compiler_params=pltpu.CompilerParams(dimension_semantics=("arbitrary",), vmem_limit_bytes=48 * 2**20),
        cost_estimate=pl.CostEstimate(
            flops=4 * products * 2 * HALF * ROWS * 2 * 4 * BLK * HD,
            bytes_accessed=8 * BLK * HALF * QW,
            transcendentals=HALF * ROWS * 2 * 4 * BLK,
        ),
        name=name,
    )


def forward(*args):
    return attention_call(
        forward_kernel, "tree_forward", 3,
        [OWN, PARTNER, OWN, PARTNER, KEYS],
        [OWN, PARTNER, GRADS, STATS],
        [OWN_SHAPE, PARTNER_SHAPE, GRADS_SHAPE, STATS_SHAPE],
        [
            ((NG, PAIRS, 2 * BLK, HD), LOW),
            ((NG, PAIRS, HD, 2 * BLK), LOW),
            ((NG, ROWS, HD), LOW),
            ((NG, ROWS, HD), LOW),
            ((NG, HD, ROWS), LOW),
            ((NG, PAIRS, 2 * BLK, ROWS), LOW),
            ((NG, 2 * BLK, ROWS), LOW),
            ((NG, 8, ROWS), F32),
            ((NG, PAIRS, 8, ROWS), F32),
            ((NG, 8, ROWS), F32),
            ((NG, HD, ROWS), F32),
            ((NG, SLOTS, BLK, HD), F32),
        ],
    )(*args)


def backward(*args):
    return attention_call(
        backward_kernel, "tree_backward", 4,
        [OWN, PARTNER, OWN, PARTNER, KEYS, STATS],
        [OWN, PARTNER, GRADS],
        [OWN_SHAPE, PARTNER_SHAPE, GRADS_SHAPE],
        [
            ((NG, 2 * BLK, HD), LOW),
            ((NG, 2 * BLK, HD), LOW),
            ((NG, HD, 2 * BLK), LOW),
            ((NG, ROWS, HD), LOW),
            ((NG, ROWS, HD), LOW),
            ((NG, 2 * BLK, ROWS), LOW),
            ((NG, HD, ROWS), F32),
            ((NG, SLOTS, BLK, HD), F32),
        ],
    )(*args)


def weight_kernel(place, x_own, x_other, dv, out):
    tokens = NZ * BLK
    c = place[1]
    own = dv[:, pl.ds(c, 1)].reshape(tokens, -1)
    other = dv[:, pl.ds(1 - c, 1)].reshape(tokens, -1)
    total = dot_tn(x_own[...].reshape(tokens, -1), own) + dot_tn(x_other[...].reshape(tokens, -1), other)
    out[...] = total.astype(LOW)


def weight_partial(place, x_own, x_other, dv):
    tall, wide, step = x_own.shape[2], dv.shape[3], 256
    x_spec = pl.BlockSpec((NZ, BLK, step), lambda i, place: (0, 0, i))
    return pl.pallas_call(
        weight_kernel,
        grid_spec=pltpu.PrefetchScalarGridSpec(
            num_scalar_prefetch=1,
            grid=(tall // step,),
            in_specs=[x_spec, x_spec, pl.BlockSpec((NZ, 2, BLK, wide), lambda i, place: (0, 0, 0, 0))],
            out_specs=pl.BlockSpec((step, wide), lambda i, place: (i, 0)),
        ),
        out_shape=jax.ShapeDtypeStruct((tall, wide), LOW),
        cost_estimate=pl.CostEstimate(
            flops=2 * NZ * 2 * BLK * tall * wide, bytes_accessed=NZ * 2 * BLK * (tall + wide) * 2, transcendentals=0
        ),
        name="weight_partial",
    )(place, x_own, x_other, dv)


def kv_kernel(k, v, out):
    for half in range(2):
        at = slice(half * HALF * HD, (half + 1) * HALF * HD)
        out[half, 0] = k[:, at]
        out[half, 1] = v[:, at]


def kv_sends(k, v):
    width = HALF * HD
    row = pl.BlockSpec((BLK, 2 * width), lambda i: (0, 0))
    return pl.pallas_call(
        kv_kernel,
        grid=(NY,),
        in_specs=[row, row],
        out_specs=pl.BlockSpec((2, 2, BLK, width), lambda i: (i, 0, 0, 0)),
        out_shape=jax.ShapeDtypeStruct((SLOTS, 2, BLK, width), LOW),
        name="kv_sends",
    )(k, v)


def x_kernel(x, out):
    piece = x.shape[1] // (NX * NZ)
    for j in range(NZ):
        for i in range(NX):
            at = (i * NZ + j) * piece
            out[j, :, i * piece : (i + 1) * piece] = x[:, at : at + piece]


def x_sends(x):
    return pl.pallas_call(
        x_kernel,
        out_shape=jax.ShapeDtypeStruct((NZ, BLK, x.shape[1] // NZ), LOW),
        name="x_sends",
    )(x)


def sum_kernel(terms, out):
    for e in range(2):
        acc = terms[0, e].astype(F32)
        for i in range(1, NY):
            acc = acc + terms[i, e].astype(F32)
        for i in range(NZ):
            out[i, e] = acc.astype(LOW)


def sum_blocks(terms):
    return pl.pallas_call(
        sum_kernel, out_shape=jax.ShapeDtypeStruct((NZ,) + terms.shape[1:], LOW), name="sum_blocks"
    )(terms)


def finish_kernel(parts, out):
    width = parts.shape[2]
    for half in range(2):
        acc = parts[half].astype(F32)
        for i in range(1, NX * NY):
            acc = acc + parts[2 * i + half].astype(F32)
        out[:, half * width : (half + 1) * width] = acc * (16 * SLOTS * BLK) ** -0.5


def finish_weight(parts):
    rows, width = parts.shape[1:]
    return pl.pallas_call(
        finish_kernel, out_shape=jax.ShapeDtypeStruct((rows, 2 * width), F32), name="finish_weight"
    )(parts)


def device(x, z, y, c):
    return (x * NZ + z) * SLOTS + y * 2 + c


def per_device(query_rows, key_rows, value_rows, layer_input, out_grad, parents, labels):
    ctx = lax.axis_index("ctx")
    y, c = ctx // 2, ctx % 2
    place = jnp.stack([y, c]).astype(jnp.int32)
    q, k, v, g, x = query_rows[0], key_rows[0], value_rows[0], out_grad[0], layer_input[0]
    along_y = [[2 * m + n for m in range(NY)] for n in range(2)]
    along_z = [[i * NZ + j for j in range(NZ)] for i in range(NX)]
    across = [[device(i, j, m, n) for i in range(NX) for m in range(NY) for n in range(2)] for j in range(NZ)]

    def swap(a):
        return lax.ppermute(a, "ctx", [(i, i ^ 1) for i in range(SLOTS)])

    def earlier(a, d):
        return lax.ppermute(a, "ctx", [(i + 2 * d, i) for i in range(SLOTS - 2 * d)])

    def cols(a, start, width):
        return lax.dynamic_slice_in_dim(a, start, width, 1)

    def pick(a, i):
        return lax.dynamic_index_in_dim(a, i, 0, keepdims=False)

    at = (1 - c) * HALF * QW
    kv = lax.all_to_all(kv_sends(k, v), "ctx", 0, 0)
    q_par = swap(cols(q, at, HALF * QW))
    g_par = swap(cols(g, at, HALF * QW))
    x, _ = lax.optimization_barrier((x, kv))
    x_own = lax.all_to_all(x_sends(x), "dp", 0, 0, axis_index_groups=along_z)
    o_own, o_par, dv, stats = forward(place, parents, labels, q, q_par, g, g_par, kv)
    dv, x_own = lax.optimization_barrier((dv, x_own))
    dv = lax.all_to_all(dv.reshape(NY, 2, BLK, HALF * HD), "ctx", 0, 0, axis_index_groups=along_y)
    x_other = swap(x_own)
    o_swapped = swap(o_par)
    dq_own, dq_par, dk = backward(place, parents, labels, q, q_par, g, g_par, kv, stats)
    dv, dk = lax.optimization_barrier((dv, dk))
    dv_sends = sum_blocks(dv)
    dv_all = lax.all_to_all(dv_sends, "dp", 0, 0, axis_index_groups=along_z)
    dk = dk.reshape(NY, 2, BLK, HALF * HD)
    dk_sum = pick(dk, y).astype(F32)
    for d in range(1, NY):
        dk_sum = dk_sum + earlier(pick(dk, jnp.maximum(y - d, 0)), d).astype(F32)
    dk_sum = dk_sum.astype(LOW)
    partial = weight_partial(place, x_own, x_other, dv_all).reshape(2 * NX * NY, -1, HALF * HD)
    weight_grad = finish_weight(lax.all_to_all(partial, ("dp", "ctx"), 0, 0, axis_index_groups=across))
    out = lax.dynamic_update_slice_in_dim(o_own, o_swapped, at, 1)
    query_grad = lax.dynamic_update_slice_in_dim(dq_own, swap(dq_par), at, 1)
    both = jnp.stack([dk_sum, dv_sends[0]], axis=1)
    mine, other = pick(both, c), swap(pick(both, 1 - c))
    both = jnp.concatenate([jnp.where(c == 0, mine, other), jnp.where(c == 0, other, mine)], axis=-1)
    return out[None], query_grad[None], both[0][None], both[1][None], weight_grad


def solution(mesh):
    rows = P("dp", "ctx", None)
    return jax.shard_map(
        per_device,
        mesh=mesh,
        in_specs=(rows,) * 5 + (P("dp", None), P("dp", None)),
        out_specs=(rows,) * 4 + (P(("dp", "ctx"), None),),
        check_vma=False,
    )
```

```python
import jax
import jax.numpy as jnp
from jax import lax
from jax.experimental import pallas as pl
from jax.experimental.pallas import tpu as pltpu
from jax.sharding import PartitionSpec as P

HD = 128
BLK = 128
GRP = 8
NY = 4
NZ = 4
NX = 4
HALF = 4
QW = GRP * HD
SLOTS = 2 * NY
PAIRS = 4
NG = 2
LOW = jnp.bfloat16
F32 = jnp.float32
SCALE = HD**-0.5
EXP_SCALE = SCALE * 1.4426950408889634
MASKED = -1e30


def dot_nt(a, b):
    return lax.dot_general(a, b, (((1,), (1,)), ((), ())), preferred_element_type=F32)


def dot_nn(a, b):
    return lax.dot_general(a, b, (((1,), (0,)), ((), ())), preferred_element_type=F32)


def dot_tn(a, b):
    return lax.dot_general(a, b, (((0,), (0,)), ((), ())), preferred_element_type=F32)


def walk(parents, block, chain):
    def above(step, carry):
        current, count = carry
        parent = parents[0, current]
        more = parent != current
        current = jnp.where(more, parent, current)
        chain[step + 1] = current
        return current, count + more.astype(jnp.int32)

    chain[0] = block
    return lax.fori_loop(0, SLOTS - 1, above, (block, jnp.int32(1)))[1]


def fold(a, op):
    while a.shape[0] > 8:
        half = a.shape[0] // 2
        a = op(a[:half], a[half:])
    return a


def causal_mask():
    key_pos = lax.broadcasted_iota(jnp.int32, (BLK, BLK), 0)
    query_pos = lax.broadcasted_iota(jnp.int32, (BLK, BLK), 1)
    causal = jnp.where(key_pos <= query_pos, 0.0, MASKED).astype(F32)
    return jnp.concatenate([causal] * GRP, axis=1)


def block_sign(labels, block):
    return jnp.full((BLK, HD), jnp.where(labels[0, block] == 2, -1.0, 1.0), F32).astype(LOW)


def masked(s, t, count, first, causal):
    second = jnp.where(2 * t + 1 < count, 0.0, MASKED).astype(F32)
    s_a = s[:BLK]
    if first:
        s_a = s_a + causal
    return s_a, s[BLK:] + second


def over_pairs(step, pairs):
    def more(t, carry):
        step(t, False)
        return carry

    step(0, True)
    lax.fori_loop(1, pairs, more, 0)


def forward_kernel(
    place, parents, labels,
    q_own, q_par, g_own, g_par, kv,
    o_own, o_par, dv_out, stats,
    chain, k_pair, vt_pair, q_st, g_st, gt_st, p_st, w_st, m_st, mt_st, l_st, ot_st, dv_acc,
):
    y = place[0]
    c = place[1]
    heads = range(NG)
    dv_acc[...] = jnp.zeros_like(dv_acc)
    causal = causal_mask()

    def one_block(which, block, q_ref, g_ref, o_ref):
        count = walk(parents, block, chain)
        pairs = (count + 1) // 2
        sign = block_sign(labels, block)
        for n in heads:
            for h in range(GRP):
                rows = slice(h * BLK, (h + 1) * BLK)
                cols = slice(n * QW + h * HD, n * QW + (h + 1) * HD)
                q_st[n, rows, :] = q_ref[:, cols]
                g = g_ref[:, cols] * sign
                g_st[n, rows, :] = g
                gt_st[n, :, rows] = g.T

        def scores(t, first):
            for n in heads:
                for e in range(2):
                    s = chain[2 * t + e]
                    rows = slice(e * BLK, (e + 1) * BLK)
                    k_pair[n, t, rows, :] = kv[s, 0, :, n * HD : (n + 1) * HD]
                    vt_pair[n, t, :, rows] = kv[s, 1, :, n * HD : (n + 1) * HD].T
            for n in heads:
                s_a, s_b = masked(dot_nt(k_pair[n, t], q_st[n]), t, count, first, causal)
                top = jnp.max(fold(jnp.maximum(s_a, s_b), jnp.maximum), axis=0, keepdims=True)
                if not first:
                    old = m_st[n, 0:1, :]
                    top = jnp.maximum(top, old)
                    alpha = jnp.exp2((old - top) * EXP_SCALE)
                p_a = jnp.exp2((s_a - top) * EXP_SCALE)
                p_b = jnp.exp2((s_b - top) * EXP_SCALE)
                p_low = jnp.concatenate([p_a.astype(LOW), p_b.astype(LOW)], axis=0)
                p_st[n, t] = p_low
                total = fold(p_a + p_b, jnp.add)
                out = dot_nn(vt_pair[n, t], p_low)
                if first:
                    l_st[n] = total
                    ot_st[n] = out
                else:
                    l_st[n] = l_st[n] * alpha + total
                    ot_st[n] = ot_st[n] * alpha + out
                m_st[n, 0:1, :] = top
                mt_st[n, t, 0:1, :] = top

        over_pairs(scores, pairs)
        for n in heads:
            total = jnp.sum(l_st[n], axis=0, keepdims=True)
            l_st[n, 0:1, :] = 1.0 / total
            stats[n, which, 0:1, :] = m_st[n, 0:1, :] * EXP_SCALE + jnp.log2(total)
        for h in range(GRP):
            for n in heads:
                cols = slice(h * BLK, (h + 1) * BLK)
                out = (ot_st[n, :, cols] * l_st[n, 0:1, cols]).astype(LOW)
                o_ref[:, n * QW + h * HD : n * QW + (h + 1) * HD] = out.T
                stats[n, which, 1:2, cols] = jnp.sum(
                    gt_st[n, :, cols].astype(F32) * out.astype(F32), axis=0, keepdims=True
                )

        def values(t, first):
            for n in heads:
                f = jnp.exp2((mt_st[n, t, 0:1, :] - m_st[n, 0:1, :]) * EXP_SCALE) * l_st[n, 0:1, :]
                w_st[n] = (p_st[n, t].astype(F32) * f).astype(LOW)
            for n in heads:
                dv = dot_nn(w_st[n], g_st[n])
                for e in range(2):
                    dv_acc[n, chain[2 * t + e]] += dv[e * BLK : (e + 1) * BLK, :]

        over_pairs(values, pairs)

    one_block(0, 2 * y + c, q_own, g_own, o_own)
    one_block(1, 2 * y + 1 - c, q_par, g_par, o_par)
    for s in range(SLOTS):
        for n in heads:
            dv_out[s, :, n * HD : (n + 1) * HD] = dv_acc[n, s].astype(LOW)


def backward_kernel(
    place, parents, labels,
    q_own, q_par, g_own, g_par, kv, stats,
    dq_own, dq_par, dk_out,
    chain, k_pair, v_pair, kt_pair, q_st, g_st, ds_st, dqt_st, dk_acc,
):
    y = place[0]
    c = place[1]
    heads = range(NG)
    dk_acc[...] = jnp.zeros_like(dk_acc)
    causal = causal_mask()

    def one_block(which, block, q_ref, g_ref, dq_ref):
        count = walk(parents, block, chain)
        sign = block_sign(labels, block)
        for n in heads:
            for h in range(GRP):
                rows = slice(h * BLK, (h + 1) * BLK)
                cols = slice(n * QW + h * HD, n * QW + (h + 1) * HD)
                q_st[n, rows, :] = q_ref[:, cols]
                g_st[n, rows, :] = g_ref[:, cols] * sign

        def grads(t, first):
            for n in heads:
                for e in range(2):
                    s = chain[2 * t + e]
                    rows = slice(e * BLK, (e + 1) * BLK)
                    k = kv[s, 0, :, n * HD : (n + 1) * HD]
                    k_pair[n, rows, :] = k
                    kt_pair[n, :, rows] = k.T
                    v_pair[n, rows, :] = kv[s, 1, :, n * HD : (n + 1) * HD]
            for n in heads:
                s_a, s_b = masked(dot_nt(k_pair[n], q_st[n]), t, count, first, causal)
                dp = dot_nt(v_pair[n], g_st[n])
                lse, inner = stats[n, which, 0:1, :], stats[n, which, 1:2, :]
                ds_a = jnp.exp2(s_a * EXP_SCALE - lse) * (dp[:BLK] - inner)
                ds_b = jnp.exp2(s_b * EXP_SCALE - lse) * (dp[BLK:] - inner)
                ds = jnp.concatenate([ds_a.astype(LOW), ds_b.astype(LOW)], axis=0)
                ds_st[n] = ds
                dq = dot_nn(kt_pair[n], ds)
                if first:
                    dqt_st[n] = dq
                else:
                    dqt_st[n] += dq
            for n in heads:
                dk = dot_nn(ds_st[n], q_st[n])
                for e in range(2):
                    dk_acc[n, chain[2 * t + e]] += dk[e * BLK : (e + 1) * BLK, :]

        over_pairs(grads, (count + 1) // 2)
        for h in range(GRP):
            for n in heads:
                cols = slice(h * BLK, (h + 1) * BLK)
                dq_ref[:, n * QW + h * HD : n * QW + (h + 1) * HD] = (dqt_st[n, :, cols] * SCALE).astype(LOW).T

    one_block(0, 2 * y + c, q_own, g_own, dq_own)
    one_block(1, 2 * y + 1 - c, q_par, g_par, dq_par)
    for s in range(SLOTS):
        for n in heads:
            dk_out[s, :, n * HD : (n + 1) * HD] = (dk_acc[n, s] * SCALE).astype(LOW)


ROWS = GRP * BLK
OWN = pl.BlockSpec((BLK, NG * QW), lambda i, place, par, lab: (0, place[1] * (HALF // NG) + i))
PARTNER = pl.BlockSpec((BLK, NG * QW), lambda i, place, par, lab: (0, i))
KEYS = pl.BlockSpec((SLOTS, 2, BLK, NG * HD), lambda i, place, par, lab: (0, 0, 0, i))
GRADS = pl.BlockSpec((SLOTS, BLK, NG * HD), lambda i, place, par, lab: (0, 0, i))
STATS = pl.BlockSpec((NG, 2, 8, ROWS), lambda i, place, par, lab: (i, 0, 0, 0))
OWN_SHAPE = jax.ShapeDtypeStruct((BLK, 2 * HALF * QW), LOW)
PARTNER_SHAPE = jax.ShapeDtypeStruct((BLK, HALF * QW), LOW)
GRADS_SHAPE = jax.ShapeDtypeStruct((SLOTS, BLK, HALF * HD), LOW)
STATS_SHAPE = jax.ShapeDtypeStruct((HALF, 2, 8, ROWS), F32)


def attention_call(kernel, name, products, in_specs, out_specs, out_shape, scratch):
    return pl.pallas_call(
        kernel,
        grid_spec=pltpu.PrefetchScalarGridSpec(
            num_scalar_prefetch=3,
            grid=(HALF // NG,),
            in_specs=in_specs,
            out_specs=out_specs,
            scratch_shapes=[pltpu.SMEM((SLOTS,), jnp.int32)] + [pltpu.VMEM(*s) for s in scratch],
        ),
        out_shape=out_shape,
        compiler_params=pltpu.CompilerParams(dimension_semantics=("arbitrary",), vmem_limit_bytes=48 * 2**20),
        cost_estimate=pl.CostEstimate(
            flops=4 * products * 2 * HALF * ROWS * 2 * 4 * BLK * HD,
            bytes_accessed=8 * BLK * HALF * QW,
            transcendentals=HALF * ROWS * 2 * 4 * BLK,
        ),
        name=name,
    )


def forward(*args):
    return attention_call(
        forward_kernel, "tree_forward", 3,
        [OWN, PARTNER, OWN, PARTNER, KEYS],
        [OWN, PARTNER, GRADS, STATS],
        [OWN_SHAPE, PARTNER_SHAPE, GRADS_SHAPE, STATS_SHAPE],
        [
            ((NG, PAIRS, 2 * BLK, HD), LOW),
            ((NG, PAIRS, HD, 2 * BLK), LOW),
            ((NG, ROWS, HD), LOW),
            ((NG, ROWS, HD), LOW),
            ((NG, HD, ROWS), LOW),
            ((NG, PAIRS, 2 * BLK, ROWS), LOW),
            ((NG, 2 * BLK, ROWS), LOW),
            ((NG, 8, ROWS), F32),
            ((NG, PAIRS, 8, ROWS), F32),
            ((NG, 8, ROWS), F32),
            ((NG, HD, ROWS), F32),
            ((NG, SLOTS, BLK, HD), F32),
        ],
    )(*args)


def backward(*args):
    return attention_call(
        backward_kernel, "tree_backward", 4,
        [OWN, PARTNER, OWN, PARTNER, KEYS, STATS],
        [OWN, PARTNER, GRADS],
        [OWN_SHAPE, PARTNER_SHAPE, GRADS_SHAPE],
        [
            ((NG, 2 * BLK, HD), LOW),
            ((NG, 2 * BLK, HD), LOW),
            ((NG, HD, 2 * BLK), LOW),
            ((NG, ROWS, HD), LOW),
            ((NG, ROWS, HD), LOW),
            ((NG, 2 * BLK, ROWS), LOW),
            ((NG, HD, ROWS), F32),
            ((NG, SLOTS, BLK, HD), F32),
        ],
    )(*args)


def weight_kernel(place, *refs):
    x_own, x_other, dv, out = refs[:NZ], refs[NZ : 2 * NZ], refs[-2], refs[-1]
    c, z = place[1], place[2]
    total = None
    for d in range(NZ):
        src = lax.rem(z + NZ - d, NZ)
        x = jnp.concatenate([x_own[d][...], x_other[d][...]], axis=1)
        term = dot_nn(x, jnp.concatenate([dv[src, c], dv[src, 1 - c]], axis=0))
        total = term if total is None else total + term
    out[...] = total.astype(LOW)


def weight_partial(place, x_own, x_other, dv):
    tall, wide, step = x_own[0].shape[0], dv.shape[3], 512
    x_spec = pl.BlockSpec((step, BLK), lambda i, place: (i, 0))
    return pl.pallas_call(
        weight_kernel,
        grid_spec=pltpu.PrefetchScalarGridSpec(
            num_scalar_prefetch=1,
            grid=(tall // step,),
            in_specs=[x_spec] * (2 * NZ) + [pl.BlockSpec((NZ, 2, BLK, wide), lambda i, place: (0, 0, 0, 0))],
            out_specs=pl.BlockSpec((step, wide), lambda i, place: (i, 0)),
        ),
        out_shape=jax.ShapeDtypeStruct((tall, wide), LOW),
        cost_estimate=pl.CostEstimate(
            flops=2 * NZ * 2 * BLK * tall * wide, bytes_accessed=NZ * 2 * BLK * (tall + wide) * 2, transcendentals=0
        ),
        name="weight_partial",
    )(place, *x_own, *x_other, dv)


def kv_kernel(k, v, out):
    for half in range(2):
        at = slice(half * HALF * HD, (half + 1) * HALF * HD)
        out[half, 0] = k[:, at]
        out[half, 1] = v[:, at]


def kv_sends(k, v):
    width = HALF * HD
    row = pl.BlockSpec((BLK, 2 * width), lambda i: (0, 0))
    return pl.pallas_call(
        kv_kernel,
        grid=(NY,),
        in_specs=[row, row],
        out_specs=pl.BlockSpec((2, 2, BLK, width), lambda i: (i, 0, 0, 0)),
        out_shape=jax.ShapeDtypeStruct((SLOTS, 2, BLK, width), LOW),
        name="kv_sends",
    )(k, v)


def x_kernel(place, x, *outs):
    piece = x.shape[1] // (NX * NZ)
    for d in range(NZ):
        to = lax.rem(place[2] + d, NZ)
        for i in range(NX):
            at = pl.multiple_of((i * NZ + to) * piece, piece)
            outs[d][i * piece : (i + 1) * piece, :] = x[:, pl.ds(at, piece)].T


def x_sends(place, x):
    tall = x.shape[1] // NZ
    return pl.pallas_call(
        x_kernel,
        grid_spec=pltpu.PrefetchScalarGridSpec(
            num_scalar_prefetch=1,
            grid=(1,),
            in_specs=[pl.BlockSpec(x.shape, lambda i, place: (0, 0))],
            out_specs=[pl.BlockSpec((tall, BLK), lambda i, place: (0, 0))] * NZ,
        ),
        out_shape=[jax.ShapeDtypeStruct((tall, BLK), LOW)] * NZ,
        name="x_sends",
    )(place, x)


def sum_kernel(terms, out):
    for e in range(2):
        acc = terms[0, e].astype(F32)
        for i in range(1, NY):
            acc = acc + terms[i, e].astype(F32)
        for i in range(NZ):
            out[i, e] = acc.astype(LOW)


def sum_blocks(terms):
    return pl.pallas_call(
        sum_kernel, out_shape=jax.ShapeDtypeStruct((NZ,) + terms.shape[1:], LOW), name="sum_blocks"
    )(terms)


def finish_kernel(parts, out):
    width = parts.shape[2]
    for half in range(2):
        acc = parts[half].astype(F32)
        for i in range(1, NX * NY):
            acc = acc + parts[2 * i + half].astype(F32)
        out[:, half * width : (half + 1) * width] = acc * (16 * SLOTS * BLK) ** -0.5


def finish_weight(parts):
    rows, width = parts.shape[1:]
    return pl.pallas_call(
        finish_kernel, out_shape=jax.ShapeDtypeStruct((rows, 2 * width), F32), name="finish_weight"
    )(parts)


def device(x, z, y, c):
    return (x * NZ + z) * SLOTS + y * 2 + c


def per_device(query_rows, key_rows, value_rows, layer_input, out_grad, parents, labels):
    ctx = lax.axis_index("ctx")
    y, c, z = ctx // 2, ctx % 2, lax.axis_index("dp") % NZ
    place = jnp.stack([y, c, z]).astype(jnp.int32)
    q, k, v, g, x = query_rows[0], key_rows[0], value_rows[0], out_grad[0], layer_input[0]
    along_y = [[2 * m + n for m in range(NY)] for n in range(2)]
    along_z = [[i * NZ + j for j in range(NZ)] for i in range(NX)]
    across = [[device(i, j, m, n) for i in range(NX) for m in range(NY) for n in range(2)] for j in range(NZ)]

    def swap(a):
        return lax.ppermute(a, "ctx", [(i, i ^ 1) for i in range(SLOTS)])

    def cols(a, start, width):
        return lax.dynamic_slice_in_dim(a, start, width, 1)

    def pick(a, i):
        return lax.dynamic_index_in_dim(a, i, 0, keepdims=False)

    def further(a, d):
        return lax.ppermute(a, "dp", [(i, i // NZ * NZ + (i + d) % NZ) for i in range(NX * NZ)])

    at = (1 - c) * HALF * QW
    kv = lax.all_to_all(kv_sends(k, v), "ctx", 0, 0)
    q_par = swap(cols(q, at, HALF * QW))
    g_par = swap(cols(g, at, HALF * QW))
    x_own = x_sends(place, x)
    x_own = [x_own[0]] + [further(x_own[d], d) for d in range(1, NZ)]
    x_other = [swap(a) for a in x_own]
    kv, x_own, x_other = lax.optimization_barrier((kv, x_own, x_other))
    o_own, o_par, dv, stats = forward(place, parents, labels, q, q_par, g, g_par, kv)
    dv = lax.all_to_all(dv.reshape(NY, 2, BLK, HALF * HD), "ctx", 0, 0, axis_index_groups=along_y)
    o_swapped = swap(o_par)
    dq_own, dq_par, dk = backward(place, parents, labels, q, q_par, g, g_par, kv, stats)
    dv, dk = lax.optimization_barrier((dv, dk))
    dv_sends = sum_blocks(dv)
    dv_sends, dk, dq_par = lax.optimization_barrier((dv_sends, dk, dq_par))
    dv_all = lax.all_to_all(dv_sends, "dp", 0, 0, axis_index_groups=along_z)
    dk = dk.reshape(NY, 2, BLK, HALF * HD)
    dk_sum = lax.psum_scatter(dk, "ctx", scatter_dimension=0, axis_index_groups=along_y)
    partial = weight_partial(place, x_own, x_other, dv_all).reshape(2 * NX * NY, -1, HALF * HD)
    weight_grad = finish_weight(lax.all_to_all(partial, ("dp", "ctx"), 0, 0, axis_index_groups=across))
    out = lax.dynamic_update_slice_in_dim(o_own, o_swapped, at, 1)
    query_grad = lax.dynamic_update_slice_in_dim(dq_own, swap(dq_par), at, 1)
    both = jnp.stack([dk_sum, dv_sends[0]], axis=1)
    mine, other = pick(both, c), swap(pick(both, 1 - c))
    both = jnp.concatenate([jnp.where(c == 0, mine, other), jnp.where(c == 0, other, mine)], axis=-1)
    return out[None], query_grad[None], both[0][None], both[1][None], weight_grad


def solution(mesh):
    rows = P("dp", "ctx", None)
    return jax.shard_map(
        per_device,
        mesh=mesh,
        in_specs=(rows,) * 5 + (P("dp", None), P("dp", None)),
        out_specs=(rows,) * 4 + (P(("dp", "ctx"), None),),
        check_vma=False,
    )
```

```python
import jax
import jax.numpy as jnp
from jax import lax
from jax.experimental import pallas as pl
from jax.experimental.pallas import tpu as pltpu
from jax.sharding import PartitionSpec as P

HD = 128
BLK = 128
GRP = 8
NY = 4
NZ = 4
NX = 4
HALF = 4
QW = GRP * HD
SLOTS = 2 * NY
PAIRS = 4
NG = 2
LOW = jnp.bfloat16
F32 = jnp.float32
SCALE = HD**-0.5
EXP_SCALE = SCALE * 1.4426950408889634
MASKED = -1e30
LIGHT = pl.CostEstimate(flops=1, bytes_accessed=1, transcendentals=0)


def dot_nt(a, b):
    return lax.dot_general(a, b, (((1,), (1,)), ((), ())), preferred_element_type=F32)


def dot_nn(a, b):
    return lax.dot_general(a, b, (((1,), (0,)), ((), ())), preferred_element_type=F32)


def dot_tn(a, b):
    return lax.dot_general(a, b, (((0,), (0,)), ((), ())), preferred_element_type=F32)


def walk(parents, block, chain):
    def above(step, carry):
        current, count = carry
        parent = parents[0, current]
        more = parent != current
        current = jnp.where(more, parent, current)
        chain[step + 1] = current
        return current, count + more.astype(jnp.int32)

    chain[0] = block
    return lax.fori_loop(0, SLOTS - 1, above, (block, jnp.int32(1)))[1]


def fold(a, op):
    while a.shape[0] > 8:
        half = a.shape[0] // 2
        a = op(a[:half], a[half:])
    return a


def causal_mask():
    key_pos = lax.broadcasted_iota(jnp.int32, (BLK, BLK), 0)
    query_pos = lax.broadcasted_iota(jnp.int32, (BLK, BLK), 1)
    causal = jnp.where(key_pos <= query_pos, 0.0, MASKED).astype(F32)
    return jnp.concatenate([causal] * GRP, axis=1)


def block_sign(labels, block):
    return jnp.full((BLK, HD), jnp.where(labels[0, block] == 2, -1.0, 1.0), F32).astype(LOW)


def masked(s, t, count, first, causal):
    second = jnp.where(2 * t + 1 < count, 0.0, MASKED).astype(F32)
    s_a = s[:BLK]
    if first:
        s_a = s_a + causal
    return s_a, s[BLK:] + second


def over_pairs(step, pairs):
    def more(t, carry):
        step(t, False)
        return carry

    step(0, True)
    lax.fori_loop(1, pairs, more, 0)


def values_kernel(
    place, parents, labels,
    q_own, q_par, g_own, g_par, keys,
    dv_out, stats,
    chain, k_pair, q_st, g_st, p_st, w_st, m_st, mt_st, l_st, dv_acc,
):
    y = place[0]
    c = place[1]
    heads = range(NG)
    dv_acc[...] = jnp.zeros_like(dv_acc)
    causal = causal_mask()

    def one_block(which, block, q_ref, g_ref):
        count = walk(parents, block, chain)
        pairs = (count + 1) // 2
        sign = block_sign(labels, block)
        for n in heads:
            for h in range(GRP):
                rows = slice(h * BLK, (h + 1) * BLK)
                cols = slice(n * QW + h * HD, n * QW + (h + 1) * HD)
                q_st[n, rows, :] = q_ref[:, cols]
                g_st[n, rows, :] = g_ref[:, cols] * sign

        def scores(t, first):
            for n in heads:
                for e in range(2):
                    k_pair[n, e * BLK : (e + 1) * BLK, :] = keys[chain[2 * t + e], :, n * HD : (n + 1) * HD]
            for n in heads:
                s_a, s_b = masked(dot_nt(k_pair[n], q_st[n]), t, count, first, causal)
                top = jnp.max(fold(jnp.maximum(s_a, s_b), jnp.maximum), axis=0, keepdims=True)
                if not first:
                    old = m_st[n, 0:1, :]
                    top = jnp.maximum(top, old)
                    alpha = jnp.exp2((old - top) * EXP_SCALE)
                p_a = jnp.exp2((s_a - top) * EXP_SCALE)
                p_b = jnp.exp2((s_b - top) * EXP_SCALE)
                p_st[n, t] = jnp.concatenate([p_a.astype(LOW), p_b.astype(LOW)], axis=0)
                total = fold(p_a + p_b, jnp.add)
                if first:
                    l_st[n] = total
                else:
                    l_st[n] = l_st[n] * alpha + total
                m_st[n, 0:1, :] = top
                mt_st[n, t, 0:1, :] = top

        over_pairs(scores, pairs)
        for n in heads:
            total = jnp.sum(l_st[n], axis=0, keepdims=True)
            l_st[n, 0:1, :] = 1.0 / total
            stats[n, which, 0:1, :] = m_st[n, 0:1, :] * EXP_SCALE + jnp.log2(total)

        def values(t, first):
            for n in heads:
                f = jnp.exp2((mt_st[n, t, 0:1, :] - m_st[n, 0:1, :]) * EXP_SCALE) * l_st[n, 0:1, :]
                w_st[n] = (p_st[n, t].astype(F32) * f).astype(LOW)
            for n in heads:
                dv = dot_nn(w_st[n], g_st[n])
                for e in range(2):
                    dv_acc[n, chain[2 * t + e]] += dv[e * BLK : (e + 1) * BLK, :]

        over_pairs(values, pairs)

    one_block(0, 2 * y + c, q_own, g_own)
    one_block(1, 2 * y + 1 - c, q_par, g_par)
    for s in range(SLOTS):
        for n in heads:
            dv_out[s, :, n * HD : (n + 1) * HD] = dv_acc[n, s].astype(LOW)


def output_kernel(
    place, parents, labels,
    q_own, q_par, g_own, g_par, keys, vals, stats,
    o_own, o_par, dq_own, dq_par, dk_out,
    chain, k_pair, v_pair, kt_pair, vt_pair, q_st, g_st, gt_st, w_st, ds_st, in_st, ot_st, dqt_st, dk_acc,
):
    y = place[0]
    c = place[1]
    heads = range(NG)
    dk_acc[...] = jnp.zeros_like(dk_acc)
    causal = causal_mask()

    def one_block(which, block, q_ref, g_ref, o_ref, dq_ref):
        count = walk(parents, block, chain)
        pairs = (count + 1) // 2
        sign = block_sign(labels, block)
        for n in heads:
            for h in range(GRP):
                rows = slice(h * BLK, (h + 1) * BLK)
                cols = slice(n * QW + h * HD, n * QW + (h + 1) * HD)
                q_st[n, rows, :] = q_ref[:, cols]
                g = g_ref[:, cols] * sign
                g_st[n, rows, :] = g
                gt_st[n, :, rows] = g.T

        def outputs(t, first):
            for n in heads:
                for e in range(2):
                    s = chain[2 * t + e]
                    rows = slice(e * BLK, (e + 1) * BLK)
                    k = keys[s, :, n * HD : (n + 1) * HD]
                    v = vals[s, :, n * HD : (n + 1) * HD]
                    k_pair[n, t, rows, :] = k
                    v_pair[n, t, rows, :] = v
                    kt_pair[n, t, :, rows] = k.T
                    vt_pair[n, t, :, rows] = v.T
            for n in heads:
                s_a, s_b = masked(dot_nt(k_pair[n, t], q_st[n]), t, count, first, causal)
                lse = stats[n, which, 0:1, :]
                w_a = jnp.exp2(s_a * EXP_SCALE - lse).astype(LOW)
                w_b = jnp.exp2(s_b * EXP_SCALE - lse).astype(LOW)
                w = jnp.concatenate([w_a, w_b], axis=0)
                w_st[n, t] = w
                out = dot_nn(vt_pair[n, t], w)
                if first:
                    ot_st[n] = out
                else:
                    ot_st[n] += out

        over_pairs(outputs, pairs)
        for h in range(GRP):
            for n in heads:
                cols = slice(h * BLK, (h + 1) * BLK)
                out = ot_st[n, :, cols].astype(LOW)
                o_ref[:, n * QW + h * HD : n * QW + (h + 1) * HD] = out.T
                in_st[n, 0:1, cols] = jnp.sum(
                    gt_st[n, :, cols].astype(F32) * out.astype(F32), axis=0, keepdims=True
                )

        def grads(t, first):
            for n in heads:
                dp = dot_nn(v_pair[n, t], gt_st[n])
                ds = (w_st[n, t].astype(F32) * (dp - in_st[n, 0:1, :])).astype(LOW)
                ds_st[n] = ds
                dq = dot_nn(kt_pair[n, t], ds)
                if first:
                    dqt_st[n] = dq
                else:
                    dqt_st[n] += dq
            for n in heads:
                dk = dot_nn(ds_st[n], q_st[n])
                for e in range(2):
                    dk_acc[n, chain[2 * t + e]] += dk[e * BLK : (e + 1) * BLK, :]

        over_pairs(grads, pairs)
        for h in range(GRP):
            for n in heads:
                cols = slice(h * BLK, (h + 1) * BLK)
                dq_ref[:, n * QW + h * HD : n * QW + (h + 1) * HD] = (dqt_st[n, :, cols] * SCALE).astype(LOW).T

    one_block(0, 2 * y + c, q_own, g_own, o_own, dq_own)
    one_block(1, 2 * y + 1 - c, q_par, g_par, o_par, dq_par)
    for s in range(SLOTS):
        for n in heads:
            dk_out[s, :, n * HD : (n + 1) * HD] = (dk_acc[n, s] * SCALE).astype(LOW)


def output_onward_kernel(*refs):
    output_kernel(*refs[:10], *refs[13:])


ROWS = GRP * BLK


def attention_call(kernel, name, steps, in_specs, out_specs, out_shape, scratch, aliases={}):
    return pl.pallas_call(
        kernel,
        grid_spec=pltpu.PrefetchScalarGridSpec(
            num_scalar_prefetch=3,
            grid=(steps,),
            in_specs=in_specs,
            out_specs=out_specs,
            scratch_shapes=[pltpu.SMEM((SLOTS,), jnp.int32)] + [pltpu.VMEM(*s) for s in scratch],
        ),
        out_shape=out_shape,
        input_output_aliases=aliases,
        compiler_params=pltpu.CompilerParams(dimension_semantics=("arbitrary",), vmem_limit_bytes=48 * 2**20),
        cost_estimate=LIGHT,
        name=name,
    )


def own_spec(start):
    return pl.BlockSpec((BLK, NG * QW), lambda i, place, par, lab: (0, place[1] * (HALF // NG) + start + i))


def partner_spec(start):
    return pl.BlockSpec((BLK, NG * QW), lambda i, place, par, lab: (0, start + i))


def blocks_spec(start):
    return pl.BlockSpec((SLOTS, BLK, NG * HD), lambda i, place, par, lab: (0, 0, start + i))


def stats_spec(start):
    return pl.BlockSpec((NG, 2, 8, ROWS), lambda i, place, par, lab: (start + i, 0, 0, 0))


def value_gradient(*args):
    own, partner = own_spec(0), partner_spec(0)
    return attention_call(
        values_kernel, "tree_values", HALF // NG,
        [own, partner, own, partner, blocks_spec(0)],
        [blocks_spec(0), stats_spec(0)],
        [jax.ShapeDtypeStruct((SLOTS, BLK, HALF * HD), LOW), jax.ShapeDtypeStruct((HALF, 2, 8, ROWS), F32)],
        [
            ((NG, 2 * BLK, HD), LOW),
            ((NG, ROWS, HD), LOW),
            ((NG, ROWS, HD), LOW),
            ((NG, PAIRS, 2 * BLK, ROWS), LOW),
            ((NG, 2 * BLK, ROWS), LOW),
            ((NG, 8, ROWS), F32),
            ((NG, PAIRS, 8, ROWS), F32),
            ((NG, 8, ROWS), F32),
            ((NG, SLOTS, BLK, HD), F32),
        ],
    )(*args)


def output_and_gradients(start, before, *args):
    own, partner, partner_out = own_spec(start), partner_spec(start), partner_spec(0)
    own_shape = jax.ShapeDtypeStruct((BLK, 2 * HALF * QW), LOW)
    partner_shape = jax.ShapeDtypeStruct((BLK, NG * QW), LOW)
    return attention_call(
        output_onward_kernel if before else output_kernel, "tree_outputs", 1,
        [own, partner, own, partner, blocks_spec(start), blocks_spec(start), stats_spec(start)]
        + [pl.BlockSpec(memory_space=pl.ANY)] * len(before),
        [own, partner_out, own, partner_out, blocks_spec(start)],
        [own_shape, partner_shape, own_shape, partner_shape, jax.ShapeDtypeStruct((SLOTS, BLK, HALF * HD), LOW)],
        [
            ((NG, PAIRS, 2 * BLK, HD), LOW),
            ((NG, PAIRS, 2 * BLK, HD), LOW),
            ((NG, PAIRS, HD, 2 * BLK), LOW),
            ((NG, PAIRS, HD, 2 * BLK), LOW),
            ((NG, ROWS, HD), LOW),
            ((NG, ROWS, HD), LOW),
            ((NG, HD, ROWS), LOW),
            ((NG, PAIRS, 2 * BLK, ROWS), LOW),
            ((NG, 2 * BLK, ROWS), LOW),
            ((NG, 8, ROWS), F32),
            ((NG, HD, ROWS), F32),
            ((NG, HD, ROWS), F32),
            ((NG, SLOTS, BLK, HD), F32),
        ],
        {10: 0, 11: 2, 12: 4} if before else {},
    )(*args, *before)


def weight_kernel(place, *refs):
    x_own, x_other, dv, out, x_all = refs[:NZ], refs[NZ : 2 * NZ], refs[-3], refs[-2], refs[-1]
    c, z = place[1], place[2]
    for d in range(NZ):
        src = lax.rem(z + NZ - d, NZ)
        for x, core in ((x_own[d], c), (x_other[d], 1 - c)):
            x_all[:, pl.ds(pl.multiple_of((2 * src + core) * BLK, BLK), BLK)] = x[...]
    out[...] = dot_nn(x_all[...], dv[...].reshape(2 * NZ * BLK, -1)).astype(LOW)


def weight_partial(place, x_own, x_other, dv):
    tall, wide, step = x_own[0].shape[0], dv.shape[3], 256
    x_spec = pl.BlockSpec((step, BLK), lambda i, place: (i, 0))
    return pl.pallas_call(
        weight_kernel,
        grid_spec=pltpu.PrefetchScalarGridSpec(
            num_scalar_prefetch=1,
            grid=(tall // step,),
            in_specs=[x_spec] * (2 * NZ) + [pl.BlockSpec((NZ, 2, BLK, wide), lambda i, place: (0, 0, 0, 0))],
            out_specs=pl.BlockSpec((step, wide), lambda i, place: (i, 0)),
            scratch_shapes=[pltpu.VMEM((step, 2 * NZ * BLK), LOW)],
        ),
        out_shape=jax.ShapeDtypeStruct((tall, wide), LOW),
        compiler_params=pltpu.CompilerParams(vmem_limit_bytes=60 * 2**20),
        cost_estimate=LIGHT,
        name="weight_partial",
    )(place, *x_own, *x_other, dv)


def halves_kernel(rows, out, done):
    width = out.shape[2]
    copies = [
        pltpu.make_async_copy(rows.at[:, pl.ds(i % 2 * width, width)], out.at[i], done.at[i]) for i in range(SLOTS)
    ]
    for copy in copies:
        copy.start()
    for copy in copies:
        copy.wait()


def halves(rows):
    width = rows.shape[1] // 2
    return pl.pallas_call(
        halves_kernel,
        out_shape=jax.ShapeDtypeStruct((SLOTS, BLK, width), LOW),
        out_specs=pl.BlockSpec(memory_space=pl.ANY),
        scratch_shapes=[pltpu.SemaphoreType.DMA((SLOTS,))],
        cost_estimate=LIGHT,
        name="halves",
    )(rows)


def run_copies(pairs, done):
    copies = [pltpu.make_async_copy(a, b, done.at[i]) for i, (a, b) in enumerate(pairs)]
    for copy in copies:
        copy.start()
    for copy in copies:
        copy.wait()


def partner_kernel(place, q, g, q_out, g_out, done):
    width = HALF * QW
    at = pl.multiple_of((1 - place[1]) * width, width)
    step = BLK // 4
    pairs = []
    for a, b in ((q, q_out), (g, g_out)):
        for i in range(4):
            rows = pl.ds(i * step, step)
            pairs.append((a.at[rows, pl.ds(at, width)], b.at[rows, :]))
    run_copies(pairs, done)


def partner_halves(place, q, g):
    out = jax.ShapeDtypeStruct((BLK, HALF * QW), LOW)
    anywhere = pl.BlockSpec(memory_space=pl.ANY)
    return pl.pallas_call(
        partner_kernel,
        grid_spec=pltpu.PrefetchScalarGridSpec(
            num_scalar_prefetch=1,
            grid=(1,),
            in_specs=[anywhere] * 2,
            out_specs=[anywhere] * 2,
            scratch_shapes=[pltpu.SemaphoreType.DMA((8,))],
        ),
        out_shape=[out, out],
        cost_estimate=LIGHT,
        name="partner_halves",
    )(place, q, g)


def fill_kernel(place, o_before, dq_before, o_a, o_b, dq_a, dq_b, o_all, dq_all, done):
    width = NG * QW
    pairs = []
    for whole, parts in ((o_all, (o_a, o_b)), (dq_all, (dq_a, dq_b))):
        for i, part in enumerate(parts):
            at = pl.multiple_of((1 - place[1]) * HALF * QW + i * width, width)
            for j in range(2):
                rows = pl.ds(j * BLK // 2, BLK // 2)
                pairs.append((part.at[rows, :], whole.at[rows, pl.ds(at, width)]))
    run_copies(pairs, done)


def fill_partner(place, o_all, dq_all, o_parts, dq_parts):
    anywhere = pl.BlockSpec(memory_space=pl.ANY)
    return pl.pallas_call(
        fill_kernel,
        grid_spec=pltpu.PrefetchScalarGridSpec(
            num_scalar_prefetch=1,
            grid=(1,),
            in_specs=[anywhere] * 6,
            out_specs=[anywhere] * 2,
            scratch_shapes=[pltpu.SemaphoreType.DMA((8,))],
        ),
        out_shape=[jax.ShapeDtypeStruct(o_all.shape, LOW)] * 2,
        input_output_aliases={1: 0, 2: 1},
        cost_estimate=LIGHT,
        name="fill_partner",
    )(place, o_all, dq_all, *o_parts, *dq_parts)


def split_kernel(place, dk, r1, r2, r3, dv, after, mine, other):
    c = place[1]
    for out, e in ((mine, c), (other, 1 - c)):
        acc = dk[0, e].astype(F32)
        for r in (r1, r2, r3):
            acc = acc + r[e].astype(F32)
        out[0] = acc.astype(LOW)
        out[1] = dv[0, e]


def split_grads(place, dk, received, dv, after):
    width = dk.shape[3]
    pair = pl.BlockSpec((2, BLK, width), lambda i, place: (0, 0, 0))
    return pl.pallas_call(
        split_kernel,
        grid_spec=pltpu.PrefetchScalarGridSpec(
            num_scalar_prefetch=1,
            grid=(1,),
            in_specs=[pl.BlockSpec((1, 2, BLK, width), lambda i, place: (place[0], 0, 0, 0))]
            + [pair] * 3
            + [pl.BlockSpec((1, 2, BLK, width), lambda i, place: (0, 0, 0, 0)), pl.BlockSpec(memory_space=pl.ANY)],
            out_specs=[pair, pair],
        ),
        out_shape=[jax.ShapeDtypeStruct((2, BLK, width), LOW)] * 2,
        cost_estimate=LIGHT,
        name="split_grads",
    )(place, dk, *received, dv, after)


def join_kernel(place, mine, other, key_grad, value_grad):
    width = mine.shape[2]
    for i, out in enumerate((key_grad, value_grad)):
        out[:, pl.ds(pl.multiple_of(place[1] * width, width), width)] = mine[i]
        out[:, pl.ds(pl.multiple_of((1 - place[1]) * width, width), width)] = other[i]


def join_grads(place, mine, other):
    width = mine.shape[2]
    pair = pl.BlockSpec((2, BLK, width), lambda i, place: (0, 0, 0))
    rows = pl.BlockSpec((BLK, 2 * width), lambda i, place: (0, 0))
    return pl.pallas_call(
        join_kernel,
        grid_spec=pltpu.PrefetchScalarGridSpec(
            num_scalar_prefetch=1, grid=(1,), in_specs=[pair, pair], out_specs=[rows, rows]
        ),
        out_shape=[jax.ShapeDtypeStruct((BLK, 2 * width), LOW)] * 2,
        cost_estimate=LIGHT,
        name="join_grads",
    )(place, mine, other)


def x_kernel(place, x, *outs):
    piece = x.shape[1] // (NX * NZ)
    for d in range(NZ):
        to = lax.rem(place[2] + d, NZ)
        for i in range(NX):
            at = pl.multiple_of((i * NZ + to) * piece, piece)
            outs[d][i * piece : (i + 1) * piece, :] = x[:, pl.ds(at, piece)].T


def x_sends(place, x):
    tall = x.shape[1] // NZ
    return pl.pallas_call(
        x_kernel,
        grid_spec=pltpu.PrefetchScalarGridSpec(
            num_scalar_prefetch=1,
            grid=(1,),
            in_specs=[pl.BlockSpec(x.shape, lambda i, place: (0, 0))],
            out_specs=[pl.BlockSpec((tall, BLK), lambda i, place: (0, 0))] * NZ,
        ),
        out_shape=[jax.ShapeDtypeStruct((tall, BLK), LOW)] * NZ,
        cost_estimate=LIGHT,
        name="x_sends",
    )(place, x)


def sum_kernel(terms, out, total, done):
    for e in range(2):
        acc = terms[0, e].astype(F32)
        for i in range(1, NY):
            acc = acc + terms[i, e].astype(F32)
        total[e] = acc.astype(LOW)
    copies = [pltpu.make_async_copy(total, out.at[i], done.at[i]) for i in range(NZ)]
    for copy in copies:
        copy.start()
    for copy in copies:
        copy.wait()


def sum_blocks(terms):
    return pl.pallas_call(
        sum_kernel,
        out_shape=jax.ShapeDtypeStruct((NZ,) + terms.shape[1:], LOW),
        out_specs=pl.BlockSpec(memory_space=pl.ANY),
        scratch_shapes=[pltpu.VMEM(terms.shape[1:], LOW), pltpu.SemaphoreType.DMA((NZ,))],
        compiler_params=pltpu.CompilerParams(vmem_limit_bytes=60 * 2**20),
        cost_estimate=LIGHT,
        name="sum_blocks",
    )(terms)


def finish_kernel(parts, out):
    width = parts.shape[2]
    for half in range(2):
        acc = parts[half].astype(F32)
        for i in range(1, NX * NY):
            acc = acc + parts[2 * i + half].astype(F32)
        out[:, half * width : (half + 1) * width] = acc * (16 * SLOTS * BLK) ** -0.5


def finish_weight(parts):
    rows, width = parts.shape[1:]
    return pl.pallas_call(
        finish_kernel,
        out_shape=jax.ShapeDtypeStruct((rows, 2 * width), F32),
        compiler_params=pltpu.CompilerParams(vmem_limit_bytes=60 * 2**20),
        cost_estimate=LIGHT,
        name="finish_weight",
    )(parts)


def device(x, z, y, c):
    return (x * NZ + z) * SLOTS + y * 2 + c


def per_device(query_rows, key_rows, value_rows, layer_input, out_grad, parents, labels):
    ctx = lax.axis_index("ctx")
    y, c, z = ctx // 2, ctx % 2, lax.axis_index("dp") % NZ
    place = jnp.stack([y, c, z]).astype(jnp.int32)
    q, k, v, g, x = query_rows[0], key_rows[0], value_rows[0], out_grad[0], layer_input[0]
    along_y = [[2 * m + n for m in range(NY)] for n in range(2)]
    along_z = [[i * NZ + j for j in range(NZ)] for i in range(NX)]
    across = [[device(i, j, m, n) for i in range(NX) for m in range(NY) for n in range(2)] for j in range(NZ)]

    def swap(a):
        return lax.ppermute(a, "ctx", [(i, i ^ 1) for i in range(SLOTS)])

    def pick(a, i):
        return lax.dynamic_index_in_dim(a, i, 0, keepdims=False)

    def further(a, d):
        return lax.ppermute(a, "dp", [(i, i // NZ * NZ + (i + d) % NZ) for i in range(NX * NZ)])

    def earlier(a, d):
        return lax.ppermute(a, "ctx", [(i + 2 * d, i) for i in range(SLOTS - 2 * d)])

    keys = lax.all_to_all(halves(k), "ctx", 0, 0)
    q_par, g_par = [swap(a) for a in partner_halves(place, q, g)]
    x_own = x_sends(place, x)
    v_sends = halves(v)
    x_own = [x_own[0]] + [further(x_own[d], d) for d in range(1, NZ)]
    keys, v_sends, x_own[1], x_own[3] = lax.optimization_barrier((keys, v_sends, x_own[1], x_own[3]))
    vals = lax.all_to_all(v_sends, "ctx", 0, 0)
    dv, stats = value_gradient(place, parents, labels, q, q_par, g, g_par, keys)
    dv, vals, x_own = lax.optimization_barrier((dv, vals, x_own))
    dv = lax.all_to_all(dv.reshape(NY, 2, BLK, HALF * HD), "ctx", 0, 0, axis_index_groups=along_y)
    args = (place, parents, labels, q, q_par, g, g_par, keys, vals, stats)
    o_own, o_par, dq_own, dq_par, dk = output_and_gradients(0, (), *args)
    o_pars, dq_pars = [o_par], [dq_par]
    dv, dk, x_own = lax.optimization_barrier((dv, dk, x_own))
    x_other = [swap(a) for a in x_own]
    dv_sends = sum_blocks(dv)
    dv_sends, dk = lax.optimization_barrier((dv_sends, dk))
    dv_all = lax.all_to_all(dv_sends, "dp", 0, 0, axis_index_groups=along_z)
    o_own, o_par, dq_own, dq_par, dk = output_and_gradients(1, (o_own, dq_own, dk), *args)
    o_pars, dq_pars = o_pars + [o_par], dq_pars + [dq_par]
    dk = dk.reshape(NY, 2, BLK, HALF * HD)
    received = [earlier(pick(dk, jnp.maximum(y - d, 0)), d) for d in range(1, NY)]
    partial = weight_partial(place, x_own, x_other, dv_all).reshape(2 * NX * NY, -1, HALF * HD)
    after, o_pars, dq_pars = lax.optimization_barrier((partial, o_pars, dq_pars))
    o_pars, dq_pars = [swap(a) for a in o_pars], [swap(a) for a in dq_pars]
    weight_grad = finish_weight(lax.all_to_all(partial, ("dp", "ctx"), 0, 0, axis_index_groups=across))
    out, query_grad = fill_partner(place, o_own, dq_own, o_pars, dq_pars)
    mine, other = split_grads(place, dk, received, dv_sends, after)
    key_grad, value_grad = join_grads(place, mine, swap(other))
    return out[None], query_grad[None], key_grad[None], value_grad[None], weight_grad


def solution(mesh):
    rows = P("dp", "ctx", None)
    return jax.shard_map(
        per_device,
        mesh=mesh,
        in_specs=(rows,) * 5 + (P("dp", None), P("dp", None)),
        out_specs=(rows,) * 4 + (P(("dp", "ctx"), None),),
        check_vma=False,
    )
```

```python
import jax
import jax.numpy as jnp
from jax import lax
from jax.experimental import pallas as pl
from jax.experimental.pallas import tpu as pltpu
from jax.sharding import PartitionSpec as P

HD = 128
BLK = 128
GRP = 8
NY = 4
NZ = 4
NX = 4
HALF = 4
QW = GRP * HD
SLOTS = 2 * NY
PAIRS = 4
NG = 2
LOW = jnp.bfloat16
F32 = jnp.float32
SCALE = HD**-0.5
EXP_SCALE = SCALE * 1.4426950408889634
MASKED = -1e30
LIGHT = pl.CostEstimate(flops=1, bytes_accessed=1, transcendentals=0)


def dot_nt(a, b):
    return lax.dot_general(a, b, (((1,), (1,)), ((), ())), preferred_element_type=F32)


def dot_nn(a, b):
    return lax.dot_general(a, b, (((1,), (0,)), ((), ())), preferred_element_type=F32)


def dot_tn(a, b):
    return lax.dot_general(a, b, (((0,), (0,)), ((), ())), preferred_element_type=F32)


def walk(parents, block, chain):
    def above(step, carry):
        current, count = carry
        parent = parents[0, current]
        more = parent != current
        current = jnp.where(more, parent, current)
        chain[step + 1] = current
        return current, count + more.astype(jnp.int32)

    chain[0] = block
    return lax.fori_loop(0, SLOTS - 1, above, (block, jnp.int32(1)))[1]


def fold(a, op):
    while a.shape[0] > 8:
        half = a.shape[0] // 2
        a = op(a[:half], a[half:])
    return a


def causal_mask():
    key_pos = lax.broadcasted_iota(jnp.int32, (BLK, BLK), 0)
    query_pos = lax.broadcasted_iota(jnp.int32, (BLK, BLK), 1)
    causal = jnp.where(key_pos <= query_pos, 0.0, MASKED).astype(F32)
    return jnp.concatenate([causal] * GRP, axis=1)


def block_sign(labels, block):
    return jnp.full((BLK, HD), jnp.where(labels[0, block] == 2, -1.0, 1.0), F32).astype(LOW)


def masked(s, t, count, first, causal):
    second = jnp.where(2 * t + 1 < count, 0.0, MASKED).astype(F32)
    s_a = s[:BLK]
    if first:
        s_a = s_a + causal
    return s_a, s[BLK:] + second


def over_pairs(step, pairs):
    def more(t, carry):
        step(t, False)
        return carry

    step(0, True)
    lax.fori_loop(1, pairs, more, 0)


def values_kernel(
    place, parents, labels,
    q_own, q_par, g_own, g_par, keys,
    dv_out, stats,
    chain, k_pair, q_st, g_st, p_st, w_st, m_st, mt_st, l_st, dv_acc,
):
    y = place[0]
    c = place[1]
    heads = range(NG)
    dv_acc[...] = jnp.zeros_like(dv_acc)
    causal = causal_mask()

    def one_block(which, block, q_ref, g_ref):
        count = walk(parents, block, chain)
        pairs = (count + 1) // 2
        sign = block_sign(labels, block)
        for n in heads:
            for h in range(GRP):
                rows = slice(h * BLK, (h + 1) * BLK)
                cols = slice(n * QW + h * HD, n * QW + (h + 1) * HD)
                q_st[n, rows, :] = q_ref[:, cols]
                g_st[n, rows, :] = g_ref[:, cols] * sign

        def scores(t, first):
            for n in heads:
                for e in range(2):
                    k_pair[n, e * BLK : (e + 1) * BLK, :] = keys[chain[2 * t + e], :, n * HD : (n + 1) * HD]
            for n in heads:
                s_a, s_b = masked(dot_nt(k_pair[n], q_st[n]), t, count, first, causal)
                top = jnp.max(fold(jnp.maximum(s_a, s_b), jnp.maximum), axis=0, keepdims=True)
                if not first:
                    old = m_st[n, 0:1, :]
                    top = jnp.maximum(top, old)
                    alpha = jnp.exp2((old - top) * EXP_SCALE)
                p_a = jnp.exp2((s_a - top) * EXP_SCALE)
                p_b = jnp.exp2((s_b - top) * EXP_SCALE)
                p_st[n, t] = jnp.concatenate([p_a.astype(LOW), p_b.astype(LOW)], axis=0)
                total = fold(p_a + p_b, jnp.add)
                if first:
                    l_st[n] = total
                else:
                    l_st[n] = l_st[n] * alpha + total
                m_st[n, 0:1, :] = top
                mt_st[n, t, 0:1, :] = top

        over_pairs(scores, pairs)
        for n in heads:
            total = jnp.sum(l_st[n], axis=0, keepdims=True)
            l_st[n, 0:1, :] = 1.0 / total
            stats[n, which, 0:1, :] = m_st[n, 0:1, :] * EXP_SCALE + jnp.log2(total)

        def values(t, first):
            for n in heads:
                f = jnp.exp2((mt_st[n, t, 0:1, :] - m_st[n, 0:1, :]) * EXP_SCALE) * l_st[n, 0:1, :]
                w_st[n] = (p_st[n, t].astype(F32) * f).astype(LOW)
            for n in heads:
                dv = dot_nn(w_st[n], g_st[n])
                for e in range(2):
                    dv_acc[n, chain[2 * t + e]] += dv[e * BLK : (e + 1) * BLK, :]

        over_pairs(values, pairs)

    one_block(0, 2 * y + c, q_own, g_own)
    one_block(1, 2 * y + 1 - c, q_par, g_par)
    for s in range(SLOTS):
        for n in heads:
            dv_out[s, :, n * HD : (n + 1) * HD] = dv_acc[n, s].astype(LOW)


def output_kernel(
    place, parents, labels,
    q_own, q_par, g_own, g_par, keys, vals, stats,
    o_own, o_par, dq_own, dq_par, dk_out,
    chain, k_pair, v_pair, kt_pair, vt_pair, q_st, g_st, gt_st, w_st, ds_st, in_st, ot_st, dqt_st, dk_acc,
):
    y = place[0]
    c = place[1]
    heads = range(NG)
    dk_acc[...] = jnp.zeros_like(dk_acc)
    causal = causal_mask()

    def one_block(which, block, q_ref, g_ref, o_ref, dq_ref):
        count = walk(parents, block, chain)
        pairs = (count + 1) // 2
        sign = block_sign(labels, block)
        for n in heads:
            for h in range(GRP):
                rows = slice(h * BLK, (h + 1) * BLK)
                cols = slice(n * QW + h * HD, n * QW + (h + 1) * HD)
                q_st[n, rows, :] = q_ref[:, cols]
                g = g_ref[:, cols] * sign
                g_st[n, rows, :] = g
                gt_st[n, :, rows] = g.T

        def outputs(t, first):
            for n in heads:
                for e in range(2):
                    s = chain[2 * t + e]
                    rows = slice(e * BLK, (e + 1) * BLK)
                    k = keys[s, :, n * HD : (n + 1) * HD]
                    v = vals[s, :, n * HD : (n + 1) * HD]
                    k_pair[n, t, rows, :] = k
                    v_pair[n, t, rows, :] = v
                    kt_pair[n, t, :, rows] = k.T
                    vt_pair[n, t, :, rows] = v.T
            for n in heads:
                s_a, s_b = masked(dot_nt(k_pair[n, t], q_st[n]), t, count, first, causal)
                lse = stats[n, which, 0:1, :]
                w_a = jnp.exp2(s_a * EXP_SCALE - lse).astype(LOW)
                w_b = jnp.exp2(s_b * EXP_SCALE - lse).astype(LOW)
                w = jnp.concatenate([w_a, w_b], axis=0)
                w_st[n, t] = w
                out = dot_nn(vt_pair[n, t], w)
                if first:
                    ot_st[n] = out
                else:
                    ot_st[n] += out

        over_pairs(outputs, pairs)
        for h in range(GRP):
            for n in heads:
                cols = slice(h * BLK, (h + 1) * BLK)
                out = ot_st[n, :, cols].astype(LOW)
                o_ref[:, n * QW + h * HD : n * QW + (h + 1) * HD] = out.T
                in_st[n, 0:1, cols] = jnp.sum(
                    gt_st[n, :, cols].astype(F32) * out.astype(F32), axis=0, keepdims=True
                )

        def grads(t, first):
            for n in heads:
                dp = dot_nn(v_pair[n, t], gt_st[n])
                ds = (w_st[n, t].astype(F32) * (dp - in_st[n, 0:1, :])).astype(LOW)
                ds_st[n] = ds
                dq = dot_nn(kt_pair[n, t], ds)
                if first:
                    dqt_st[n] = dq
                else:
                    dqt_st[n] += dq
            for n in heads:
                dk = dot_nn(ds_st[n], q_st[n])
                for e in range(2):
                    dk_acc[n, chain[2 * t + e]] += dk[e * BLK : (e + 1) * BLK, :]

        over_pairs(grads, pairs)
        for h in range(GRP):
            for n in heads:
                cols = slice(h * BLK, (h + 1) * BLK)
                dq_ref[:, n * QW + h * HD : n * QW + (h + 1) * HD] = (dqt_st[n, :, cols] * SCALE).astype(LOW).T

    one_block(0, 2 * y + c, q_own, g_own, o_own, dq_own)
    one_block(1, 2 * y + 1 - c, q_par, g_par, o_par, dq_par)
    for s in range(SLOTS):
        for n in heads:
            dk_out[s, :, n * HD : (n + 1) * HD] = (dk_acc[n, s] * SCALE).astype(LOW)


def output_onward_kernel(*refs):
    output_kernel(*refs[:10], *refs[13:])


ROWS = GRP * BLK


def attention_call(kernel, name, steps, in_specs, out_specs, out_shape, scratch, aliases={}):
    return pl.pallas_call(
        kernel,
        grid_spec=pltpu.PrefetchScalarGridSpec(
            num_scalar_prefetch=3,
            grid=(steps,),
            in_specs=in_specs,
            out_specs=out_specs,
            scratch_shapes=[pltpu.SMEM((SLOTS,), jnp.int32)] + [pltpu.VMEM(*s) for s in scratch],
        ),
        out_shape=out_shape,
        input_output_aliases=aliases,
        compiler_params=pltpu.CompilerParams(dimension_semantics=("arbitrary",), vmem_limit_bytes=48 * 2**20),
        cost_estimate=LIGHT,
        name=name,
    )


def own_spec(start):
    return pl.BlockSpec((BLK, NG * QW), lambda i, place, par, lab: (0, place[1] * (HALF // NG) + start + i))


def partner_spec(start):
    return pl.BlockSpec((BLK, NG * QW), lambda i, place, par, lab: (0, start + i))


def blocks_spec(start):
    return pl.BlockSpec((SLOTS, BLK, NG * HD), lambda i, place, par, lab: (0, 0, start + i))


def stats_spec(start):
    return pl.BlockSpec((NG, 2, 8, ROWS), lambda i, place, par, lab: (start + i, 0, 0, 0))


def value_gradient(*args):
    own, partner = own_spec(0), partner_spec(0)
    return attention_call(
        values_kernel, "tree_values", HALF // NG,
        [own, partner, own, partner, blocks_spec(0)],
        [blocks_spec(0), stats_spec(0)],
        [jax.ShapeDtypeStruct((SLOTS, BLK, HALF * HD), LOW), jax.ShapeDtypeStruct((HALF, 2, 8, ROWS), F32)],
        [
            ((NG, 2 * BLK, HD), LOW),
            ((NG, ROWS, HD), LOW),
            ((NG, ROWS, HD), LOW),
            ((NG, PAIRS, 2 * BLK, ROWS), LOW),
            ((NG, 2 * BLK, ROWS), LOW),
            ((NG, 8, ROWS), F32),
            ((NG, PAIRS, 8, ROWS), F32),
            ((NG, 8, ROWS), F32),
            ((NG, SLOTS, BLK, HD), F32),
        ],
    )(*args)


def output_and_gradients(start, before, *args):
    own, partner, partner_out = own_spec(start), partner_spec(start), partner_spec(0)
    own_shape = jax.ShapeDtypeStruct((BLK, 2 * HALF * QW), LOW)
    partner_shape = jax.ShapeDtypeStruct((BLK, NG * QW), LOW)
    return attention_call(
        output_onward_kernel if before else output_kernel, "tree_outputs", 1,
        [own, partner, own, partner, blocks_spec(start), blocks_spec(start), stats_spec(start)]
        + [pl.BlockSpec(memory_space=pl.ANY)] * len(before),
        [own, partner_out, own, partner_out, blocks_spec(start)],
        [own_shape, partner_shape, own_shape, partner_shape, jax.ShapeDtypeStruct((SLOTS, BLK, HALF * HD), LOW)],
        [
            ((NG, PAIRS, 2 * BLK, HD), LOW),
            ((NG, PAIRS, 2 * BLK, HD), LOW),
            ((NG, PAIRS, HD, 2 * BLK), LOW),
            ((NG, PAIRS, HD, 2 * BLK), LOW),
            ((NG, ROWS, HD), LOW),
            ((NG, ROWS, HD), LOW),
            ((NG, HD, ROWS), LOW),
            ((NG, PAIRS, 2 * BLK, ROWS), LOW),
            ((NG, 2 * BLK, ROWS), LOW),
            ((NG, 8, ROWS), F32),
            ((NG, HD, ROWS), F32),
            ((NG, HD, ROWS), F32),
            ((NG, SLOTS, BLK, HD), F32),
        ],
        {10: 0, 11: 2, 12: 4} if before else {},
    )(*args, *before)


def weight_kernel(place, *refs):
    x_own, x_other, dv, out, x_all = refs[:NZ], refs[NZ : 2 * NZ], refs[-3], refs[-2], refs[-1]
    c, z = place[1], place[2]
    for d in range(NZ):
        src = lax.rem(z + NZ - d, NZ)
        for x, core in ((x_own[d], c), (x_other[d], 1 - c)):
            x_all[:, pl.ds(pl.multiple_of((2 * src + core) * BLK, BLK), BLK)] = x[...]
    out[...] = dot_nn(x_all[...], dv[...].reshape(2 * NZ * BLK, -1)).astype(LOW)


def weight_partial(place, x_own, x_other, dv):
    tall, wide, step = x_own[0].shape[0], dv.shape[3], 1024
    x_spec = pl.BlockSpec((step, BLK), lambda i, place: (i, 0))
    return pl.pallas_call(
        weight_kernel,
        grid_spec=pltpu.PrefetchScalarGridSpec(
            num_scalar_prefetch=1,
            grid=(tall // step,),
            in_specs=[x_spec] * (2 * NZ) + [pl.BlockSpec((NZ, 2, BLK, wide), lambda i, place: (0, 0, 0, 0))],
            out_specs=pl.BlockSpec((step, wide), lambda i, place: (i, 0)),
            scratch_shapes=[pltpu.VMEM((step, 2 * NZ * BLK), LOW)],
        ),
        out_shape=jax.ShapeDtypeStruct((tall, wide), LOW),
        compiler_params=pltpu.CompilerParams(vmem_limit_bytes=24 * 2**20),
        cost_estimate=LIGHT,
        name="weight_partial",
    )(place, *x_own, *x_other, dv)


def halves_kernel(rows, out, done):
    width = out.shape[2]
    copies = [
        pltpu.make_async_copy(rows.at[:, pl.ds(i % 2 * width, width)], out.at[i], done.at[i]) for i in range(SLOTS)
    ]
    for copy in copies:
        copy.start()
    for copy in copies:
        copy.wait()


def halves(rows):
    width = rows.shape[1] // 2
    return pl.pallas_call(
        halves_kernel,
        out_shape=jax.ShapeDtypeStruct((SLOTS, BLK, width), LOW),
        out_specs=pl.BlockSpec(memory_space=pl.ANY),
        scratch_shapes=[pltpu.SemaphoreType.DMA((SLOTS,))],
        cost_estimate=LIGHT,
        name="halves",
    )(rows)


def partner_kernel(place, q, g, q_out, g_out):
    q_out[...] = q[...]
    g_out[...] = g[...]


def partner_halves(place, q, g):
    src = pl.BlockSpec((BLK, QW), lambda i, place: (0, (1 - place[1]) * HALF + i))
    dst = pl.BlockSpec((BLK, QW), lambda i, place: (0, i))
    return pl.pallas_call(
        partner_kernel,
        grid_spec=pltpu.PrefetchScalarGridSpec(
            num_scalar_prefetch=1, grid=(HALF,), in_specs=[src] * 2, out_specs=[dst] * 2
        ),
        out_shape=[jax.ShapeDtypeStruct((BLK, HALF * QW), LOW)] * 2,
        cost_estimate=LIGHT,
        name="partner_halves",
    )(place, q, g)


def fill_kernel(place, o_before, dq_before, o_a, o_b, dq_a, dq_b, o_all, dq_all):
    early = pl.program_id(0) < NG

    @pl.when(early)
    def _():
        o_all[...] = o_a[...]
        dq_all[...] = dq_a[...]

    @pl.when(jnp.logical_not(early))
    def _():
        o_all[...] = o_b[...]
        dq_all[...] = dq_b[...]


def fill_partner(place, o_all, dq_all, o_parts, dq_parts):
    anywhere = pl.BlockSpec(memory_space=pl.ANY)
    first = pl.BlockSpec((BLK, QW), lambda i, place: (0, jnp.minimum(i, NG - 1)))
    second = pl.BlockSpec((BLK, QW), lambda i, place: (0, jnp.maximum(i - NG, 0)))
    whole = pl.BlockSpec((BLK, QW), lambda i, place: (0, (1 - place[1]) * HALF + i))
    return pl.pallas_call(
        fill_kernel,
        grid_spec=pltpu.PrefetchScalarGridSpec(
            num_scalar_prefetch=1,
            grid=(HALF,),
            in_specs=[anywhere, anywhere, first, second, first, second],
            out_specs=[whole, whole],
        ),
        out_shape=[jax.ShapeDtypeStruct(o_all.shape, LOW)] * 2,
        input_output_aliases={1: 0, 2: 1},
        cost_estimate=LIGHT,
        name="fill_partner",
    )(place, o_all, dq_all, *o_parts, *dq_parts)


def split_kernel(place, dk, r1, r2, r3, dv, after, mine, other):
    c = place[1]
    for out, e in ((mine, c), (other, 1 - c)):
        acc = dk[0, e].astype(F32)
        for r in (r1, r2, r3):
            acc = acc + r[e].astype(F32)
        out[0] = acc.astype(LOW)
        out[1] = dv[0, e]


def split_grads(place, dk, received, dv, after):
    width = dk.shape[3]
    pair = pl.BlockSpec((2, BLK, width), lambda i, place: (0, 0, 0))
    return pl.pallas_call(
        split_kernel,
        grid_spec=pltpu.PrefetchScalarGridSpec(
            num_scalar_prefetch=1,
            grid=(1,),
            in_specs=[pl.BlockSpec((1, 2, BLK, width), lambda i, place: (place[0], 0, 0, 0))]
            + [pair] * 3
            + [pl.BlockSpec((1, 2, BLK, width), lambda i, place: (0, 0, 0, 0)), pl.BlockSpec(memory_space=pl.ANY)],
            out_specs=[pair, pair],
        ),
        out_shape=[jax.ShapeDtypeStruct((2, BLK, width), LOW)] * 2,
        cost_estimate=LIGHT,
        name="split_grads",
    )(place, dk, *received, dv, after)


def join_kernel(place, mine, other, key_grad, value_grad):
    width = mine.shape[2]
    for i, out in enumerate((key_grad, value_grad)):
        out[:, pl.ds(pl.multiple_of(place[1] * width, width), width)] = mine[i]
        out[:, pl.ds(pl.multiple_of((1 - place[1]) * width, width), width)] = other[i]


def join_grads(place, mine, other):
    width = mine.shape[2]
    pair = pl.BlockSpec((2, BLK, width), lambda i, place: (0, 0, 0))
    rows = pl.BlockSpec((BLK, 2 * width), lambda i, place: (0, 0))
    return pl.pallas_call(
        join_kernel,
        grid_spec=pltpu.PrefetchScalarGridSpec(
            num_scalar_prefetch=1, grid=(1,), in_specs=[pair, pair], out_specs=[rows, rows]
        ),
        out_shape=[jax.ShapeDtypeStruct((BLK, 2 * width), LOW)] * 2,
        cost_estimate=LIGHT,
        name="join_grads",
    )(place, mine, other)


def x_kernel(place, x, *outs):
    piece = x.shape[1] // (NX * NZ)
    for d in range(NZ):
        to = lax.rem(place[2] + d, NZ)
        for i in range(NX):
            at = pl.multiple_of((i * NZ + to) * piece, piece)
            outs[d][i * piece : (i + 1) * piece, :] = x[:, pl.ds(at, piece)].T


def x_sends(place, x):
    tall = x.shape[1] // NZ
    return pl.pallas_call(
        x_kernel,
        grid_spec=pltpu.PrefetchScalarGridSpec(
            num_scalar_prefetch=1,
            grid=(1,),
            in_specs=[pl.BlockSpec(x.shape, lambda i, place: (0, 0))],
            out_specs=[pl.BlockSpec((tall, BLK), lambda i, place: (0, 0))] * NZ,
        ),
        out_shape=[jax.ShapeDtypeStruct((tall, BLK), LOW)] * NZ,
        cost_estimate=LIGHT,
        name="x_sends",
    )(place, x)


def sum_kernel(terms, out, total, done):
    for e in range(2):
        acc = terms[0, e].astype(F32)
        for i in range(1, NY):
            acc = acc + terms[i, e].astype(F32)
        total[e] = acc.astype(LOW)
    copies = [pltpu.make_async_copy(total, out.at[i], done.at[i]) for i in range(NZ)]
    for copy in copies:
        copy.start()
    for copy in copies:
        copy.wait()


def sum_blocks(terms):
    return pl.pallas_call(
        sum_kernel,
        out_shape=jax.ShapeDtypeStruct((NZ,) + terms.shape[1:], LOW),
        out_specs=pl.BlockSpec(memory_space=pl.ANY),
        scratch_shapes=[pltpu.VMEM(terms.shape[1:], LOW), pltpu.SemaphoreType.DMA((NZ,))],
        compiler_params=pltpu.CompilerParams(vmem_limit_bytes=60 * 2**20),
        cost_estimate=LIGHT,
        name="sum_blocks",
    )(terms)


def finish_kernel(parts, out):
    width = parts.shape[2]
    for half in range(2):
        acc = parts[half].astype(F32)
        for i in range(1, NX * NY):
            acc = acc + parts[2 * i + half].astype(F32)
        out[:, half * width : (half + 1) * width] = acc * (16 * SLOTS * BLK) ** -0.5


def finish_weight(parts):
    rows, width = parts.shape[1:]
    return pl.pallas_call(
        finish_kernel,
        out_shape=jax.ShapeDtypeStruct((rows, 2 * width), F32),
        compiler_params=pltpu.CompilerParams(vmem_limit_bytes=60 * 2**20),
        cost_estimate=LIGHT,
        name="finish_weight",
    )(parts)


def device(x, z, y, c):
    return (x * NZ + z) * SLOTS + y * 2 + c


def per_device(query_rows, key_rows, value_rows, layer_input, out_grad, parents, labels):
    ctx = lax.axis_index("ctx")
    y, c, z = ctx // 2, ctx % 2, lax.axis_index("dp") % NZ
    place = jnp.stack([y, c, z]).astype(jnp.int32)
    q, k, v, g, x = query_rows[0], key_rows[0], value_rows[0], out_grad[0], layer_input[0]
    along_y = [[2 * m + n for m in range(NY)] for n in range(2)]
    along_z = [[i * NZ + j for j in range(NZ)] for i in range(NX)]
    across = [[device(i, j, m, n) for i in range(NX) for m in range(NY) for n in range(2)] for j in range(NZ)]

    def swap(a):
        return lax.ppermute(a, "ctx", [(i, i ^ 1) for i in range(SLOTS)])

    def pick(a, i):
        return lax.dynamic_index_in_dim(a, i, 0, keepdims=False)

    def further(a, d):
        return lax.ppermute(a, "dp", [(i, i // NZ * NZ + (i + d) % NZ) for i in range(NX * NZ)])

    def earlier(a, d):
        return lax.ppermute(a, "ctx", [(i + 2 * d, i) for i in range(SLOTS - 2 * d)])

    keys = lax.all_to_all(halves(k), "ctx", 0, 0)
    q_par, g_par = [swap(a) for a in partner_halves(place, q, g)]
    x_own = x_sends(place, x)
    v_sends = halves(v)
    x_own = [x_own[0]] + [further(x_own[d], d) for d in range(1, NZ)]
    keys, v_sends, x_own[1], x_own[3] = lax.optimization_barrier((keys, v_sends, x_own[1], x_own[3]))
    vals = lax.all_to_all(v_sends, "ctx", 0, 0)
    dv, stats = value_gradient(place, parents, labels, q, q_par, g, g_par, keys)
    dv, vals, x_own = lax.optimization_barrier((dv, vals, x_own))
    dv = lax.all_to_all(dv.reshape(NY, 2, BLK, HALF * HD), "ctx", 0, 0, axis_index_groups=along_y)
    args = (place, parents, labels, q, q_par, g, g_par, keys, vals, stats)
    o_own, o_par, dq_own, dq_par, dk = output_and_gradients(0, (), *args)
    o_pars, dq_pars = [o_par], [dq_par]
    dv, dk, x_own = lax.optimization_barrier((dv, dk, x_own))
    x_other = [swap(a) for a in x_own]
    dv_sends = sum_blocks(dv)
    dv_sends, dk = lax.optimization_barrier((dv_sends, dk))
    dv_all = lax.all_to_all(dv_sends, "dp", 0, 0, axis_index_groups=along_z)
    o_own, o_par, dq_own, dq_par, dk = output_and_gradients(1, (o_own, dq_own, dk), *args)
    o_pars, dq_pars = o_pars + [o_par], dq_pars + [dq_par]
    dv_all, dk = lax.optimization_barrier((dv_all, dk))
    dk = dk.reshape(NY, 2, BLK, HALF * HD)
    received = [earlier(pick(dk, jnp.maximum(y - d, 0)), d) for d in range(1, NY)]
    partial = weight_partial(place, x_own, x_other, dv_all).reshape(2 * NX * NY, -1, HALF * HD)
    after, o_pars, dq_pars = lax.optimization_barrier((partial, o_pars, dq_pars))
    o_pars, dq_pars = [swap(a) for a in o_pars], [swap(a) for a in dq_pars]
    weight_grad = finish_weight(lax.all_to_all(partial, ("dp", "ctx"), 0, 0, axis_index_groups=across))
    out, query_grad = fill_partner(place, o_own, dq_own, o_pars, dq_pars)
    mine, other = split_grads(place, dk, received, dv_sends, after)
    key_grad, value_grad = join_grads(place, mine, swap(other))
    return out[None], query_grad[None], key_grad[None], value_grad[None], weight_grad


def solution(mesh):
    rows = P("dp", "ctx", None)
    return jax.shard_map(
        per_device,
        mesh=mesh,
        in_specs=(rows,) * 5 + (P("dp", None), P("dp", None)),
        out_specs=(rows,) * 4 + (P(("dp", "ctx"), None),),
        check_vma=False,
    )
```

```python
import jax
import jax.numpy as jnp
from jax import lax
from jax.experimental import pallas as pl
from jax.experimental.pallas import tpu as pltpu
from jax.sharding import PartitionSpec as P

HD = 128
BLK = 128
GRP = 8
NY = 4
NZ = 4
NX = 4
HALF = 4
QW = GRP * HD
SLOTS = 2 * NY
PAIRS = 4
NG = 2
LOW = jnp.bfloat16
F32 = jnp.float32
SCALE = HD**-0.5
EXP_SCALE = SCALE * 1.4426950408889634
MASKED = -1e30
LIGHT = pl.CostEstimate(flops=1, bytes_accessed=1, transcendentals=0)


def dot_nt(a, b):
    return lax.dot_general(a, b, (((1,), (1,)), ((), ())), preferred_element_type=F32)


def dot_nn(a, b):
    return lax.dot_general(a, b, (((1,), (0,)), ((), ())), preferred_element_type=F32)


def dot_tn(a, b):
    return lax.dot_general(a, b, (((0,), (0,)), ((), ())), preferred_element_type=F32)


def walk(parents, block, chain):
    def above(step, carry):
        current, count = carry
        parent = parents[0, current]
        more = parent != current
        current = jnp.where(more, parent, current)
        chain[step + 1] = current
        return current, count + more.astype(jnp.int32)

    chain[0] = block
    return lax.fori_loop(0, SLOTS - 1, above, (block, jnp.int32(1)))[1]


def fold(a, op):
    while a.shape[0] > 8:
        half = a.shape[0] // 2
        a = op(a[:half], a[half:])
    return a


def causal_mask():
    key_pos = lax.broadcasted_iota(jnp.int32, (BLK, BLK), 0)
    query_pos = lax.broadcasted_iota(jnp.int32, (BLK, BLK), 1)
    causal = jnp.where(key_pos <= query_pos, 0.0, MASKED).astype(F32)
    return jnp.concatenate([causal] * GRP, axis=1)


def block_sign(labels, block):
    return jnp.full((BLK, HD), jnp.where(labels[0, block] == 2, -1.0, 1.0), F32).astype(LOW)


def masked(s, t, count, first, causal):
    second = jnp.where(2 * t + 1 < count, 0.0, MASKED).astype(F32)
    s_a = s[:BLK]
    if first:
        s_a = s_a + causal
    return s_a, s[BLK:] + second


def over_pairs(step, pairs):
    def more(t, carry):
        step(t, False)
        return carry

    step(0, True)
    lax.fori_loop(1, pairs, more, 0)


def values_kernel(
    place, parents, labels,
    q_own, q_par, g_own, g_par, keys,
    dv_out, stats,
    chain, k_pair, q_st, g_st, p_st, w_st, m_st, mt_st, l_st, dv_acc,
):
    y = place[0]
    c = place[1]
    heads = range(NG)
    dv_acc[...] = jnp.zeros_like(dv_acc)
    causal = causal_mask()

    def one_block(which, block, q_ref, g_ref):
        count = walk(parents, block, chain)
        pairs = (count + 1) // 2
        sign = block_sign(labels, block)
        for n in heads:
            for h in range(GRP):
                rows = slice(h * BLK, (h + 1) * BLK)
                cols = slice(n * QW + h * HD, n * QW + (h + 1) * HD)
                q_st[n, rows, :] = q_ref[:, cols]
                g_st[n, rows, :] = g_ref[:, cols] * sign

        def scores(t, first):
            for n in heads:
                for e in range(2):
                    k_pair[n, e * BLK : (e + 1) * BLK, :] = keys[chain[2 * t + e], :, n * HD : (n + 1) * HD]
            for n in heads:
                s_a, s_b = masked(dot_nt(k_pair[n], q_st[n]), t, count, first, causal)
                top = jnp.max(fold(jnp.maximum(s_a, s_b), jnp.maximum), axis=0, keepdims=True)
                if not first:
                    old = m_st[n, 0:1, :]
                    top = jnp.maximum(top, old)
                    alpha = jnp.exp2((old - top) * EXP_SCALE)
                p_a = jnp.exp2((s_a - top) * EXP_SCALE)
                p_b = jnp.exp2((s_b - top) * EXP_SCALE)
                p_st[n, t] = jnp.concatenate([p_a.astype(LOW), p_b.astype(LOW)], axis=0)
                total = fold(p_a + p_b, jnp.add)
                if first:
                    l_st[n] = total
                else:
                    l_st[n] = l_st[n] * alpha + total
                m_st[n, 0:1, :] = top
                mt_st[n, t, 0:1, :] = top

        over_pairs(scores, pairs)
        for n in heads:
            total = jnp.sum(l_st[n], axis=0, keepdims=True)
            l_st[n, 0:1, :] = 1.0 / total
            stats[n, which, 0:1, :] = m_st[n, 0:1, :] * EXP_SCALE + jnp.log2(total)

        def values(t, first):
            for n in heads:
                f = jnp.exp2((mt_st[n, t, 0:1, :] - m_st[n, 0:1, :]) * EXP_SCALE) * l_st[n, 0:1, :]
                w_st[n] = (p_st[n, t].astype(F32) * f).astype(LOW)
            for n in heads:
                dv = dot_nn(w_st[n], g_st[n])
                for e in range(2):
                    dv_acc[n, chain[2 * t + e]] += dv[e * BLK : (e + 1) * BLK, :]

        over_pairs(values, pairs)

    one_block(0, 2 * y + c, q_own, g_own)
    one_block(1, 2 * y + 1 - c, q_par, g_par)
    for s in range(SLOTS):
        for n in heads:
            dv_out[s, :, n * HD : (n + 1) * HD] = dv_acc[n, s].astype(LOW)


def output_kernel(
    place, parents, labels,
    q_own, q_par, g_own, g_par, keys, vals, stats,
    o_own, o_par, dq_own, dq_par, dk_out,
    chain, k_pair, v_pair, kt_pair, vt_pair, q_st, g_st, gt_st, w_st, ds_st, in_st, ot_st, dqt_st, dk_acc,
):
    y = place[0]
    c = place[1]
    heads = range(NG)
    dk_acc[...] = jnp.zeros_like(dk_acc)
    causal = causal_mask()

    def one_block(which, block, q_ref, g_ref, o_ref, dq_ref):
        count = walk(parents, block, chain)
        pairs = (count + 1) // 2
        sign = block_sign(labels, block)
        for n in heads:
            for h in range(GRP):
                rows = slice(h * BLK, (h + 1) * BLK)
                cols = slice(n * QW + h * HD, n * QW + (h + 1) * HD)
                q_st[n, rows, :] = q_ref[:, cols]
                g = g_ref[:, cols] * sign
                g_st[n, rows, :] = g
                gt_st[n, :, rows] = g.T

        def outputs(t, first):
            for n in heads:
                for e in range(2):
                    s = chain[2 * t + e]
                    rows = slice(e * BLK, (e + 1) * BLK)
                    k = keys[s, :, n * HD : (n + 1) * HD]
                    v = vals[s, :, n * HD : (n + 1) * HD]
                    k_pair[n, t, rows, :] = k
                    v_pair[n, t, rows, :] = v
                    kt_pair[n, t, :, rows] = k.T
                    vt_pair[n, t, :, rows] = v.T
            for n in heads:
                s_a, s_b = masked(dot_nt(k_pair[n, t], q_st[n]), t, count, first, causal)
                lse = stats[n, which, 0:1, :]
                w_a = jnp.exp2(s_a * EXP_SCALE - lse).astype(LOW)
                w_b = jnp.exp2(s_b * EXP_SCALE - lse).astype(LOW)
                w = jnp.concatenate([w_a, w_b], axis=0)
                w_st[n, t] = w
                out = dot_nn(vt_pair[n, t], w)
                if first:
                    ot_st[n] = out
                else:
                    ot_st[n] += out

        over_pairs(outputs, pairs)
        for h in range(GRP):
            for n in heads:
                cols = slice(h * BLK, (h + 1) * BLK)
                out = ot_st[n, :, cols].astype(LOW)
                o_ref[:, n * QW + h * HD : n * QW + (h + 1) * HD] = out.T
                in_st[n, 0:1, cols] = jnp.sum(
                    gt_st[n, :, cols].astype(F32) * out.astype(F32), axis=0, keepdims=True
                )

        def grads(t, first):
            for n in heads:
                dp = dot_nn(v_pair[n, t], gt_st[n])
                ds = (w_st[n, t].astype(F32) * (dp - in_st[n, 0:1, :])).astype(LOW)
                ds_st[n] = ds
                dq = dot_nn(kt_pair[n, t], ds)
                if first:
                    dqt_st[n] = dq
                else:
                    dqt_st[n] += dq
            for n in heads:
                dk = dot_nn(ds_st[n], q_st[n])
                for e in range(2):
                    dk_acc[n, chain[2 * t + e]] += dk[e * BLK : (e + 1) * BLK, :]

        over_pairs(grads, pairs)
        for h in range(GRP):
            for n in heads:
                cols = slice(h * BLK, (h + 1) * BLK)
                dq_ref[:, n * QW + h * HD : n * QW + (h + 1) * HD] = (dqt_st[n, :, cols] * SCALE).astype(LOW).T

    one_block(0, 2 * y + c, q_own, g_own, o_own, dq_own)
    one_block(1, 2 * y + 1 - c, q_par, g_par, o_par, dq_par)
    for s in range(SLOTS):
        for n in heads:
            dk_out[s, :, n * HD : (n + 1) * HD] = (dk_acc[n, s] * SCALE).astype(LOW)


def output_onward_kernel(*refs):
    output_kernel(*refs[:10], *refs[13:])


ROWS = GRP * BLK


def attention_call(kernel, name, steps, in_specs, out_specs, out_shape, scratch, aliases={}):
    return pl.pallas_call(
        kernel,
        grid_spec=pltpu.PrefetchScalarGridSpec(
            num_scalar_prefetch=3,
            grid=(steps,),
            in_specs=in_specs,
            out_specs=out_specs,
            scratch_shapes=[pltpu.SMEM((SLOTS,), jnp.int32)] + [pltpu.VMEM(*s) for s in scratch],
        ),
        out_shape=out_shape,
        input_output_aliases=aliases,
        compiler_params=pltpu.CompilerParams(dimension_semantics=("arbitrary",), vmem_limit_bytes=60 * 2**20),
        cost_estimate=LIGHT,
        name=name,
    )


def own_spec(start):
    return pl.BlockSpec((BLK, NG * QW), lambda i, place, par, lab: (0, place[1] * (HALF // NG) + start + i))


def partner_spec(start):
    return pl.BlockSpec((BLK, NG * QW), lambda i, place, par, lab: (0, start + i))


def blocks_spec(start):
    return pl.BlockSpec((SLOTS, BLK, NG * HD), lambda i, place, par, lab: (0, 0, start + i))


def stats_spec(start):
    return pl.BlockSpec((NG, 2, 8, ROWS), lambda i, place, par, lab: (start + i, 0, 0, 0))


def value_gradient(*args):
    own, partner = own_spec(0), partner_spec(0)
    return attention_call(
        values_kernel, "tree_values", HALF // NG,
        [own, partner, own, partner, blocks_spec(0)],
        [blocks_spec(0), stats_spec(0)],
        [jax.ShapeDtypeStruct((SLOTS, BLK, HALF * HD), LOW), jax.ShapeDtypeStruct((HALF, 2, 8, ROWS), F32)],
        [
            ((NG, 2 * BLK, HD), LOW),
            ((NG, ROWS, HD), LOW),
            ((NG, ROWS, HD), LOW),
            ((NG, PAIRS, 2 * BLK, ROWS), LOW),
            ((NG, 2 * BLK, ROWS), LOW),
            ((NG, 8, ROWS), F32),
            ((NG, PAIRS, 8, ROWS), F32),
            ((NG, 8, ROWS), F32),
            ((NG, SLOTS, BLK, HD), F32),
        ],
    )(*args)


def output_and_gradients(start, before, *args):
    own, partner, partner_out = own_spec(start), partner_spec(start), partner_spec(0)
    own_shape = jax.ShapeDtypeStruct((BLK, 2 * HALF * QW), LOW)
    partner_shape = jax.ShapeDtypeStruct((BLK, NG * QW), LOW)
    return attention_call(
        output_onward_kernel if before else output_kernel, "tree_outputs", 1,
        [own, partner, own, partner, blocks_spec(start), blocks_spec(start), stats_spec(start)]
        + [pl.BlockSpec(memory_space=pl.ANY)] * len(before),
        [own, partner_out, own, partner_out, blocks_spec(start)],
        [own_shape, partner_shape, own_shape, partner_shape, jax.ShapeDtypeStruct((SLOTS, BLK, HALF * HD), LOW)],
        [
            ((NG, PAIRS, 2 * BLK, HD), LOW),
            ((NG, PAIRS, 2 * BLK, HD), LOW),
            ((NG, PAIRS, HD, 2 * BLK), LOW),
            ((NG, PAIRS, HD, 2 * BLK), LOW),
            ((NG, ROWS, HD), LOW),
            ((NG, ROWS, HD), LOW),
            ((NG, HD, ROWS), LOW),
            ((NG, PAIRS, 2 * BLK, ROWS), LOW),
            ((NG, 2 * BLK, ROWS), LOW),
            ((NG, 8, ROWS), F32),
            ((NG, HD, ROWS), F32),
            ((NG, HD, ROWS), F32),
            ((NG, SLOTS, BLK, HD), F32),
        ],
        {10: 0, 11: 2, 12: 4} if before else {},
    )(*args, *before)


def weight_kernel(place, *refs):
    x_own, x_other, dv, out, x_all = refs[:NZ], refs[NZ : 2 * NZ], refs[-3], refs[-2], refs[-1]
    c, z = place[1], place[2]
    for d in range(NZ):
        src = lax.rem(z + NZ - d, NZ)
        for x, core in ((x_own[d], c), (x_other[d], 1 - c)):
            x_all[:, pl.ds(pl.multiple_of((2 * src + core) * BLK, BLK), BLK)] = x[...]
    out[...] = dot_nn(x_all[...], dv[...].reshape(2 * NZ * BLK, -1)).astype(LOW)


def weight_partial(place, x_own, x_other, dv):
    tall, wide, step = x_own[0].shape[0], dv.shape[3], 1024
    x_spec = pl.BlockSpec((step, BLK), lambda i, place: (i, 0))
    return pl.pallas_call(
        weight_kernel,
        grid_spec=pltpu.PrefetchScalarGridSpec(
            num_scalar_prefetch=1,
            grid=(tall // step,),
            in_specs=[x_spec] * (2 * NZ) + [pl.BlockSpec((NZ, 2, BLK, wide), lambda i, place: (0, 0, 0, 0))],
            out_specs=pl.BlockSpec((step, wide), lambda i, place: (i, 0)),
            scratch_shapes=[pltpu.VMEM((step, 2 * NZ * BLK), LOW)],
        ),
        out_shape=jax.ShapeDtypeStruct((tall, wide), LOW),
        compiler_params=pltpu.CompilerParams(vmem_limit_bytes=24 * 2**20),
        cost_estimate=LIGHT,
        name="weight_partial",
    )(place, *x_own, *x_other, dv)


def halves_kernel(k, v, k_out, v_out, done):
    width = k_out.shape[2]
    copies = [
        pltpu.make_async_copy(rows.at[:, pl.ds(i % 2 * width, width)], out.at[i], done.at[j, i])
        for j, (rows, out) in enumerate(((k, k_out), (v, v_out)))
        for i in range(SLOTS)
    ]
    for copy in copies:
        copy.start()
    for copy in copies:
        copy.wait()


def halves(k, v):
    width = k.shape[1] // 2
    return pl.pallas_call(
        halves_kernel,
        out_shape=[jax.ShapeDtypeStruct((SLOTS, BLK, width), LOW)] * 2,
        out_specs=[pl.BlockSpec(memory_space=pl.ANY)] * 2,
        scratch_shapes=[pltpu.SemaphoreType.DMA((2, SLOTS))],
        cost_estimate=LIGHT,
        name="halves",
    )(k, v)


def partner_kernel(place, q, g, q_out, g_out):
    q_out[...] = q[...]
    g_out[...] = g[...]


def partner_halves(place, q, g):
    steps = 2
    src = pl.BlockSpec((BLK, HALF * QW // steps), lambda i, place: (0, (1 - place[1]) * steps + i))
    dst = pl.BlockSpec((BLK, HALF * QW // steps), lambda i, place: (0, i))
    return pl.pallas_call(
        partner_kernel,
        grid_spec=pltpu.PrefetchScalarGridSpec(
            num_scalar_prefetch=1, grid=(steps,), in_specs=[src] * 2, out_specs=[dst] * 2
        ),
        out_shape=[jax.ShapeDtypeStruct((BLK, HALF * QW), LOW)] * 2,
        cost_estimate=LIGHT,
        name="partner_halves",
    )(place, q, g)


def fill_kernel(place, o_before, dq_before, o_a, o_b, dq_a, dq_b, o_all, dq_all):
    early = pl.program_id(0) < NG

    @pl.when(early)
    def _():
        o_all[...] = o_a[...]
        dq_all[...] = dq_a[...]

    @pl.when(jnp.logical_not(early))
    def _():
        o_all[...] = o_b[...]
        dq_all[...] = dq_b[...]


def fill_partner(place, o_all, dq_all, o_parts, dq_parts):
    anywhere = pl.BlockSpec(memory_space=pl.ANY)
    first = pl.BlockSpec((BLK, QW), lambda i, place: (0, jnp.minimum(i, NG - 1)))
    second = pl.BlockSpec((BLK, QW), lambda i, place: (0, jnp.maximum(i - NG, 0)))
    whole = pl.BlockSpec((BLK, QW), lambda i, place: (0, (1 - place[1]) * HALF + i))
    return pl.pallas_call(
        fill_kernel,
        grid_spec=pltpu.PrefetchScalarGridSpec(
            num_scalar_prefetch=1,
            grid=(HALF,),
            in_specs=[anywhere, anywhere, first, second, first, second],
            out_specs=[whole, whole],
        ),
        out_shape=[jax.ShapeDtypeStruct(o_all.shape, LOW)] * 2,
        input_output_aliases={1: 0, 2: 1},
        cost_estimate=LIGHT,
        name="fill_partner",
    )(place, o_all, dq_all, *o_parts, *dq_parts)


def split_kernel(place, dk, r1, r2, r3, dv, after, mine, other):
    c = place[1]
    for out, e in ((mine, c), (other, 1 - c)):
        acc = dk[0, e].astype(F32)
        for r in (r1, r2, r3):
            acc = acc + r[e].astype(F32)
        out[0] = acc.astype(LOW)
        out[1] = dv[0, e]


def split_grads(place, dk, received, dv, after):
    width = dk.shape[3]
    pair = pl.BlockSpec((2, BLK, width), lambda i, place: (0, 0, 0))
    return pl.pallas_call(
        split_kernel,
        grid_spec=pltpu.PrefetchScalarGridSpec(
            num_scalar_prefetch=1,
            grid=(1,),
            in_specs=[pl.BlockSpec((1, 2, BLK, width), lambda i, place: (place[0], 0, 0, 0))]
            + [pair] * 3
            + [pl.BlockSpec((1, 2, BLK, width), lambda i, place: (0, 0, 0, 0)), pl.BlockSpec(memory_space=pl.ANY)],
            out_specs=[pair, pair],
        ),
        out_shape=[jax.ShapeDtypeStruct((2, BLK, width), LOW)] * 2,
        cost_estimate=LIGHT,
        name="split_grads",
    )(place, dk, *received, dv, after)


def join_kernel(place, mine, other, key_grad, value_grad):
    width = mine.shape[2]
    for i, out in enumerate((key_grad, value_grad)):
        out[:, pl.ds(pl.multiple_of(place[1] * width, width), width)] = mine[i]
        out[:, pl.ds(pl.multiple_of((1 - place[1]) * width, width), width)] = other[i]


def join_grads(place, mine, other):
    width = mine.shape[2]
    pair = pl.BlockSpec((2, BLK, width), lambda i, place: (0, 0, 0))
    rows = pl.BlockSpec((BLK, 2 * width), lambda i, place: (0, 0))
    return pl.pallas_call(
        join_kernel,
        grid_spec=pltpu.PrefetchScalarGridSpec(
            num_scalar_prefetch=1, grid=(1,), in_specs=[pair, pair], out_specs=[rows, rows]
        ),
        out_shape=[jax.ShapeDtypeStruct((BLK, 2 * width), LOW)] * 2,
        cost_estimate=LIGHT,
        name="join_grads",
    )(place, mine, other)


def x_kernel(place, x, *outs):
    piece = x.shape[1] // (NX * NZ)
    for d in range(NZ):
        to = lax.rem(place[2] + d, NZ)
        for i in range(NX):
            at = pl.multiple_of((i * NZ + to) * piece, piece)
            outs[d][i * piece : (i + 1) * piece, :] = x[:, pl.ds(at, piece)].T


def x_sends(place, x):
    tall = x.shape[1] // NZ
    return pl.pallas_call(
        x_kernel,
        grid_spec=pltpu.PrefetchScalarGridSpec(
            num_scalar_prefetch=1,
            grid=(1,),
            in_specs=[pl.BlockSpec(x.shape, lambda i, place: (0, 0))],
            out_specs=[pl.BlockSpec((tall, BLK), lambda i, place: (0, 0))] * NZ,
        ),
        out_shape=[jax.ShapeDtypeStruct((tall, BLK), LOW)] * NZ,
        cost_estimate=LIGHT,
        name="x_sends",
    )(place, x)


def sum_kernel(terms, out, total, done):
    for e in range(2):
        acc = terms[0, e].astype(F32)
        for i in range(1, NY):
            acc = acc + terms[i, e].astype(F32)
        total[e] = acc.astype(LOW)
    copies = [pltpu.make_async_copy(total, out.at[i], done.at[i]) for i in range(NZ)]
    for copy in copies:
        copy.start()
    for copy in copies:
        copy.wait()


def sum_blocks(terms):
    return pl.pallas_call(
        sum_kernel,
        out_shape=jax.ShapeDtypeStruct((NZ,) + terms.shape[1:], LOW),
        out_specs=pl.BlockSpec(memory_space=pl.ANY),
        scratch_shapes=[pltpu.VMEM(terms.shape[1:], LOW), pltpu.SemaphoreType.DMA((NZ,))],
        compiler_params=pltpu.CompilerParams(vmem_limit_bytes=60 * 2**20),
        cost_estimate=LIGHT,
        name="sum_blocks",
    )(terms)


def finish_kernel(parts, out):
    width = parts.shape[2]
    for half in range(2):
        acc = parts[half].astype(F32)
        for i in range(1, NX * NY):
            acc = acc + parts[2 * i + half].astype(F32)
        out[:, half * width : (half + 1) * width] = acc * (16 * SLOTS * BLK) ** -0.5


def finish_weight(parts):
    rows, width = parts.shape[1:]
    return pl.pallas_call(
        finish_kernel,
        out_shape=jax.ShapeDtypeStruct((rows, 2 * width), F32),
        compiler_params=pltpu.CompilerParams(vmem_limit_bytes=60 * 2**20),
        cost_estimate=LIGHT,
        name="finish_weight",
    )(parts)


def device(x, z, y, c):
    return (x * NZ + z) * SLOTS + y * 2 + c


def per_device(query_rows, key_rows, value_rows, layer_input, out_grad, parents, labels):
    ctx = lax.axis_index("ctx")
    y, c, z = ctx // 2, ctx % 2, lax.axis_index("dp") % NZ
    place = jnp.stack([y, c, z]).astype(jnp.int32)
    q, k, v, g, x = query_rows[0], key_rows[0], value_rows[0], out_grad[0], layer_input[0]
    along_y = [[2 * m + n for m in range(NY)] for n in range(2)]
    along_z = [[i * NZ + j for j in range(NZ)] for i in range(NX)]
    across = [[device(i, j, m, n) for i in range(NX) for m in range(NY) for n in range(2)] for j in range(NZ)]

    def swap(a):
        return lax.ppermute(a, "ctx", [(i, i ^ 1) for i in range(SLOTS)])

    def pick(a, i):
        return lax.dynamic_index_in_dim(a, i, 0, keepdims=False)

    def further(a, d):
        return lax.ppermute(a, "dp", [(i, i // NZ * NZ + (i + d) % NZ) for i in range(NX * NZ)])

    def earlier(a, d):
        return lax.ppermute(a, "ctx", [(i + 2 * d, i) for i in range(SLOTS - 2 * d)])

    k_sends, v_sends = halves(k, v)
    keys = lax.all_to_all(k_sends, "ctx", 0, 0)
    q_par, g_par = [swap(a) for a in partner_halves(place, q, g)]
    x_own = x_sends(place, x)
    x_own = [x_own[0]] + [further(x_own[d], d) for d in range(1, NZ)]
    keys, v_sends, x_own[1], x_own[3] = lax.optimization_barrier((keys, v_sends, x_own[1], x_own[3]))
    vals = lax.all_to_all(v_sends, "ctx", 0, 0)
    dv, stats = value_gradient(place, parents, labels, q, q_par, g, g_par, keys)
    dv, vals, x_own = lax.optimization_barrier((dv, vals, x_own))
    dv = lax.all_to_all(dv.reshape(NY, 2, BLK, HALF * HD), "ctx", 0, 0, axis_index_groups=along_y)
    args = (place, parents, labels, q, q_par, g, g_par, keys, vals, stats)
    o_own, o_par, dq_own, dq_par, dk = output_and_gradients(0, (), *args)
    o_pars, dq_pars = [o_par], [dq_par]
    dv, dk, x_own = lax.optimization_barrier((dv, dk, x_own))
    x_other = [swap(a) for a in x_own]
    dv_sends = sum_blocks(dv)
    dv_sends, dk = lax.optimization_barrier((dv_sends, dk))
    dv_all = lax.all_to_all(dv_sends, "dp", 0, 0, axis_index_groups=along_z)
    o_own, o_par, dq_own, dq_par, dk = output_and_gradients(1, (o_own, dq_own, dk), *args)
    o_pars, dq_pars = o_pars + [o_par], dq_pars + [dq_par]
    dv_all, dk = lax.optimization_barrier((dv_all, dk))
    dk = dk.reshape(NY, 2, BLK, HALF * HD)
    received = [earlier(pick(dk, jnp.maximum(y - d, 0)), d) for d in range(1, NY)]
    partial = weight_partial(place, x_own, x_other, dv_all).reshape(2 * NX * NY, -1, HALF * HD)
    _, o_pars, dq_pars = lax.optimization_barrier((partial, o_pars, dq_pars))
    o_pars, dq_pars = [swap(a) for a in o_pars], [swap(a) for a in dq_pars]
    weight_grad = finish_weight(lax.all_to_all(partial, ("dp", "ctx"), 0, 0, axis_index_groups=across))
    out, query_grad = fill_partner(place, o_own, dq_own, o_pars, dq_pars)
    mine, other = split_grads(place, dk, received, dv_sends, query_grad)
    key_grad, value_grad = join_grads(place, mine, swap(other))
    return out[None], query_grad[None], key_grad[None], value_grad[None], weight_grad


def solution(mesh):
    rows = P("dp", "ctx", None)
    return jax.shard_map(
        per_device,
        mesh=mesh,
        in_specs=(rows,) * 5 + (P("dp", None), P("dp", None)),
        out_specs=(rows,) * 4 + (P(("dp", "ctx"), None),),
        check_vma=False,
    )
```

```python
import jax
import jax.numpy as jnp
from jax import lax
from jax.experimental import pallas as pl
from jax.experimental.pallas import tpu as pltpu
from jax.sharding import PartitionSpec as P

HD = 128
BLK = 128
GRP = 8
NY = 4
NZ = 4
NX = 4
HALF = 4
QW = GRP * HD
SLOTS = 2 * NY
PAIRS = 4
NG = 2
LOW = jnp.bfloat16
F32 = jnp.float32
SCALE = HD**-0.5
EXP_SCALE = SCALE * 1.4426950408889634
MASKED = -1e30
LIGHT = pl.CostEstimate(flops=1, bytes_accessed=1, transcendentals=0)


def dot_nt(a, b):
    return lax.dot_general(a, b, (((1,), (1,)), ((), ())), preferred_element_type=F32)


def dot_nn(a, b):
    return lax.dot_general(a, b, (((1,), (0,)), ((), ())), preferred_element_type=F32)


def dot_tn(a, b):
    return lax.dot_general(a, b, (((0,), (0,)), ((), ())), preferred_element_type=F32)


def walk(parents, block, chain):
    def above(step, carry):
        current, count = carry
        parent = parents[0, current]
        more = parent != current
        current = jnp.where(more, parent, current)
        chain[step + 1] = current
        return current, count + more.astype(jnp.int32)

    chain[0] = block
    return lax.fori_loop(0, SLOTS - 1, above, (block, jnp.int32(1)))[1]


def fold(a, op):
    while a.shape[0] > 8:
        half = a.shape[0] // 2
        a = op(a[:half], a[half:])
    return a


def causal_mask():
    key_pos = lax.broadcasted_iota(jnp.int32, (BLK, BLK), 0)
    query_pos = lax.broadcasted_iota(jnp.int32, (BLK, BLK), 1)
    causal = jnp.where(key_pos <= query_pos, 0.0, MASKED).astype(F32)
    return jnp.concatenate([causal] * GRP, axis=1)


def block_sign(labels, block):
    return jnp.full((BLK, HD), jnp.where(labels[0, block] == 2, -1.0, 1.0), F32).astype(LOW)


def masked(s, t, count, first, causal):
    second = jnp.where(2 * t + 1 < count, 0.0, MASKED).astype(F32)
    s_a = s[:BLK]
    if first:
        s_a = s_a + causal
    return s_a, s[BLK:] + second


def over_pairs(step, pairs):
    def more(t, carry):
        step(t, False)
        return carry

    step(0, True)
    lax.fori_loop(1, pairs, more, 0)


def values_kernel(
    place, parents, labels,
    q_own, q_par, g_own, g_par, keys,
    dv_out, stats,
    chain, k_pair, q_st, g_st, p_st, w_st, m_st, mt_st, l_st, dv_acc,
):
    y = place[0]
    c = place[1]
    heads = range(NG)
    dv_acc[...] = jnp.zeros_like(dv_acc)
    causal = causal_mask()

    def one_block(which, block, q_ref, g_ref):
        count = walk(parents, block, chain)
        pairs = (count + 1) // 2
        sign = block_sign(labels, block)
        for n in heads:
            for h in range(GRP):
                rows = slice(h * BLK, (h + 1) * BLK)
                cols = slice(n * QW + h * HD, n * QW + (h + 1) * HD)
                q_st[n, rows, :] = q_ref[:, cols]
                g_st[n, rows, :] = g_ref[:, cols] * sign

        def scores(t, first):
            for n in heads:
                for e in range(2):
                    k_pair[n, e * BLK : (e + 1) * BLK, :] = keys[chain[2 * t + e], :, n * HD : (n + 1) * HD]
            for n in heads:
                s_a, s_b = masked(dot_nt(k_pair[n], q_st[n]), t, count, first, causal)
                top = jnp.max(fold(jnp.maximum(s_a, s_b), jnp.maximum), axis=0, keepdims=True)
                if not first:
                    old = m_st[n, 0:1, :]
                    top = jnp.maximum(top, old)
                    alpha = jnp.exp2((old - top) * EXP_SCALE)
                p_a = jnp.exp2((s_a - top) * EXP_SCALE)
                p_b = jnp.exp2((s_b - top) * EXP_SCALE)
                p_st[n, t] = jnp.concatenate([p_a.astype(LOW), p_b.astype(LOW)], axis=0)
                total = fold(p_a + p_b, jnp.add)
                if first:
                    l_st[n] = total
                else:
                    l_st[n] = l_st[n] * alpha + total
                m_st[n, 0:1, :] = top
                mt_st[n, t, 0:1, :] = top

        over_pairs(scores, pairs)
        for n in heads:
            total = jnp.sum(l_st[n], axis=0, keepdims=True)
            l_st[n, 0:1, :] = 1.0 / total
            stats[n, which, 0:1, :] = m_st[n, 0:1, :] * EXP_SCALE + jnp.log2(total)

        def values(t, first):
            for n in heads:
                f = jnp.exp2((mt_st[n, t, 0:1, :] - m_st[n, 0:1, :]) * EXP_SCALE) * l_st[n, 0:1, :]
                w_st[n] = (p_st[n, t].astype(F32) * f).astype(LOW)
            for n in heads:
                dv = dot_nn(w_st[n], g_st[n])
                for e in range(2):
                    dv_acc[n, chain[2 * t + e]] += dv[e * BLK : (e + 1) * BLK, :]

        over_pairs(values, pairs)

    one_block(0, 2 * y + c, q_own, g_own)
    one_block(1, 2 * y + 1 - c, q_par, g_par)
    for s in range(SLOTS):
        for n in heads:
            dv_out[s, :, n * HD : (n + 1) * HD] = dv_acc[n, s].astype(LOW)


def output_kernel(
    place, parents, labels,
    q_own, q_par, g_own, g_par, keys, vals, stats,
    o_own, o_par, dq_own, dq_par, dk_out,
    chain, k_pair, v_pair, kt_pair, vt_pair, q_st, g_st, gt_st, w_st, ds_st, in_st, ot_st, dqt_st, dk_acc,
):
    y = place[0]
    c = place[1]
    heads = range(NG)
    dk_acc[...] = jnp.zeros_like(dk_acc)
    causal = causal_mask()

    def one_block(which, block, q_ref, g_ref, o_ref, dq_ref):
        count = walk(parents, block, chain)
        pairs = (count + 1) // 2
        sign = block_sign(labels, block)
        for n in heads:
            for h in range(GRP):
                rows = slice(h * BLK, (h + 1) * BLK)
                cols = slice(n * QW + h * HD, n * QW + (h + 1) * HD)
                q_st[n, rows, :] = q_ref[:, cols]
                g = g_ref[:, cols] * sign
                g_st[n, rows, :] = g
                gt_st[n, :, rows] = g.T

        def outputs(t, first):
            for n in heads:
                for e in range(2):
                    s = chain[2 * t + e]
                    rows = slice(e * BLK, (e + 1) * BLK)
                    k = keys[s, :, n * HD : (n + 1) * HD]
                    v = vals[s, :, n * HD : (n + 1) * HD]
                    k_pair[n, t, rows, :] = k
                    v_pair[n, t, rows, :] = v
                    kt_pair[n, t, :, rows] = k.T
                    vt_pair[n, t, :, rows] = v.T
            for n in heads:
                s_a, s_b = masked(dot_nt(k_pair[n, t], q_st[n]), t, count, first, causal)
                lse = stats[n, which, 0:1, :]
                w_a = jnp.exp2(s_a * EXP_SCALE - lse).astype(LOW)
                w_b = jnp.exp2(s_b * EXP_SCALE - lse).astype(LOW)
                w = jnp.concatenate([w_a, w_b], axis=0)
                w_st[n, t] = w
                out = dot_nn(vt_pair[n, t], w)
                if first:
                    ot_st[n] = out
                else:
                    ot_st[n] += out

        over_pairs(outputs, pairs)
        for h in range(GRP):
            for n in heads:
                cols = slice(h * BLK, (h + 1) * BLK)
                out = ot_st[n, :, cols].astype(LOW)
                o_ref[:, n * QW + h * HD : n * QW + (h + 1) * HD] = out.T
                in_st[n, 0:1, cols] = jnp.sum(
                    gt_st[n, :, cols].astype(F32) * out.astype(F32), axis=0, keepdims=True
                )

        def grads(t, first):
            for n in heads:
                dp = dot_nn(v_pair[n, t], gt_st[n])
                ds = (w_st[n, t].astype(F32) * (dp - in_st[n, 0:1, :])).astype(LOW)
                ds_st[n] = ds
                dq = dot_nn(kt_pair[n, t], ds)
                if first:
                    dqt_st[n] = dq
                else:
                    dqt_st[n] += dq
            for n in heads:
                dk = dot_nn(ds_st[n], q_st[n])
                for e in range(2):
                    dk_acc[n, chain[2 * t + e]] += dk[e * BLK : (e + 1) * BLK, :]

        over_pairs(grads, pairs)
        for h in range(GRP):
            for n in heads:
                cols = slice(h * BLK, (h + 1) * BLK)
                dq_ref[:, n * QW + h * HD : n * QW + (h + 1) * HD] = (dqt_st[n, :, cols] * SCALE).astype(LOW).T

    one_block(0, 2 * y + c, q_own, g_own, o_own, dq_own)
    one_block(1, 2 * y + 1 - c, q_par, g_par, o_par, dq_par)
    for s in range(SLOTS):
        for n in heads:
            dk_out[s, :, n * HD : (n + 1) * HD] = (dk_acc[n, s] * SCALE).astype(LOW)


def output_onward_kernel(*refs):
    output_kernel(*refs[:10], *refs[13:])


ROWS = GRP * BLK


def attention_call(kernel, name, steps, in_specs, out_specs, out_shape, scratch, aliases={}):
    return pl.pallas_call(
        kernel,
        grid_spec=pltpu.PrefetchScalarGridSpec(
            num_scalar_prefetch=3,
            grid=(steps,),
            in_specs=in_specs,
            out_specs=out_specs,
            scratch_shapes=[pltpu.SMEM((SLOTS,), jnp.int32)] + [pltpu.VMEM(*s) for s in scratch],
        ),
        out_shape=out_shape,
        input_output_aliases=aliases,
        compiler_params=pltpu.CompilerParams(dimension_semantics=("arbitrary",), vmem_limit_bytes=60 * 2**20),
        cost_estimate=LIGHT,
        name=name,
    )


def own_spec(start):
    return pl.BlockSpec((BLK, NG * QW), lambda i, place, par, lab: (0, place[1] * (HALF // NG) + start + i))


def partner_spec(start):
    return pl.BlockSpec((BLK, NG * QW), lambda i, place, par, lab: (0, start + i))


def blocks_spec(start):
    return pl.BlockSpec((SLOTS, BLK, NG * HD), lambda i, place, par, lab: (0, 0, start + i))


def stats_spec(start):
    return pl.BlockSpec((NG, 2, 8, ROWS), lambda i, place, par, lab: (start + i, 0, 0, 0))


def value_gradient(*args):
    own, partner = own_spec(0), partner_spec(0)
    return attention_call(
        values_kernel, "tree_values", HALF // NG,
        [own, partner, own, partner, blocks_spec(0)],
        [blocks_spec(0), stats_spec(0)],
        [jax.ShapeDtypeStruct((SLOTS, BLK, HALF * HD), LOW), jax.ShapeDtypeStruct((HALF, 2, 8, ROWS), F32)],
        [
            ((NG, 2 * BLK, HD), LOW),
            ((NG, ROWS, HD), LOW),
            ((NG, ROWS, HD), LOW),
            ((NG, PAIRS, 2 * BLK, ROWS), LOW),
            ((NG, 2 * BLK, ROWS), LOW),
            ((NG, 8, ROWS), F32),
            ((NG, PAIRS, 8, ROWS), F32),
            ((NG, 8, ROWS), F32),
            ((NG, SLOTS, BLK, HD), F32),
        ],
    )(*args)


def output_and_gradients(start, before, *args):
    own, partner, partner_out = own_spec(start), partner_spec(start), partner_spec(0)
    own_shape = jax.ShapeDtypeStruct((BLK, 2 * HALF * QW), LOW)
    partner_shape = jax.ShapeDtypeStruct((BLK, NG * QW), LOW)
    return attention_call(
        output_onward_kernel if before else output_kernel, "tree_outputs", 1,
        [own, partner, own, partner, blocks_spec(start), blocks_spec(start), stats_spec(start)]
        + [pl.BlockSpec(memory_space=pl.ANY)] * len(before),
        [own, partner_out, own, partner_out, blocks_spec(start)],
        [own_shape, partner_shape, own_shape, partner_shape, jax.ShapeDtypeStruct((SLOTS, BLK, HALF * HD), LOW)],
        [
            ((NG, PAIRS, 2 * BLK, HD), LOW),
            ((NG, PAIRS, 2 * BLK, HD), LOW),
            ((NG, PAIRS, HD, 2 * BLK), LOW),
            ((NG, PAIRS, HD, 2 * BLK), LOW),
            ((NG, ROWS, HD), LOW),
            ((NG, ROWS, HD), LOW),
            ((NG, HD, ROWS), LOW),
            ((NG, PAIRS, 2 * BLK, ROWS), LOW),
            ((NG, 2 * BLK, ROWS), LOW),
            ((NG, 8, ROWS), F32),
            ((NG, HD, ROWS), F32),
            ((NG, HD, ROWS), F32),
            ((NG, SLOTS, BLK, HD), F32),
        ],
        {10: 0, 11: 2, 12: 4} if before else {},
    )(*args, *before)


def weight_kernel(place, *refs):
    x_own, x_other, dv, out, x_all = refs[:NZ], refs[NZ : 2 * NZ], refs[-3], refs[-2], refs[-1]
    c, z = place[1], place[2]
    for d in range(NZ):
        src = lax.rem(z + NZ - d, NZ)
        for x, core in ((x_own[d], c), (x_other[d], 1 - c)):
            x_all[:, pl.ds(pl.multiple_of((2 * src + core) * BLK, BLK), BLK)] = x[...]
    out[...] = dot_nn(x_all[...], dv[...].reshape(2 * NZ * BLK, -1)).astype(LOW)


def weight_partial(place, x_own, x_other, dv):
    tall, wide, step = x_own[0].shape[0], dv.shape[3], 1024
    x_spec = pl.BlockSpec((step, BLK), lambda i, place: (i, 0))
    return pl.pallas_call(
        weight_kernel,
        grid_spec=pltpu.PrefetchScalarGridSpec(
            num_scalar_prefetch=1,
            grid=(tall // step,),
            in_specs=[x_spec] * (2 * NZ) + [pl.BlockSpec((NZ, 2, BLK, wide), lambda i, place: (0, 0, 0, 0))],
            out_specs=pl.BlockSpec((step, wide), lambda i, place: (i, 0)),
            scratch_shapes=[pltpu.VMEM((step, 2 * NZ * BLK), LOW)],
        ),
        out_shape=jax.ShapeDtypeStruct((tall, wide), LOW),
        compiler_params=pltpu.CompilerParams(vmem_limit_bytes=24 * 2**20),
        cost_estimate=LIGHT,
        name="weight_partial",
    )(place, *x_own, *x_other, dv)


def halves_kernel(k, v, k_out, v_out, done):
    width = k_out.shape[2]
    copies = [
        pltpu.make_async_copy(rows.at[:, pl.ds(i % 2 * width, width)], out.at[i], done.at[j, i])
        for j, (rows, out) in enumerate(((k, k_out), (v, v_out)))
        for i in range(SLOTS)
    ]
    for copy in copies:
        copy.start()
    for copy in copies:
        copy.wait()


def halves(k, v):
    width = k.shape[1] // 2
    return pl.pallas_call(
        halves_kernel,
        out_shape=[jax.ShapeDtypeStruct((SLOTS, BLK, width), LOW)] * 2,
        out_specs=[pl.BlockSpec(memory_space=pl.ANY)] * 2,
        scratch_shapes=[pltpu.SemaphoreType.DMA((2, SLOTS))],
        cost_estimate=LIGHT,
        name="halves",
    )(k, v)


def partner_kernel(place, q, g, q_out, g_out):
    q_out[...] = q[...]
    g_out[...] = g[...]


def partner_halves(place, q, g):
    steps = 2
    src = pl.BlockSpec((BLK, HALF * QW // steps), lambda i, place: (0, (1 - place[1]) * steps + i))
    dst = pl.BlockSpec((BLK, HALF * QW // steps), lambda i, place: (0, i))
    return pl.pallas_call(
        partner_kernel,
        grid_spec=pltpu.PrefetchScalarGridSpec(
            num_scalar_prefetch=1, grid=(steps,), in_specs=[src] * 2, out_specs=[dst] * 2
        ),
        out_shape=[jax.ShapeDtypeStruct((BLK, HALF * QW), LOW)] * 2,
        cost_estimate=LIGHT,
        name="partner_halves",
    )(place, q, g)


def fill_kernel(place, o_before, dq_before, o_a, o_b, dq_a, dq_b, o_all, dq_all):
    early = pl.program_id(0) < NG

    @pl.when(early)
    def _():
        o_all[...] = o_a[...]
        dq_all[...] = dq_a[...]

    @pl.when(jnp.logical_not(early))
    def _():
        o_all[...] = o_b[...]
        dq_all[...] = dq_b[...]


def fill_partner(place, o_all, dq_all, o_parts, dq_parts):
    anywhere = pl.BlockSpec(memory_space=pl.ANY)
    first = pl.BlockSpec((BLK, QW), lambda i, place: (0, jnp.minimum(i, NG - 1)))
    second = pl.BlockSpec((BLK, QW), lambda i, place: (0, jnp.maximum(i - NG, 0)))
    whole = pl.BlockSpec((BLK, QW), lambda i, place: (0, (1 - place[1]) * HALF + i))
    return pl.pallas_call(
        fill_kernel,
        grid_spec=pltpu.PrefetchScalarGridSpec(
            num_scalar_prefetch=1,
            grid=(HALF,),
            in_specs=[anywhere, anywhere, first, second, first, second],
            out_specs=[whole, whole],
        ),
        out_shape=[jax.ShapeDtypeStruct(o_all.shape, LOW)] * 2,
        input_output_aliases={1: 0, 2: 1},
        cost_estimate=LIGHT,
        name="fill_partner",
    )(place, o_all, dq_all, *o_parts, *dq_parts)


def x_kernel(place, x, *outs):
    piece = x.shape[1] // (NX * NZ)
    for d in range(NZ):
        to = lax.rem(place[2] + d, NZ)
        for i in range(NX):
            at = pl.multiple_of((i * NZ + to) * piece, piece)
            outs[d][i * piece : (i + 1) * piece, :] = x[:, pl.ds(at, piece)].T


def x_sends(place, x):
    tall = x.shape[1] // NZ
    return pl.pallas_call(
        x_kernel,
        grid_spec=pltpu.PrefetchScalarGridSpec(
            num_scalar_prefetch=1,
            grid=(1,),
            in_specs=[pl.BlockSpec(x.shape, lambda i, place: (0, 0))],
            out_specs=[pl.BlockSpec((tall, BLK), lambda i, place: (0, 0))] * NZ,
        ),
        out_shape=[jax.ShapeDtypeStruct((tall, BLK), LOW)] * NZ,
        cost_estimate=LIGHT,
        name="x_sends",
    )(place, x)


def sum_kernel(terms, out, total, done):
    for e in range(2):
        acc = terms[0, e].astype(F32)
        for i in range(1, NY):
            acc = acc + terms[i, e].astype(F32)
        total[e] = acc.astype(LOW)
    copies = [pltpu.make_async_copy(total, out.at[i], done.at[i]) for i in range(NZ)]
    for copy in copies:
        copy.start()
    for copy in copies:
        copy.wait()


def sum_blocks(terms):
    return pl.pallas_call(
        sum_kernel,
        out_shape=jax.ShapeDtypeStruct((NZ,) + terms.shape[1:], LOW),
        out_specs=pl.BlockSpec(memory_space=pl.ANY),
        scratch_shapes=[pltpu.VMEM(terms.shape[1:], LOW), pltpu.SemaphoreType.DMA((NZ,))],
        compiler_params=pltpu.CompilerParams(vmem_limit_bytes=60 * 2**20),
        cost_estimate=LIGHT,
        name="sum_blocks",
    )(terms)


def finish_kernel(parts, out):
    width = parts.shape[2]
    for half in range(2):
        acc = parts[half].astype(F32)
        for i in range(1, NX * NY):
            acc = acc + parts[2 * i + half].astype(F32)
        out[:, half * width : (half + 1) * width] = acc * (16 * SLOTS * BLK) ** -0.5


def finish_weight(parts):
    rows, width = parts.shape[1:]
    return pl.pallas_call(
        finish_kernel,
        out_shape=jax.ShapeDtypeStruct((rows, 2 * width), F32),
        compiler_params=pltpu.CompilerParams(vmem_limit_bytes=60 * 2**20),
        cost_estimate=LIGHT,
        name="finish_weight",
    )(parts)


def device(x, z, y, c):
    return (x * NZ + z) * SLOTS + y * 2 + c


def per_device(query_rows, key_rows, value_rows, layer_input, out_grad, parents, labels):
    ctx = lax.axis_index("ctx")
    y, c, z = ctx // 2, ctx % 2, lax.axis_index("dp") % NZ
    place = jnp.stack([y, c, z]).astype(jnp.int32)
    q, k, v, g, x = query_rows[0], key_rows[0], value_rows[0], out_grad[0], layer_input[0]
    along_y = [[2 * m + n for m in range(NY)] for n in range(2)]
    along_z = [[i * NZ + j for j in range(NZ)] for i in range(NX)]
    across = [[device(i, j, m, n) for i in range(NX) for m in range(NY) for n in range(2)] for j in range(NZ)]

    def swap(a):
        return lax.ppermute(a, "ctx", [(i, i ^ 1) for i in range(SLOTS)])

    def pick(a, i):
        return lax.dynamic_index_in_dim(a, i, 0, keepdims=False)

    def further(a, d):
        return lax.ppermute(a, "dp", [(i, i // NZ * NZ + (i + d) % NZ) for i in range(NX * NZ)])

    def earlier(a, d):
        return lax.ppermute(a, "ctx", [(i + 2 * d, i) for i in range(SLOTS - 2 * d)])

    k_sends, v_sends = halves(k, v)
    keys = lax.all_to_all(k_sends, "ctx", 0, 0)
    q_par, g_par = [swap(a) for a in partner_halves(place, q, g)]
    x_own = x_sends(place, x)
    x_own = [x_own[0]] + [further(x_own[d], d) for d in range(1, NZ)]
    keys, v_sends, x_own[1], x_own[3] = lax.optimization_barrier((keys, v_sends, x_own[1], x_own[3]))
    vals = lax.all_to_all(v_sends, "ctx", 0, 0)
    dv, stats = value_gradient(place, parents, labels, q, q_par, g, g_par, keys)
    dv, vals, x_own = lax.optimization_barrier((dv, vals, x_own))
    dv = lax.all_to_all(dv.reshape(NY, 2, BLK, HALF * HD), "ctx", 0, 0, axis_index_groups=along_y)
    args = (place, parents, labels, q, q_par, g, g_par, keys, vals, stats)
    o_own, o_par, dq_own, dq_par, dk = output_and_gradients(0, (), *args)
    o_pars, dq_pars = [o_par], [dq_par]
    dv, dk, x_own = lax.optimization_barrier((dv, dk, x_own))
    x_other = [swap(a) for a in x_own]
    dv_sends = sum_blocks(dv)
    dv_sends, dk = lax.optimization_barrier((dv_sends, dk))
    dv_all = lax.all_to_all(dv_sends, "dp", 0, 0, axis_index_groups=along_z)
    o_own, o_par, dq_own, dq_par, dk = output_and_gradients(1, (o_own, dq_own, dk), *args)
    o_pars, dq_pars = o_pars + [o_par], dq_pars + [dq_par]
    dv_all, dk = lax.optimization_barrier((dv_all, dk))
    dk = dk.reshape(NY, 2, BLK, HALF * HD)
    received = [earlier(pick(dk, jnp.maximum(y - d, 0)), d) for d in range(1, NY)]
    partial = weight_partial(place, x_own, x_other, dv_all).reshape(2 * NX * NY, -1, HALF * HD)
    _, o_pars, dq_pars = lax.optimization_barrier((partial, o_pars, dq_pars))
    o_pars, dq_pars = [swap(a) for a in o_pars], [swap(a) for a in dq_pars]
    weight_grad = finish_weight(lax.all_to_all(partial, ("dp", "ctx"), 0, 0, axis_index_groups=across))
    out, query_grad = fill_partner(place, o_own, dq_own, o_pars, dq_pars)
    dk, query_grad = lax.optimization_barrier((dk, query_grad))
    dk_sum = pick(dk, y).astype(F32)
    for term in received:
        dk_sum = dk_sum + term.astype(F32)
    both = jnp.stack([dk_sum.astype(LOW), dv_sends[0]], axis=1)
    mine, other = pick(both, c), swap(pick(both, 1 - c))
    key_grad, value_grad = jnp.concatenate([jnp.where(c == 0, mine, other), jnp.where(c == 0, other, mine)], axis=-1)
    return out[None], query_grad[None], key_grad[None], value_grad[None], weight_grad


def solution(mesh):
    rows = P("dp", "ctx", None)
    return jax.shard_map(
        per_device,
        mesh=mesh,
        in_specs=(rows,) * 5 + (P("dp", None), P("dp", None)),
        out_specs=(rows,) * 4 + (P(("dp", "ctx"), None),),
        check_vma=False,
    )
```

```python
import jax
import jax.numpy as jnp
from jax import lax
from jax.experimental import pallas as pl
from jax.experimental.pallas import tpu as pltpu
from jax.sharding import PartitionSpec as P

HD = 128
BLK = 128
GRP = 8
NY = 4
NZ = 4
NX = 4
HALF = 4
QW = GRP * HD
SLOTS = 2 * NY
PAIRS = 4
NG = 2
LOW = jnp.bfloat16
F32 = jnp.float32
SCALE = HD**-0.5
EXP_SCALE = SCALE * 1.4426950408889634
MASKED = -1e30
LIGHT = pl.CostEstimate(flops=1, bytes_accessed=1, transcendentals=0)


def dot_nt(a, b):
    return lax.dot_general(a, b, (((1,), (1,)), ((), ())), preferred_element_type=F32)


def dot_nn(a, b):
    return lax.dot_general(a, b, (((1,), (0,)), ((), ())), preferred_element_type=F32)


def dot_tn(a, b):
    return lax.dot_general(a, b, (((0,), (0,)), ((), ())), preferred_element_type=F32)


def walk(parents, block, chain):
    def above(step, carry):
        current, count = carry
        parent = parents[0, current]
        more = parent != current
        current = jnp.where(more, parent, current)
        chain[step + 1] = current
        return current, count + more.astype(jnp.int32)

    chain[0] = block
    return lax.fori_loop(0, SLOTS - 1, above, (block, jnp.int32(1)))[1]


def fold(a, op):
    while a.shape[0] > 8:
        half = a.shape[0] // 2
        a = op(a[:half], a[half:])
    return a


def causal_mask():
    key_pos = lax.broadcasted_iota(jnp.int32, (BLK, BLK), 0)
    query_pos = lax.broadcasted_iota(jnp.int32, (BLK, BLK), 1)
    causal = jnp.where(key_pos <= query_pos, 0.0, MASKED).astype(F32)
    return jnp.concatenate([causal] * GRP, axis=1)


def block_sign(labels, block):
    return jnp.full((BLK, HD), jnp.where(labels[0, block] == 2, -1.0, 1.0), F32).astype(LOW)


def masked(s, t, count, first, causal):
    second = jnp.where(2 * t + 1 < count, 0.0, MASKED).astype(F32)
    s_a = s[:BLK]
    if first:
        s_a = s_a + causal
    return s_a, s[BLK:] + second


def over_pairs(step, pairs):
    def more(t, carry):
        step(t, False)
        return carry

    step(0, True)
    lax.fori_loop(1, pairs, more, 0)


def values_kernel(
    place, parents, labels,
    q_own, q_par, g_own, g_par, keys,
    dv_out, stats,
    chain, k_pair, q_st, g_st, p_st, w_st, m_st, mt_st, l_st, dv_acc,
):
    y = place[0]
    c = place[1]
    heads = range(NG)
    dv_acc[...] = jnp.zeros_like(dv_acc)
    causal = causal_mask()

    def one_block(which, block, q_ref, g_ref):
        count = walk(parents, block, chain)
        pairs = (count + 1) // 2
        sign = block_sign(labels, block)
        for n in heads:
            for h in range(GRP):
                rows = slice(h * BLK, (h + 1) * BLK)
                cols = slice(n * QW + h * HD, n * QW + (h + 1) * HD)
                q_st[n, rows, :] = q_ref[:, cols]
                g_st[n, rows, :] = g_ref[:, cols] * sign

        def scores(t, first):
            for n in heads:
                for e in range(2):
                    k_pair[n, e * BLK : (e + 1) * BLK, :] = keys[chain[2 * t + e], :, n * HD : (n + 1) * HD]
            for n in heads:
                s_a, s_b = masked(dot_nt(k_pair[n], q_st[n]), t, count, first, causal)
                top = jnp.max(fold(jnp.maximum(s_a, s_b), jnp.maximum), axis=0, keepdims=True)
                if not first:
                    old = m_st[n, 0:1, :]
                    top = jnp.maximum(top, old)
                    alpha = jnp.exp2((old - top) * EXP_SCALE)
                p_a = jnp.exp2((s_a - top) * EXP_SCALE)
                p_b = jnp.exp2((s_b - top) * EXP_SCALE)
                p_st[n, t] = jnp.concatenate([p_a.astype(LOW), p_b.astype(LOW)], axis=0)
                total = fold(p_a + p_b, jnp.add)
                if first:
                    l_st[n] = total
                else:
                    l_st[n] = l_st[n] * alpha + total
                m_st[n, 0:1, :] = top
                mt_st[n, t, 0:1, :] = top

        over_pairs(scores, pairs)
        for n in heads:
            total = jnp.sum(l_st[n], axis=0, keepdims=True)
            l_st[n, 0:1, :] = 1.0 / total
            stats[n, which, 0:1, :] = m_st[n, 0:1, :] * EXP_SCALE + jnp.log2(total)

        def values(t, first):
            for n in heads:
                f = jnp.exp2((mt_st[n, t, 0:1, :] - m_st[n, 0:1, :]) * EXP_SCALE) * l_st[n, 0:1, :]
                w_st[n] = (p_st[n, t].astype(F32) * f).astype(LOW)
            for n in heads:
                dv = dot_nn(w_st[n], g_st[n])
                for e in range(2):
                    dv_acc[n, chain[2 * t + e]] += dv[e * BLK : (e + 1) * BLK, :]

        over_pairs(values, pairs)

    one_block(0, 2 * y + c, q_own, g_own)
    one_block(1, 2 * y + 1 - c, q_par, g_par)
    for s in range(SLOTS):
        for n in heads:
            dv_out[s, :, n * HD : (n + 1) * HD] = dv_acc[n, s].astype(LOW)


def output_kernel(
    place, parents, labels,
    q_own, q_par, g_own, g_par, keys, vals, stats,
    o_own, o_par, dq_own, dq_par, dk0, dk1, dk2, dk3,
    chain, k_pair, v_pair, kt_pair, vt_pair, q_st, g_st, gt_st, w_st, ds_st, in_st, ot_st, dqt_st, dk_acc,
):
    y = place[0]
    c = place[1]
    heads = range(NG)
    dk_acc[...] = jnp.zeros_like(dk_acc)
    causal = causal_mask()

    def one_block(which, block, q_ref, g_ref, o_ref, dq_ref):
        count = walk(parents, block, chain)
        pairs = (count + 1) // 2
        sign = block_sign(labels, block)
        for n in heads:
            for h in range(GRP):
                rows = slice(h * BLK, (h + 1) * BLK)
                cols = slice(n * QW + h * HD, n * QW + (h + 1) * HD)
                q_st[n, rows, :] = q_ref[:, cols]
                g = g_ref[:, cols] * sign
                g_st[n, rows, :] = g
                gt_st[n, :, rows] = g.T

        def outputs(t, first):
            for n in heads:
                for e in range(2):
                    s = chain[2 * t + e]
                    rows = slice(e * BLK, (e + 1) * BLK)
                    k = keys[s, :, n * HD : (n + 1) * HD]
                    v = vals[s, :, n * HD : (n + 1) * HD]
                    k_pair[n, t, rows, :] = k
                    v_pair[n, t, rows, :] = v
                    kt_pair[n, t, :, rows] = k.T
                    vt_pair[n, t, :, rows] = v.T
            for n in heads:
                s_a, s_b = masked(dot_nt(k_pair[n, t], q_st[n]), t, count, first, causal)
                lse = stats[n, which, 0:1, :]
                w_a = jnp.exp2(s_a * EXP_SCALE - lse).astype(LOW)
                w_b = jnp.exp2(s_b * EXP_SCALE - lse).astype(LOW)
                w = jnp.concatenate([w_a, w_b], axis=0)
                w_st[n, t] = w
                out = dot_nn(vt_pair[n, t], w)
                if first:
                    ot_st[n] = out
                else:
                    ot_st[n] += out

        over_pairs(outputs, pairs)
        for h in range(GRP):
            for n in heads:
                cols = slice(h * BLK, (h + 1) * BLK)
                out = ot_st[n, :, cols].astype(LOW)
                o_ref[:, n * QW + h * HD : n * QW + (h + 1) * HD] = out.T
                in_st[n, 0:1, cols] = jnp.sum(
                    gt_st[n, :, cols].astype(F32) * out.astype(F32), axis=0, keepdims=True
                )

        def grads(t, first):
            for n in heads:
                dp = dot_nn(v_pair[n, t], gt_st[n])
                ds = (w_st[n, t].astype(F32) * (dp - in_st[n, 0:1, :])).astype(LOW)
                ds_st[n] = ds
                dq = dot_nn(kt_pair[n, t], ds)
                if first:
                    dqt_st[n] = dq
                else:
                    dqt_st[n] += dq
            for n in heads:
                dk = dot_nn(ds_st[n], q_st[n])
                for e in range(2):
                    dk_acc[n, chain[2 * t + e]] += dk[e * BLK : (e + 1) * BLK, :]

        over_pairs(grads, pairs)
        for h in range(GRP):
            for n in heads:
                cols = slice(h * BLK, (h + 1) * BLK)
                dq_ref[:, n * QW + h * HD : n * QW + (h + 1) * HD] = (dqt_st[n, :, cols] * SCALE).astype(LOW).T

    one_block(0, 2 * y + c, q_own, g_own, o_own, dq_own)
    one_block(1, 2 * y + 1 - c, q_par, g_par, o_par, dq_par)
    for d, out in enumerate((dk0, dk1, dk2, dk3)):
        for e in range(2):
            s = 2 * jnp.maximum(y - d, 0) + e
            for n in heads:
                out[e, :, n * HD : (n + 1) * HD] = (dk_acc[n, s] * SCALE).astype(LOW)


def output_onward_kernel(*refs):
    output_kernel(*refs[:10], *refs[16:])


ROWS = GRP * BLK


def attention_call(kernel, name, steps, in_specs, out_specs, out_shape, scratch, aliases={}):
    return pl.pallas_call(
        kernel,
        grid_spec=pltpu.PrefetchScalarGridSpec(
            num_scalar_prefetch=3,
            grid=(steps,),
            in_specs=in_specs,
            out_specs=out_specs,
            scratch_shapes=[pltpu.SMEM((SLOTS,), jnp.int32)] + [pltpu.VMEM(*s) for s in scratch],
        ),
        out_shape=out_shape,
        input_output_aliases=aliases,
        compiler_params=pltpu.CompilerParams(dimension_semantics=("arbitrary",), vmem_limit_bytes=60 * 2**20),
        cost_estimate=LIGHT,
        name=name,
    )


def own_spec(start):
    return pl.BlockSpec((BLK, NG * QW), lambda i, place, par, lab: (0, place[1] * (HALF // NG) + start + i))


def partner_spec(start):
    return pl.BlockSpec((BLK, NG * QW), lambda i, place, par, lab: (0, start + i))


def blocks_spec(start):
    return pl.BlockSpec((SLOTS, BLK, NG * HD), lambda i, place, par, lab: (0, 0, start + i))


def stats_spec(start):
    return pl.BlockSpec((NG, 2, 8, ROWS), lambda i, place, par, lab: (start + i, 0, 0, 0))


def value_gradient(*args):
    own, partner = own_spec(0), partner_spec(0)
    return attention_call(
        values_kernel, "tree_values", HALF // NG,
        [own, partner, own, partner, blocks_spec(0)],
        [blocks_spec(0), stats_spec(0)],
        [jax.ShapeDtypeStruct((SLOTS, BLK, HALF * HD), LOW), jax.ShapeDtypeStruct((HALF, 2, 8, ROWS), F32)],
        [
            ((NG, 2 * BLK, HD), LOW),
            ((NG, ROWS, HD), LOW),
            ((NG, ROWS, HD), LOW),
            ((NG, PAIRS, 2 * BLK, ROWS), LOW),
            ((NG, 2 * BLK, ROWS), LOW),
            ((NG, 8, ROWS), F32),
            ((NG, PAIRS, 8, ROWS), F32),
            ((NG, 8, ROWS), F32),
            ((NG, SLOTS, BLK, HD), F32),
        ],
    )(*args)


def output_and_gradients(start, before, *args):
    own, partner, partner_out = own_spec(start), partner_spec(start), partner_spec(0)
    own_shape = jax.ShapeDtypeStruct((BLK, 2 * HALF * QW), LOW)
    partner_shape = jax.ShapeDtypeStruct((BLK, NG * QW), LOW)
    grads = pl.BlockSpec((2, BLK, NG * HD), lambda i, place, par, lab: (0, 0, start + i))
    grads_shape = jax.ShapeDtypeStruct((2, BLK, HALF * HD), LOW)
    return attention_call(
        output_onward_kernel if before else output_kernel, "tree_outputs", 1,
        [own, partner, own, partner, blocks_spec(start), blocks_spec(start), stats_spec(start)]
        + [pl.BlockSpec(memory_space=pl.ANY)] * len(before),
        [own, partner_out, own, partner_out] + [grads] * NY,
        [own_shape, partner_shape, own_shape, partner_shape] + [grads_shape] * NY,
        [
            ((NG, PAIRS, 2 * BLK, HD), LOW),
            ((NG, PAIRS, 2 * BLK, HD), LOW),
            ((NG, PAIRS, HD, 2 * BLK), LOW),
            ((NG, PAIRS, HD, 2 * BLK), LOW),
            ((NG, ROWS, HD), LOW),
            ((NG, ROWS, HD), LOW),
            ((NG, HD, ROWS), LOW),
            ((NG, PAIRS, 2 * BLK, ROWS), LOW),
            ((NG, 2 * BLK, ROWS), LOW),
            ((NG, 8, ROWS), F32),
            ((NG, HD, ROWS), F32),
            ((NG, HD, ROWS), F32),
            ((NG, SLOTS, BLK, HD), F32),
        ],
        {10: 0, 11: 2, 12: 4, 13: 5, 14: 6, 15: 7} if before else {},
    )(*args, *before)


def weight_kernel(place, *refs):
    x_own, x_other, dv, out, x_all = refs[:NZ], refs[NZ : 2 * NZ], refs[-3], refs[-2], refs[-1]
    c, z = place[1], place[2]
    for d in range(NZ):
        src = lax.rem(z + NZ - d, NZ)
        for x, core in ((x_own[d], c), (x_other[d], 1 - c)):
            x_all[:, pl.ds(pl.multiple_of((2 * src + core) * BLK, BLK), BLK)] = x[...]
    out[...] = dot_nn(x_all[...], dv[...].reshape(2 * NZ * BLK, -1)).astype(LOW)


def weight_partial(place, x_own, x_other, dv):
    tall, wide, step = x_own[0].shape[0], dv.shape[3], 1024
    x_spec = pl.BlockSpec((step, BLK), lambda i, place: (i, 0))
    return pl.pallas_call(
        weight_kernel,
        grid_spec=pltpu.PrefetchScalarGridSpec(
            num_scalar_prefetch=1,
            grid=(tall // step,),
            in_specs=[x_spec] * (2 * NZ) + [pl.BlockSpec((NZ, 2, BLK, wide), lambda i, place: (0, 0, 0, 0))],
            out_specs=pl.BlockSpec((step, wide), lambda i, place: (i, 0)),
            scratch_shapes=[pltpu.VMEM((step, 2 * NZ * BLK), LOW)],
        ),
        out_shape=jax.ShapeDtypeStruct((tall, wide), LOW),
        compiler_params=pltpu.CompilerParams(vmem_limit_bytes=24 * 2**20),
        cost_estimate=LIGHT,
        name="weight_partial",
    )(place, *x_own, *x_other, dv)


def halves_kernel(k, v, k_out, v_out, done):
    width = k_out.shape[2]
    copies = [
        pltpu.make_async_copy(rows.at[:, pl.ds(i % 2 * width, width)], out.at[i], done.at[j, i])
        for j, (rows, out) in enumerate(((k, k_out), (v, v_out)))
        for i in range(SLOTS)
    ]
    for copy in copies:
        copy.start()
    for copy in copies:
        copy.wait()


def halves(k, v):
    width = k.shape[1] // 2
    return pl.pallas_call(
        halves_kernel,
        out_shape=[jax.ShapeDtypeStruct((SLOTS, BLK, width), LOW)] * 2,
        out_specs=[pl.BlockSpec(memory_space=pl.ANY)] * 2,
        scratch_shapes=[pltpu.SemaphoreType.DMA((2, SLOTS))],
        cost_estimate=LIGHT,
        name="halves",
    )(k, v)


def partner_kernel(place, q, g, q_out, g_out):
    q_out[...] = q[...]
    g_out[...] = g[...]


def partner_halves(place, q, g):
    steps = 2
    src = pl.BlockSpec((BLK, HALF * QW // steps), lambda i, place: (0, (1 - place[1]) * steps + i))
    dst = pl.BlockSpec((BLK, HALF * QW // steps), lambda i, place: (0, i))
    return pl.pallas_call(
        partner_kernel,
        grid_spec=pltpu.PrefetchScalarGridSpec(
            num_scalar_prefetch=1, grid=(steps,), in_specs=[src] * 2, out_specs=[dst] * 2
        ),
        out_shape=[jax.ShapeDtypeStruct((BLK, HALF * QW), LOW)] * 2,
        cost_estimate=LIGHT,
        name="partner_halves",
    )(place, q, g)


def fill_kernel(place, o_before, dq_before, o_a, o_b, dq_a, dq_b, o_all, dq_all):
    early = pl.program_id(0) < NG

    @pl.when(early)
    def _():
        o_all[...] = o_a[...]
        dq_all[...] = dq_a[...]

    @pl.when(jnp.logical_not(early))
    def _():
        o_all[...] = o_b[...]
        dq_all[...] = dq_b[...]


def fill_partner(place, o_all, dq_all, o_parts, dq_parts):
    anywhere = pl.BlockSpec(memory_space=pl.ANY)
    first = pl.BlockSpec((BLK, QW), lambda i, place: (0, jnp.minimum(i, NG - 1)))
    second = pl.BlockSpec((BLK, QW), lambda i, place: (0, jnp.maximum(i - NG, 0)))
    whole = pl.BlockSpec((BLK, QW), lambda i, place: (0, (1 - place[1]) * HALF + i))
    return pl.pallas_call(
        fill_kernel,
        grid_spec=pltpu.PrefetchScalarGridSpec(
            num_scalar_prefetch=1,
            grid=(HALF,),
            in_specs=[anywhere, anywhere, first, second, first, second],
            out_specs=[whole, whole],
        ),
        out_shape=[jax.ShapeDtypeStruct(o_all.shape, LOW)] * 2,
        input_output_aliases={1: 0, 2: 1},
        cost_estimate=LIGHT,
        name="fill_partner",
    )(place, o_all, dq_all, *o_parts, *dq_parts)


def x_kernel(place, x, *outs):
    piece = x.shape[1] // (NX * NZ)
    for d in range(NZ):
        to = lax.rem(place[2] + d, NZ)
        for i in range(NX):
            at = pl.multiple_of((i * NZ + to) * piece, piece)
            outs[d][i * piece : (i + 1) * piece, :] = x[:, pl.ds(at, piece)].T


def x_sends(place, x):
    tall = x.shape[1] // NZ
    return pl.pallas_call(
        x_kernel,
        grid_spec=pltpu.PrefetchScalarGridSpec(
            num_scalar_prefetch=1,
            grid=(1,),
            in_specs=[pl.BlockSpec(x.shape, lambda i, place: (0, 0))],
            out_specs=[pl.BlockSpec((tall, BLK), lambda i, place: (0, 0))] * NZ,
        ),
        out_shape=[jax.ShapeDtypeStruct((tall, BLK), LOW)] * NZ,
        cost_estimate=LIGHT,
        name="x_sends",
    )(place, x)


def device(x, z, y, c):
    return (x * NZ + z) * SLOTS + y * 2 + c


def per_device(query_rows, key_rows, value_rows, layer_input, out_grad, parents, labels):
    ctx = lax.axis_index("ctx")
    y, c, z = ctx // 2, ctx % 2, lax.axis_index("dp") % NZ
    place = jnp.stack([y, c, z]).astype(jnp.int32)
    q, k, v, g, x = query_rows[0], key_rows[0], value_rows[0], out_grad[0], layer_input[0]
    along_y = [[2 * m + n for m in range(NY)] for n in range(2)]
    along_z = [[i * NZ + j for j in range(NZ)] for i in range(NX)]
    across = [[device(i, j, m, n) for i in range(NX) for m in range(NY) for n in range(2)] for j in range(NZ)]

    def swap(a):
        return lax.ppermute(a, "ctx", [(i, i ^ 1) for i in range(SLOTS)])

    def pick(a, i):
        return lax.dynamic_index_in_dim(a, i, 0, keepdims=False)

    def further(a, d):
        return lax.ppermute(a, "dp", [(i, i // NZ * NZ + (i + d) % NZ) for i in range(NX * NZ)])

    def earlier(a, d):
        return lax.ppermute(a, "ctx", [(i + 2 * d, i) for i in range(SLOTS - 2 * d)])

    k_sends, v_sends = halves(k, v)
    keys = lax.all_to_all(k_sends, "ctx", 0, 0)
    q_par, g_par = [swap(a) for a in partner_halves(place, q, g)]
    x_own = x_sends(place, x)
    x_own = [x_own[0]] + [further(x_own[d], d) for d in range(1, NZ)]
    keys, v_sends, x_own[1], x_own[3] = lax.optimization_barrier((keys, v_sends, x_own[1], x_own[3]))
    vals = lax.all_to_all(v_sends, "ctx", 0, 0)
    dv, stats = value_gradient(place, parents, labels, q, q_par, g, g_par, keys)
    dv, vals, x_own = lax.optimization_barrier((dv, vals, x_own))
    dv = lax.all_to_all(dv.reshape(NY, 2, BLK, HALF * HD), "ctx", 0, 0, axis_index_groups=along_y)
    args = (place, parents, labels, q, q_par, g, g_par, keys, vals, stats)
    o_own, o_par, dq_own, dq_par, *dk = output_and_gradients(0, (), *args)
    o_pars, dq_pars = [o_par], [dq_par]
    dv, dk, x_own = lax.optimization_barrier((dv, dk, x_own))
    x_other = [swap(a) for a in x_own]
    dv_sum = sum(dv[i].astype(F32) for i in range(NY)).astype(LOW)
    dv_sends = jnp.broadcast_to(dv_sum[None], dv.shape)
    dv_sends, dk = lax.optimization_barrier((dv_sends, dk))
    dv_all = lax.all_to_all(dv_sends, "dp", 0, 0, axis_index_groups=along_z)
    o_own, o_par, dq_own, dq_par, *dk = output_and_gradients(1, (o_own, dq_own, *dk), *args)
    o_pars, dq_pars = o_pars + [o_par], dq_pars + [dq_par]
    dv_all, dk = lax.optimization_barrier((dv_all, dk))
    received = [earlier(dk[d], d) for d in range(1, NY)]
    partial = weight_partial(place, x_own, x_other, dv_all).reshape(2 * NX * NY, -1, HALF * HD)
    _, o_pars, dq_pars = lax.optimization_barrier((partial, o_pars, dq_pars))
    o_pars, dq_pars = [swap(a) for a in o_pars], [swap(a) for a in dq_pars]
    shares = lax.all_to_all(partial, ("dp", "ctx"), 0, 0, axis_index_groups=across)
    total = jnp.sum(shares.reshape(NX * NY, 2, *shares.shape[1:]).astype(F32), axis=0)
    weight_grad = jnp.concatenate([total[0], total[1]], axis=1) * (16 * SLOTS * BLK) ** -0.5
    out, query_grad = fill_partner(place, o_own, dq_own, o_pars, dq_pars)
    dk, query_grad = lax.optimization_barrier((dk, query_grad))
    dk_sum = dk[0].astype(F32)
    for term in received:
        dk_sum = dk_sum + term.astype(F32)
    both = jnp.stack([dk_sum.astype(LOW), dv_sends[0]], axis=1)
    mine, other = pick(both, c), swap(pick(both, 1 - c))
    key_grad, value_grad = jnp.concatenate([jnp.where(c == 0, mine, other), jnp.where(c == 0, other, mine)], axis=-1)
    return out[None], query_grad[None], key_grad[None], value_grad[None], weight_grad


def solution(mesh):
    rows = P("dp", "ctx", None)
    return jax.shard_map(
        per_device,
        mesh=mesh,
        in_specs=(rows,) * 5 + (P("dp", None), P("dp", None)),
        out_specs=(rows,) * 4 + (P(("dp", "ctx"), None),),
        check_vma=False,
    )
```

```python
import functools

import jax
import jax.numpy as jnp
from jax import lax
from jax.experimental import pallas as pl
from jax.experimental.pallas import tpu as pltpu
from jax.sharding import PartitionSpec as P

HD = 128
BLK = 128
GRP = 8
NY = 4
NZ = 4
NX = 4
HALF = 4
QW = GRP * HD
SLOTS = 2 * NY
PAIRS = 2
NG = 2
LOW = jnp.bfloat16
F32 = jnp.float32
SCALE = HD**-0.5
EXP_SCALE = SCALE * 1.4426950408889634
MASKED = -1e30
LIGHT = pl.CostEstimate(flops=1, bytes_accessed=1, transcendentals=0)


def dot_nt(a, b):
    return lax.dot_general(a, b, (((1,), (1,)), ((), ())), preferred_element_type=F32)


def dot_nn(a, b):
    return lax.dot_general(a, b, (((1,), (0,)), ((), ())), preferred_element_type=F32)


def dot_tn(a, b):
    return lax.dot_general(a, b, (((0,), (0,)), ((), ())), preferred_element_type=F32)


def walk(parents, block, chain):
    def above(step, carry):
        current, count = carry
        parent = parents[0, current]
        more = parent != current
        current = jnp.where(more, parent, current)
        chain[step + 1] = current
        return current, count + more.astype(jnp.int32)

    chain[0] = block
    return lax.fori_loop(0, SLOTS - 1, above, (block, jnp.int32(1)))[1]


def fold(a, op):
    while a.shape[0] > 8:
        half = a.shape[0] // 2
        a = op(a[:half], a[half:])
    return a


def causal_mask():
    key_pos = lax.broadcasted_iota(jnp.int32, (BLK, BLK), 0)
    query_pos = lax.broadcasted_iota(jnp.int32, (BLK, BLK), 1)
    causal = jnp.where(key_pos <= query_pos, 0.0, MASKED).astype(F32)
    return jnp.concatenate([causal] * GRP, axis=1)


def block_sign(labels, block):
    return jnp.full((BLK, HD), jnp.where(labels[0, block] == 2, -1.0, 1.0), F32).astype(LOW)


def halved(s, first, causal):
    parts = [s[i : i + BLK] for i in range(0, s.shape[0], BLK)]
    if first:
        parts[0] = parts[0] + causal
    return parts


def over_chain(step, count):
    rest = count - 4 * ((count - 1) // 4)
    for blocks in range(1, 5):

        @pl.when(rest == blocks)
        def _(blocks=blocks):
            step(0, True, blocks)

    def more(t, carry):
        step(t, False, 4)
        return carry

    lax.fori_loop(1, (count + 3) // 4, more, 0)


def values_kernel(
    place, parents, labels,
    q_own, q_par, g_own, g_par, keys,
    dv_out, stats,
    chain, k_pair, q_st, g_st, p_st, w_st, m_st, mt_st, l_st, dv_acc,
):
    y = place[0]
    c = place[1]
    heads = range(NG)
    dv_acc[...] = jnp.zeros_like(dv_acc)
    causal = causal_mask()

    def one_block(which, block, q_ref, g_ref):
        count = walk(parents, block, chain)
        rest = count - 4 * ((count - 1) // 4)

        def seen(t, e, first):
            return chain[e] if first else chain[4 * (t - 1) + rest + e]

        sign = block_sign(labels, block)
        for n in heads:
            for h in range(GRP):
                rows = slice(h * BLK, (h + 1) * BLK)
                cols = slice(n * QW + h * HD, n * QW + (h + 1) * HD)
                q_st[n, rows, :] = q_ref[:, cols]
                g_st[n, rows, :] = g_ref[:, cols] * sign

        def scores(t, first, blocks):
            size = blocks * BLK
            for n in heads:
                for e in range(blocks):
                    k_pair[n, e * BLK : (e + 1) * BLK, :] = keys[seen(t, e, first), :, n * HD : (n + 1) * HD]
            for n in heads:
                parts = halved(dot_nt(k_pair[n, :size], q_st[n]), first, causal)
                most = functools.reduce(jnp.maximum, parts)
                top = jnp.max(fold(most, jnp.maximum), axis=0, keepdims=True)
                if not first:
                    old = m_st[n, 0:1, :]
                    top = jnp.maximum(top, old)
                    alpha = jnp.exp2((old - top) * EXP_SCALE)
                parts = [jnp.exp2((part - top) * EXP_SCALE) for part in parts]
                p_st[n, t, :size] = jnp.concatenate([part.astype(LOW) for part in parts], axis=0)
                total = fold(sum(parts), jnp.add)
                if first:
                    l_st[n] = total
                else:
                    l_st[n] = l_st[n] * alpha + total
                m_st[n, 0:1, :] = top
                mt_st[n, t, 0:1, :] = top

        over_chain(scores, count)
        for n in heads:
            total = jnp.sum(l_st[n], axis=0, keepdims=True)
            l_st[n, 0:1, :] = 1.0 / total
            stats[n, which, 0:1, :] = m_st[n, 0:1, :] * EXP_SCALE + jnp.log2(total)

        def values(t, first, blocks):
            size = blocks * BLK
            for n in heads:
                f = jnp.exp2((mt_st[n, t, 0:1, :] - m_st[n, 0:1, :]) * EXP_SCALE) * l_st[n, 0:1, :]
                w_st[n, :size] = (p_st[n, t, :size].astype(F32) * f).astype(LOW)
            for n in heads:
                dv = dot_nn(w_st[n, :size], g_st[n])
                for e in range(blocks):
                    dv_acc[n, seen(t, e, first)] += dv[e * BLK : (e + 1) * BLK, :]

        over_chain(values, count)

    one_block(0, 2 * y + c, q_own, g_own)
    one_block(1, 2 * y + 1 - c, q_par, g_par)
    for s in range(SLOTS):
        for n in heads:
            dv_out[s, :, n * HD : (n + 1) * HD] = dv_acc[n, s].astype(LOW)


def output_kernel(
    place, parents, labels,
    q_own, q_par, g_own, g_par, keys, vals, stats,
    o_own, o_par, dq_own, dq_par, dk0, dk1, dk2, dk3,
    chain, k_pair, v_pair, kt_pair, vt_pair, q_st, g_st, gt_st, w_st, ds_st, in_st, ot_st, dqt_st, dk_acc,
):
    y = place[0]
    c = place[1]
    heads = range(NG)
    dk_acc[...] = jnp.zeros_like(dk_acc)
    causal = causal_mask()

    def one_block(which, block, q_ref, g_ref, o_ref, dq_ref):
        count = walk(parents, block, chain)
        rest = count - 4 * ((count - 1) // 4)

        def seen(t, e, first):
            return chain[e] if first else chain[4 * (t - 1) + rest + e]

        sign = block_sign(labels, block)
        for n in heads:
            for h in range(GRP):
                rows = slice(h * BLK, (h + 1) * BLK)
                cols = slice(n * QW + h * HD, n * QW + (h + 1) * HD)
                q_st[n, rows, :] = q_ref[:, cols]
                g = g_ref[:, cols] * sign
                g_st[n, rows, :] = g
                gt_st[n, :, rows] = g.T

        def outputs(t, first, blocks):
            size = blocks * BLK
            for n in heads:
                for e in range(blocks):
                    s = seen(t, e, first)
                    rows = slice(e * BLK, (e + 1) * BLK)
                    k = keys[s, :, n * HD : (n + 1) * HD]
                    v = vals[s, :, n * HD : (n + 1) * HD]
                    k_pair[n, t, rows, :] = k
                    v_pair[n, t, rows, :] = v
                    kt_pair[n, t, :, rows] = k.T
                    vt_pair[n, t, :, rows] = v.T
            for n in heads:
                parts = halved(dot_nt(k_pair[n, t, :size], q_st[n]), first, causal)
                lse = stats[n, which, 0:1, :]
                w = jnp.concatenate([jnp.exp2(part * EXP_SCALE - lse).astype(LOW) for part in parts], axis=0)
                w_st[n, t, :size] = w
                out = dot_nn(vt_pair[n, t, :, :size], w)
                if first:
                    ot_st[n] = out
                else:
                    ot_st[n] += out

        over_chain(outputs, count)
        for h in range(GRP):
            for n in heads:
                cols = slice(h * BLK, (h + 1) * BLK)
                out = ot_st[n, :, cols].astype(LOW)
                o_ref[:, n * QW + h * HD : n * QW + (h + 1) * HD] = out.T
                in_st[n, 0:1, cols] = jnp.sum(
                    gt_st[n, :, cols].astype(F32) * out.astype(F32), axis=0, keepdims=True
                )

        def grads(t, first, blocks):
            size = blocks * BLK
            for n in heads:
                dp = dot_nn(v_pair[n, t, :size], gt_st[n])
                ds = (w_st[n, t, :size].astype(F32) * (dp - in_st[n, 0:1, :])).astype(LOW)
                ds_st[n, :size] = ds
                dq = dot_nn(kt_pair[n, t, :, :size], ds)
                if first:
                    dqt_st[n] = dq
                else:
                    dqt_st[n] += dq
            for n in heads:
                dk = dot_nn(ds_st[n, :size], q_st[n])
                for e in range(blocks):
                    dk_acc[n, seen(t, e, first)] += dk[e * BLK : (e + 1) * BLK, :]

        over_chain(grads, count)
        for h in range(GRP):
            for n in heads:
                cols = slice(h * BLK, (h + 1) * BLK)
                dq_ref[:, n * QW + h * HD : n * QW + (h + 1) * HD] = (dqt_st[n, :, cols] * SCALE).astype(LOW).T

    one_block(0, 2 * y + c, q_own, g_own, o_own, dq_own)
    one_block(1, 2 * y + 1 - c, q_par, g_par, o_par, dq_par)
    for d, out in enumerate((dk0, dk1, dk2, dk3)):
        for e in range(2):
            s = 2 * jnp.maximum(y - d, 0) + e
            for n in heads:
                out[e, :, n * HD : (n + 1) * HD] = (dk_acc[n, s] * SCALE).astype(LOW)


def output_onward_kernel(*refs):
    output_kernel(*refs[:10], *refs[16:])


ROWS = GRP * BLK


def attention_call(kernel, name, steps, in_specs, out_specs, out_shape, scratch, aliases={}):
    return pl.pallas_call(
        kernel,
        grid_spec=pltpu.PrefetchScalarGridSpec(
            num_scalar_prefetch=3,
            grid=(steps,),
            in_specs=in_specs,
            out_specs=out_specs,
            scratch_shapes=[pltpu.SMEM((SLOTS,), jnp.int32)] + [pltpu.VMEM(*s) for s in scratch],
        ),
        out_shape=out_shape,
        input_output_aliases=aliases,
        compiler_params=pltpu.CompilerParams(dimension_semantics=("arbitrary",), vmem_limit_bytes=60 * 2**20),
        cost_estimate=LIGHT,
        name=name,
    )


def own_spec(start):
    return pl.BlockSpec((BLK, NG * QW), lambda i, place, par, lab: (0, place[1] * (HALF // NG) + start + i))


def partner_spec(start):
    return pl.BlockSpec((BLK, NG * QW), lambda i, place, par, lab: (0, start + i))


def blocks_spec(start):
    return pl.BlockSpec((SLOTS, BLK, NG * HD), lambda i, place, par, lab: (0, 0, start + i))


def stats_spec(start):
    return pl.BlockSpec((NG, 2, 8, ROWS), lambda i, place, par, lab: (start + i, 0, 0, 0))


def value_gradient(*args):
    own, partner = own_spec(0), partner_spec(0)
    return attention_call(
        values_kernel, "tree_values", HALF // NG,
        [own, partner, own, partner, blocks_spec(0)],
        [blocks_spec(0), stats_spec(0)],
        [jax.ShapeDtypeStruct((SLOTS, BLK, HALF * HD), LOW), jax.ShapeDtypeStruct((HALF, 2, 8, ROWS), F32)],
        [
            ((NG, 4 * BLK, HD), LOW),
            ((NG, ROWS, HD), LOW),
            ((NG, ROWS, HD), LOW),
            ((NG, PAIRS, 4 * BLK, ROWS), LOW),
            ((NG, 4 * BLK, ROWS), LOW),
            ((NG, 8, ROWS), F32),
            ((NG, PAIRS, 8, ROWS), F32),
            ((NG, 8, ROWS), F32),
            ((NG, SLOTS, BLK, HD), F32),
        ],
    )(*args)


def output_and_gradients(start, before, *args):
    own, partner, partner_out = own_spec(start), partner_spec(start), partner_spec(0)
    own_shape = jax.ShapeDtypeStruct((BLK, 2 * HALF * QW), LOW)
    partner_shape = jax.ShapeDtypeStruct((BLK, NG * QW), LOW)
    grads = pl.BlockSpec((2, BLK, NG * HD), lambda i, place, par, lab: (0, 0, start + i))
    grads_shape = jax.ShapeDtypeStruct((2, BLK, HALF * HD), LOW)
    return attention_call(
        output_onward_kernel if before else output_kernel, "tree_outputs", 1,
        [own, partner, own, partner, blocks_spec(start), blocks_spec(start), stats_spec(start)]
        + [pl.BlockSpec(memory_space=pl.ANY)] * len(before),
        [own, partner_out, own, partner_out] + [grads] * NY,
        [own_shape, partner_shape, own_shape, partner_shape] + [grads_shape] * NY,
        [
            ((NG, PAIRS, 4 * BLK, HD), LOW),
            ((NG, PAIRS, 4 * BLK, HD), LOW),
            ((NG, PAIRS, HD, 4 * BLK), LOW),
            ((NG, PAIRS, HD, 4 * BLK), LOW),
            ((NG, ROWS, HD), LOW),
            ((NG, ROWS, HD), LOW),
            ((NG, HD, ROWS), LOW),
            ((NG, PAIRS, 4 * BLK, ROWS), LOW),
            ((NG, 4 * BLK, ROWS), LOW),
            ((NG, 8, ROWS), F32),
            ((NG, HD, ROWS), F32),
            ((NG, HD, ROWS), F32),
            ((NG, SLOTS, BLK, HD), F32),
        ],
        {10: 0, 11: 2, 12: 4, 13: 5, 14: 6, 15: 7} if before else {},
    )(*args, *before)


def weight_kernel(place, *refs):
    x_own, x_other, dv, out, x_all = refs[:NZ], refs[NZ : 2 * NZ], refs[-3], refs[-2], refs[-1]
    c, z = place[1], place[2]
    for d in range(NZ):
        src = lax.rem(z + NZ - d, NZ)
        for x, core in ((x_own[d], c), (x_other[d], 1 - c)):
            x_all[:, pl.ds(pl.multiple_of((2 * src + core) * BLK, BLK), BLK)] = x[...]
    out[...] = dot_nn(x_all[...], dv[...].reshape(2 * NZ * BLK, -1)).astype(LOW)


def weight_partial(place, x_own, x_other, dv):
    tall, wide, step = x_own[0].shape[0], dv.shape[3], 1024
    x_spec = pl.BlockSpec((step, BLK), lambda i, place: (i, 0))
    return pl.pallas_call(
        weight_kernel,
        grid_spec=pltpu.PrefetchScalarGridSpec(
            num_scalar_prefetch=1,
            grid=(tall // step,),
            in_specs=[x_spec] * (2 * NZ) + [pl.BlockSpec((NZ, 2, BLK, wide), lambda i, place: (0, 0, 0, 0))],
            out_specs=pl.BlockSpec((step, wide), lambda i, place: (i, 0)),
            scratch_shapes=[pltpu.VMEM((step, 2 * NZ * BLK), LOW)],
        ),
        out_shape=jax.ShapeDtypeStruct((tall, wide), LOW),
        compiler_params=pltpu.CompilerParams(vmem_limit_bytes=24 * 2**20),
        cost_estimate=LIGHT,
        name="weight_partial",
    )(place, *x_own, *x_other, dv)


def halves_kernel(k, v, k_out, v_out, done):
    width = k_out.shape[2]
    copies = [
        pltpu.make_async_copy(rows.at[:, pl.ds(i % 2 * width, width)], out.at[i], done.at[j, i])
        for j, (rows, out) in enumerate(((k, k_out), (v, v_out)))
        for i in range(SLOTS)
    ]
    for copy in copies:
        copy.start()
    for copy in copies:
        copy.wait()


def halves(k, v):
    width = k.shape[1] // 2
    return pl.pallas_call(
        halves_kernel,
        out_shape=[jax.ShapeDtypeStruct((SLOTS, BLK, width), LOW)] * 2,
        out_specs=[pl.BlockSpec(memory_space=pl.ANY)] * 2,
        scratch_shapes=[pltpu.SemaphoreType.DMA((2, SLOTS))],
        cost_estimate=LIGHT,
        name="halves",
    )(k, v)


def partner_kernel(place, q, g, q_out, g_out):
    q_out[...] = q[...]
    g_out[...] = g[...]


def partner_halves(place, q, g):
    steps = 2
    src = pl.BlockSpec((BLK, HALF * QW // steps), lambda i, place: (0, (1 - place[1]) * steps + i))
    dst = pl.BlockSpec((BLK, HALF * QW // steps), lambda i, place: (0, i))
    return pl.pallas_call(
        partner_kernel,
        grid_spec=pltpu.PrefetchScalarGridSpec(
            num_scalar_prefetch=1, grid=(steps,), in_specs=[src] * 2, out_specs=[dst] * 2
        ),
        out_shape=[jax.ShapeDtypeStruct((BLK, HALF * QW), LOW)] * 2,
        cost_estimate=LIGHT,
        name="partner_halves",
    )(place, q, g)


def fill_kernel(place, o_before, dq_before, o_a, o_b, dq_a, dq_b, o_all, dq_all):
    early = pl.program_id(0) < NG

    @pl.when(early)
    def _():
        o_all[...] = o_a[...]
        dq_all[...] = dq_a[...]

    @pl.when(jnp.logical_not(early))
    def _():
        o_all[...] = o_b[...]
        dq_all[...] = dq_b[...]


def fill_partner(place, o_all, dq_all, o_parts, dq_parts):
    anywhere = pl.BlockSpec(memory_space=pl.ANY)
    first = pl.BlockSpec((BLK, QW), lambda i, place: (0, jnp.minimum(i, NG - 1)))
    second = pl.BlockSpec((BLK, QW), lambda i, place: (0, jnp.maximum(i - NG, 0)))
    whole = pl.BlockSpec((BLK, QW), lambda i, place: (0, (1 - place[1]) * HALF + i))
    return pl.pallas_call(
        fill_kernel,
        grid_spec=pltpu.PrefetchScalarGridSpec(
            num_scalar_prefetch=1,
            grid=(HALF,),
            in_specs=[anywhere, anywhere, first, second, first, second],
            out_specs=[whole, whole],
        ),
        out_shape=[jax.ShapeDtypeStruct(o_all.shape, LOW)] * 2,
        input_output_aliases={1: 0, 2: 1},
        cost_estimate=LIGHT,
        name="fill_partner",
    )(place, o_all, dq_all, *o_parts, *dq_parts)


def x_kernel(place, x, *outs):
    piece = x.shape[1] // (NX * NZ)
    for d in range(NZ):
        to = lax.rem(place[2] + d, NZ)
        for i in range(NX):
            at = pl.multiple_of((i * NZ + to) * piece, piece)
            outs[d][i * piece : (i + 1) * piece, :] = x[:, pl.ds(at, piece)].T


def x_sends(place, x):
    tall = x.shape[1] // NZ
    return pl.pallas_call(
        x_kernel,
        grid_spec=pltpu.PrefetchScalarGridSpec(
            num_scalar_prefetch=1,
            grid=(1,),
            in_specs=[pl.BlockSpec(x.shape, lambda i, place: (0, 0))],
            out_specs=[pl.BlockSpec((tall, BLK), lambda i, place: (0, 0))] * NZ,
        ),
        out_shape=[jax.ShapeDtypeStruct((tall, BLK), LOW)] * NZ,
        cost_estimate=LIGHT,
        name="x_sends",
    )(place, x)


def device(x, z, y, c):
    return (x * NZ + z) * SLOTS + y * 2 + c


def per_device(query_rows, key_rows, value_rows, layer_input, out_grad, parents, labels):
    ctx = lax.axis_index("ctx")
    y, c, z = ctx // 2, ctx % 2, lax.axis_index("dp") % NZ
    place = jnp.stack([y, c, z]).astype(jnp.int32)
    q, k, v, g, x = query_rows[0], key_rows[0], value_rows[0], out_grad[0], layer_input[0]
    along_y = [[2 * m + n for m in range(NY)] for n in range(2)]
    along_z = [[i * NZ + j for j in range(NZ)] for i in range(NX)]
    across = [[device(i, j, m, n) for i in range(NX) for m in range(NY) for n in range(2)] for j in range(NZ)]

    def swap(a):
        return lax.ppermute(a, "ctx", [(i, i ^ 1) for i in range(SLOTS)])

    def pick(a, i):
        return lax.dynamic_index_in_dim(a, i, 0, keepdims=False)

    def further(a, d):
        return lax.ppermute(a, "dp", [(i, i // NZ * NZ + (i + d) % NZ) for i in range(NX * NZ)])

    def earlier(a, d):
        return lax.ppermute(a, "ctx", [(i + 2 * d, i) for i in range(SLOTS - 2 * d)])

    k_sends, v_sends = halves(k, v)
    keys = lax.all_to_all(k_sends, "ctx", 0, 0)
    q_par, g_par = [swap(a) for a in partner_halves(place, q, g)]
    x_own = x_sends(place, x)
    x_own = [x_own[0]] + [further(x_own[d], d) for d in range(1, NZ)]
    keys, v_sends, x_own[1], x_own[3] = lax.optimization_barrier((keys, v_sends, x_own[1], x_own[3]))
    vals = lax.all_to_all(v_sends, "ctx", 0, 0)
    dv, stats = value_gradient(place, parents, labels, q, q_par, g, g_par, keys)
    dv, vals, x_own = lax.optimization_barrier((dv, vals, x_own))
    dv = lax.all_to_all(dv.reshape(NY, 2, BLK, HALF * HD), "ctx", 0, 0, axis_index_groups=along_y)
    args = (place, parents, labels, q, q_par, g, g_par, keys, vals, stats)
    o_own, o_par, dq_own, dq_par, *dk = output_and_gradients(0, (), *args)
    o_pars, dq_pars = [o_par], [dq_par]
    dv, dk, x_own = lax.optimization_barrier((dv, dk, x_own))
    x_other = [swap(a) for a in x_own]
    dv_sum = sum(dv[i].astype(F32) for i in range(NY)).astype(LOW)
    dv_sends = jnp.broadcast_to(dv_sum[None], dv.shape)
    dv_sends, dk = lax.optimization_barrier((dv_sends, dk))
    dv_all = lax.all_to_all(dv_sends, "dp", 0, 0, axis_index_groups=along_z)
    o_own, o_par, dq_own, dq_par, *dk = output_and_gradients(1, (o_own, dq_own, *dk), *args)
    o_pars, dq_pars = o_pars + [o_par], dq_pars + [dq_par]
    dv_all, dk = lax.optimization_barrier((dv_all, dk))
    received = [earlier(dk[d], d) for d in range(1, NY)]
    partial = weight_partial(place, x_own, x_other, dv_all).reshape(2 * NX * NY, -1, HALF * HD)
    _, o_pars, dq_pars = lax.optimization_barrier((partial, o_pars, dq_pars))
    o_pars, dq_pars = [swap(a) for a in o_pars], [swap(a) for a in dq_pars]
    shares = lax.all_to_all(partial, ("dp", "ctx"), 0, 0, axis_index_groups=across)
    total = jnp.sum(shares.reshape(NX * NY, 2, *shares.shape[1:]).astype(F32), axis=0)
    weight_grad = jnp.concatenate([total[0], total[1]], axis=1) * (16 * SLOTS * BLK) ** -0.5
    out, query_grad = fill_partner(place, o_own, dq_own, o_pars, dq_pars)
    dk, query_grad = lax.optimization_barrier((dk, query_grad))
    dk_sum = dk[0].astype(F32)
    for term in received:
        dk_sum = dk_sum + term.astype(F32)
    both = jnp.stack([dk_sum.astype(LOW), dv_sends[0]], axis=1)
    mine, other = pick(both, c), swap(pick(both, 1 - c))
    key_grad, value_grad = jnp.concatenate([jnp.where(c == 0, mine, other), jnp.where(c == 0, other, mine)], axis=-1)
    return out[None], query_grad[None], key_grad[None], value_grad[None], weight_grad


def solution(mesh):
    rows = P("dp", "ctx", None)
    return jax.shard_map(
        per_device,
        mesh=mesh,
        in_specs=(rows,) * 5 + (P("dp", None), P("dp", None)),
        out_specs=(rows,) * 4 + (P(("dp", "ctx"), None),),
        check_vma=False,
    )
```
